32 devices in a mesh: ctx: 4 (over x, core), row: 2 (over y), batch: 4 (over z).
Axes of the slice: x: 2, y: 2, z: 4, core: 2. Of those that a mesh axis runs over, the one named last changes fastest.
Arguments:
- queries: bfloat16 [3072, 5120], P(('batch', 'ctx'), 'row'), parts along dimension 0
- keys: bfloat16 [3072, 5120], P(('batch', 'ctx'), 'row'), parts along dimension 0
- values: bfloat16 [3072, 5120], P(('batch', 'ctx'), 'row'), parts along dimension 0, may hold values from -6 to 6
- gain_q: float32 [5120], P('row'), may hold values from 1.2 to 2.4
- gain_k: float32 [5120], P('row'), may hold values from 1.2 to 2.4
- clip_ids: int32 [3072], P(('batch', 'ctx')), parts along dimension 0, may hold values from 0 to 3, never falling along the last dimension, each value on 1 to 480 neighbouring positions
- clip_grid: int32 [16, 2], P('batch'), parts along dimension 0, may hold values from 8 to 40
Outputs:
- attended: bfloat16 [3072, 5120], P(('batch', 'ctx'), 'row'), parts along dimension 0
The draws below stay inside these ranges and needn't reach their ends.
There are 4 independent parts, one for each index of `batch`. The reference program is written for one: setup_inputs(seed, part) draws one part's arguments, and reference() takes and returns one part's arrays. A program takes and returns all parts, laid end to end along the dimension named above; an argument that names none is the same for every part. Nothing has to cross between parts.
Inputs may be any that keep to these rules, and one draw needn't show every extreme that they name: `clip_ids`: never falls along the tokens; each of the 4 clips has 1 to 480 tokens, and one has exactly 480.
All inputs are finite; a program needn't handle non-finite values.
Results may differ from the reference program's by a relative error of at most 0.012.
The reference program's roundings to bfloat16 on the way count: a program that leaves them out, or rounds other values in their place, can miss the bound.
Values may be sent and summed in bfloat16 or wider, within the bound.
No kernel may reach another device: no remote copies, remote signals or barrier semaphores. Data moves between devices by JAX's collectives and lax.ppermute only.
A program may use at most 64 MiB of HBM per device.

```python
import math
import jax
import jax.numpy as jnp
import numpy as np
from jax import lax

HEADS = 40
HD = 128
D = 5120
TOKENS = 768
CLIPS = 4
MOST = 480


def shared_field(key, which):
    columns = jnp.arange(D, dtype=jnp.float32)
    primary = jax.random.normal(jax.random.fold_in(key, 10 + which), (TOKENS, D), jnp.float32)
    rising = jnp.sqrt(1.0 + 2.0 * columns / (D - 1))
    row_scale = 10.0 ** jax.random.uniform(jax.random.fold_in(key, 30 + which), (TOKENS, 1), jnp.float32)
    column_scale = 10.0 ** jax.random.uniform(jax.random.fold_in(key, 40 + which), (1, D), jnp.float32) * rising[None, :]
    matrix = 0.3 * primary * row_scale * column_scale
    return matrix


def draw_queries(key, part):
    return shared_field(key, 0).astype(jnp.bfloat16)


def draw_keys(key, part):
    return shared_field(key, 1).astype(jnp.bfloat16)


def touch_ends(drawn, rng, smallest, top_value):
    dims = drawn.shape
    index_at = [jax.random.randint(jax.random.fold_in(rng, axis), (), 0, dims[axis]) for axis in range(len(dims))]
    drawn = drawn.at[tuple(index_at)].set(smallest)
    longest = dims.index(max(dims))
    index_at[longest] = (index_at[longest] + 1) % dims[longest]
    return drawn.at[tuple(index_at)].set(top_value)


def level_of(own_key, extent, shards, smallest, high):
    def one(position, shards_of):
        steps = jax.random.uniform(jax.random.fold_in(jax.random.fold_in(own_key, 6), position), (shards_of,), jnp.float32, smallest / len(shards), high / len(shards))
        return jnp.repeat(jnp.exp(steps), extent[position] // shards_of).reshape((-1,) + (1,) * (len(extent) - position - 1))

    loudness = one(*shards[0])
    for cut in shards[1:]:
        loudness = loudness * one(*cut)
    return loudness


def profile(number_of, total, limit, slope):
    weights = [(1 << 20) // math.isqrt(grade ** slope) + 1 for grade in range(2, number_of + 1)]
    spare, given = total - limit - (number_of - 1), [1] * (number_of - 1)
    while spare > 0:
        free = [i for i in range(number_of - 1) if given[i] < limit]
        mass, left = sum([weights[i] for i in free]), spare
        for i in free:
            more = min(limit - given[i], max(1, left * weights[i] // mass), spare)
            given[i] = given[i] + more
            spare = spare - more
    return np.array([limit] + given)


def ragged_sizes(stream_key, count, total, most, lean):
    if count == 2:
        one = jax.random.randint(stream_key, (), max(1, total - most), min(most, total - 1) + 1)
        return jnp.stack([one, total - one])
    lengths = jnp.asarray(profile(count, total, most, lean), jnp.int32)
    couples = (count - 1) // 2
    donor, receiver = lengths[1:1 + 2 * couples:2], lengths[2:2 + 2 * couples:2]
    margin = jnp.minimum(donor - 1, most - receiver)
    moved = jax.random.randint(jax.random.fold_in(stream_key, 1), (couples,), 0, 1 << 20) % (margin + 1)
    lengths = lengths.at[1:1 + 2 * couples:2].set(donor - moved).at[2:2 + 2 * couples:2].set(receiver + moved)
    return lengths[jax.random.permutation(jax.random.fold_in(stream_key, 2), count)]


def gaussian(key, extent, scale, limit, split=(), kind=jnp.bfloat16):
    level = level_of(key, extent, split, -0.22, 0.18) if split else 1.0
    values = jax.random.normal(key, extent, jnp.float32) * scale * level
    return jnp.minimum(jnp.maximum(values, -limit), limit).astype(kind)


def setup_inputs(seed: int = 0, part: int = 0) -> dict:
    seeds = jax.random.split(jax.random.key(seed), 8)
    part_keys = jax.random.split(jax.random.fold_in(seeds[7], part), 8)
    queries = draw_queries(jax.random.fold_in(jax.random.fold_in(seeds[7], part), 71), part)
    keys = draw_keys(jax.random.fold_in(jax.random.fold_in(seeds[7], part), 71), part)
    values = gaussian(part_keys[2], (TOKENS, D), 1.0, 6.0, ((0, 4), (1, 2)))
    gain_q = jnp.clip(1.2 + 1.2 * jax.random.uniform(seeds[3], (D,), jnp.float32) ** level_of(seeds[3], (D,), ((0, 2),), -0.2, 0.2), 1.2, 2.4)
    gain_k = jnp.clip(1.2 + 1.2 * jax.random.uniform(seeds[4], (D,), jnp.float32) ** level_of(seeds[4], (D,), ((0, 2),), -0.2, 0.2), 1.2, 2.4)
    clip_ids = jnp.searchsorted(jnp.cumsum(ragged_sizes(part_keys[5], CLIPS, TOKENS, MOST, 2)), jnp.arange(TOKENS), side="right").astype(jnp.int32)
    clip_grid = touch_ends(jax.random.randint(part_keys[6], (CLIPS, 2), 8, 41), jax.random.fold_in(part_keys[6], 1), 8, 40).astype(jnp.int32)
    return dict(queries=queries, keys=keys, values=values, gain_q=gain_q, gain_k=gain_k, clip_ids=clip_ids, clip_grid=clip_grid)


EPSILON = 1e-06
NEGATIVE = -1e+30
ROTARY_BASE = 10000.0

def lookup(lookup_table, positions):
    labels = jnp.arange(lookup_table.shape[0], dtype=jnp.int32)
    return lax.optimization_barrier(jnp.sum(jnp.where(positions[:, None] == labels[None, :], lookup_table[None, :], 0), axis=1))

def spin(matrix, offsets, clip_of, clip_grid, head_size):
    row_count = matrix.shape[0]
    sixth_part = head_size // 6
    first_dims = head_size - 4 * sixth_part
    first_freqs = 1.0 / ROTARY_BASE ** (jnp.arange(0, first_dims, 2, dtype=jnp.float32) / first_dims)
    other_freqs = 1.0 / ROTARY_BASE ** (jnp.arange(0, 2 * sixth_part, 2, dtype=jnp.float32) / (2 * sixth_part))
    heights = lookup(clip_grid[:, 0], clip_of)
    widths = lookup(clip_grid[:, 1], clip_of)
    frame_pos = offsets // (heights * widths)
    line_pos = offsets // widths % heights
    column_pos = offsets % widths
    angles = jnp.concatenate([frame_pos.astype(jnp.float32)[:, None] * first_freqs[None, :], line_pos.astype(jnp.float32)[:, None] * other_freqs[None, :], column_pos.astype(jnp.float32)[:, None] * other_freqs[None, :]], axis=1)
    cosine = jnp.repeat(jnp.cos(angles), 2, axis=1)
    sine_table = jnp.repeat(jnp.sin(angles), 2, axis=1)
    feature = jnp.arange(head_size, dtype=jnp.int32)
    is_even = (feature % 2 == 0)[None, None, :]
    head_view = matrix.reshape(row_count, -1, head_size)
    partner = jnp.where(is_even, -jnp.roll(head_view, -1, axis=2), jnp.roll(head_view, 1, axis=2))
    turned = head_view * cosine[:, None, :] + partner * sine_table[:, None, :]
    return turned.reshape(row_count, -1)

def reference(queries, keys, values, gain_q, gain_k, clip_ids, clip_grid):
    query_wide = queries.astype(jnp.float32)
    key_wide = keys.astype(jnp.float32)
    query_scale = lax.rsqrt(lax.optimization_barrier(jnp.sum(query_wide * query_wide, axis=1)) / D + EPSILON)
    key_scale = lax.rsqrt(lax.optimization_barrier(jnp.sum(key_wide * key_wide, axis=1)) / D + EPSILON)
    labels = jnp.arange(CLIPS, dtype=jnp.int32)
    counts = lax.optimization_barrier(jnp.sum((clip_ids[:, None] == labels[None, :]).astype(jnp.int32), axis=0))
    starts = jnp.cumsum(counts) - counts
    offsets = jnp.arange(TOKENS, dtype=jnp.int32) - lookup(starts, clip_ids)
    query_rot = spin(query_wide * query_scale[:, None] * gain_q[None, :], offsets, clip_ids, clip_grid, HD).astype(jnp.bfloat16)
    key_rot = spin(key_wide * key_scale[:, None] * gain_k[None, :], offsets, clip_ids, clip_grid, HD).astype(jnp.bfloat16)
    query_heads = jnp.transpose(query_rot.reshape(TOKENS, HEADS, HD), (1, 0, 2))
    key_heads = jnp.transpose(key_rot.reshape(TOKENS, HEADS, HD), (1, 0, 2))
    value_heads = jnp.transpose(values.reshape(TOKENS, HEADS, HD), (1, 0, 2))
    same = clip_ids[:, None] == clip_ids[None, :]
    score_scale = 1.0 / math.sqrt(HD)

    def one_head(operands):
        query_one, key_one, value_one = operands
        scores = jnp.dot(query_one, key_one.T, preferred_element_type=jnp.float32) * score_scale
        masked = jnp.where(same, scores, NEGATIVE)
        peak = lax.optimization_barrier(jnp.max(masked, axis=1))
        weights = jnp.where(same, jnp.exp(masked - peak[:, None]), 0.0)
        total_sum = lax.optimization_barrier(jnp.sum(weights, axis=1))
        summed = jnp.dot(weights.astype(jnp.bfloat16), value_one, preferred_element_type=jnp.float32)
        return summed / total_sum[:, None]
    outputs = lax.map(one_head, (query_heads, key_heads, value_heads))
    return jnp.transpose(outputs, (1, 0, 2)).reshape(TOKENS, D).astype(jnp.bfloat16)
```

```python
import functools
import math

import jax
import jax.numpy as jnp
from jax import lax
from jax.experimental import pallas as pl
from jax.experimental.pallas import tpu as pltpu
from jax.sharding import PartitionSpec as P

HD = 128
D = 5120
CLIPS = 4
EPSILON = 1e-06
NEGATIVE = -1e30
ROTARY_BASE = 10000.0
block_limit = 1024
GROUPS = (4, 4, 4, 4, 2, 2)
ACROSS = ((0, 2), (1, 3), (2, 0), (3, 1))
BESIDE = ((0, 1), (1, 0), (2, 3), (3, 2))


def lookup(lookup_table, positions):
    labels = jnp.arange(lookup_table.shape[0], dtype=jnp.int32)
    return jnp.sum(
        jnp.where(positions[:, None] == labels[None, :], lookup_table[None, :], 0), axis=1
    )


def angles_of(offsets, clip_of, clip_grid):
    sixth_part = HD // 6
    first_dims = HD - 4 * sixth_part
    first_freqs = 1.0 / ROTARY_BASE ** (
        jnp.arange(0, first_dims, 2, dtype=jnp.float32) / first_dims
    )
    other_freqs = 1.0 / ROTARY_BASE ** (
        jnp.arange(0, 2 * sixth_part, 2, dtype=jnp.float32) / (2 * sixth_part)
    )
    heights = lookup(clip_grid[:, 0], clip_of)
    widths = lookup(clip_grid[:, 1], clip_of)
    frame_pos = (offsets // (heights * widths)).astype(jnp.float32)[:, None]
    line_pos = (offsets // widths % heights).astype(jnp.float32)[:, None]
    column_pos = (offsets % widths).astype(jnp.float32)[:, None]
    freqs = jnp.repeat(jnp.concatenate([first_freqs, other_freqs, other_freqs]), 2)[None, :]
    feature = jnp.arange(HD, dtype=jnp.int32)[None, :]
    position = jnp.where(
        feature < first_dims,
        frame_pos,
        jnp.where(feature < first_dims + 2 * sixth_part, line_pos, column_pos),
    )
    return position * freqs


def attend_kernel(
    pieces, scale, q_ref, *refs
):
    k_refs, v_refs = refs[:pieces], refs[pieces : 2 * pieces]
    (cq, sq, ck, sk, gq, gqs, gk, gks, swap, qc, kc, o_ref, bias, krot) = refs[2 * pieces :]
    rows = q_ref.shape[0]

    @pl.when(pl.program_id(0) == 0)
    def _():
        bias[...] = jnp.where(qc[...] == kc[...], 0.0, NEGATIVE).astype(jnp.float32)

    def turn(x, gain, gain_s, cosine, sine):
        other = jnp.dot(x, swap[...], preferred_element_type=jnp.float32)
        return (
            (x.astype(jnp.float32) * gain) * cosine + (other * gain_s) * sine
        ).astype(jnp.bfloat16)

    for i in range(pieces):
        at = slice(i * rows, (i + 1) * rows)
        krot[at, :] = turn(k_refs[i][...], gk[...], gks[...], ck[at, :], sk[at, :])
    q = turn(q_ref[...], gq[...], gqs[...], cq[...], sq[...])
    scores = (
        lax.dot_general(q, krot[...], (((1,), (1,)), ((), ())), preferred_element_type=jnp.float32)
        + bias[...]
    )
    peak = jnp.max(scores, axis=1, keepdims=True)
    weights = jnp.exp2((scores - peak) * scale)
    total = jnp.sum(weights, axis=1, keepdims=True)
    weights = weights.astype(jnp.bfloat16)
    out = jnp.zeros((rows, HD), jnp.float32)
    for i in range(pieces):
        at = slice(i * rows, (i + 1) * rows)
        out += jnp.dot(weights[:, at], v_refs[i][...], preferred_element_type=jnp.float32)
    o_ref[...] = (out / total).astype(o_ref.dtype)


def attend(first, heads, q, near, far, tables, gains, swap, clips):
    rows = q.shape[0]
    cq, sq, ck, sk = tables
    qc, kc = clips
    tokens = ck.shape[0]
    pieces = len(near[0]) + len(far)
    whole = lambda a: pl.BlockSpec(a.shape, lambda h: (0,) * a.ndim)
    wide = pl.BlockSpec((rows, HD), lambda h: (0, first + h))
    k_spec = pl.BlockSpec((None, rows, HD), lambda h: (0, 0, h))
    v_spec = pl.BlockSpec((None, rows, HD), lambda h: (1, 0, h))
    gain_spec = pl.BlockSpec((1, HD), lambda h: (0, first + h))
    kernel = functools.partial(attend_kernel, pieces, math.log2(math.e) / math.sqrt(HD))
    return pl.pallas_call(
        kernel,
        grid=(heads,),
        out_shape=jax.ShapeDtypeStruct((rows, heads * HD), jnp.bfloat16),
        in_specs=[wide]
        + [wide] * len(near[0])
        + [k_spec] * len(far)
        + [wide] * len(near[1])
        + [v_spec] * len(far)
        + [whole(a) for a in (cq, sq, ck, sk)]
        + [gain_spec] * 4
        + [whole(swap), whole(qc), whole(kc)],
        out_specs=pl.BlockSpec((rows, HD), lambda h: (0, h)),
        scratch_shapes=[
            pltpu.VMEM((rows, tokens), jnp.float32),
            pltpu.VMEM((tokens, HD), jnp.bfloat16),
        ],
        compiler_params=pltpu.CompilerParams(vmem_limit_bytes=24 * 1024 * 1024),
        cost_estimate=pl.CostEstimate(
            flops=4 * heads * rows * tokens * HD * 4,
            bytes_accessed=heads * tokens * HD * 4 + tokens * HD * 8,
            transcendentals=heads * rows * tokens,
        ),
    )(q, *near[0], *far, *near[1], *far, cq, sq, ck, sk, *gains, swap, qc, kc)


def on_device(queries, keys, values, gain_q, gain_k, clip_ids, clip_grid):
    rows, width = queries.shape
    me = lax.axis_index("ctx")
    tokens = 4 * rows

    far, first = [], 0
    for heads in GROUPS:
        at = slice(first * HD, (first + heads) * HD)
        far.append(lax.ppermute(jnp.stack([keys[:, at], values[:, at]]), "ctx", ACROSS))
        first += heads
    keys_beside = lax.ppermute(keys, "ctx", BESIDE)
    values_beside = lax.ppermute(values, "ctx", BESIDE)

    q32, k32 = queries.astype(jnp.float32), keys.astype(jnp.float32)
    label = jnp.where(lax.axis_index("row") == 0, clip_ids, 0).astype(jnp.float32)
    mine = jnp.stack([jnp.sum(q32 * q32, axis=1), jnp.sum(k32 * k32, axis=1), label])
    slots = jnp.where(
        jnp.arange(4)[None, :, None] == me, mine[:, None, :], 0.0
    )
    every = lax.psum(slots, ("ctx", "row"))
    order = jnp.stack([me, me ^ 1, me ^ 2, me ^ 3])
    pick = (order[:, None] == jnp.arange(4)[None, :])[None, :, :, None]
    turned = jnp.sum(jnp.where(pick, every[:, None, :, :], 0.0), axis=2).reshape(3, tokens)
    clip_of = turned[2].astype(jnp.int32)
    labels = jnp.arange(CLIPS, dtype=jnp.int32)
    starts = jnp.sum((clip_of[:, None] < labels[None, :]).astype(jnp.int32), axis=0)
    index = (order[:, None] * rows + jnp.arange(rows)[None, :]).reshape(tokens)
    offsets = index - lookup(starts, clip_of)
    angles = angles_of(offsets, clip_of, clip_grid)
    cosine, sine = jnp.cos(angles), jnp.sin(angles)
    q_scale = lax.rsqrt(turned[0, :rows] / D + EPSILON)[:, None]
    k_scale = lax.rsqrt(turned[1] / D + EPSILON)[:, None]
    tables = (
        cosine[:rows] * q_scale,
        sine[:rows] * q_scale,
        cosine * k_scale,
        sine * k_scale,
    )

    def flip(gain):
        return gain.reshape(-1, 2)[:, ::-1].reshape(1, width)

    gains = (gain_q[None, :], flip(gain_q), gain_k[None, :], flip(gain_k))
    at_row = jnp.arange(HD)[:, None]
    at_column = jnp.arange(HD)[None, :]
    swap = jnp.where(
        at_row == (at_column ^ 1), jnp.where(at_column % 2 == 0, -1.0, 1.0), 0.0
    ).astype(jnp.bfloat16)
    clips = (clip_of[:rows, None], clip_of[None, :])

    outs, first = [], 0
    for heads, piece in zip(GROUPS, far):
        passed = lax.ppermute(piece, "ctx", BESIDE)
        outs.append(
            attend(
                first, heads, queries,
                ((keys, keys_beside), (values, values_beside)),
                (piece, passed), tables, gains, swap, clips,
            )
        )
        first += heads
    return jnp.concatenate(outs, axis=1)


def spin(matrix, offsets, clip_of, clip_grid, head_size):
    row_count = matrix.shape[0]
    sixth_part = head_size // 6
    first_dims = head_size - 4 * sixth_part
    first_freqs = 1.0 / ROTARY_BASE ** (
        jnp.arange(0, first_dims, 2, dtype=jnp.float32) / first_dims
    )
    other_freqs = 1.0 / ROTARY_BASE ** (
        jnp.arange(0, 2 * sixth_part, 2, dtype=jnp.float32) / (2 * sixth_part)
    )
    heights = lookup(clip_grid[:, 0], clip_of)
    widths = lookup(clip_grid[:, 1], clip_of)
    frame_pos = offsets // (heights * widths)
    line_pos = offsets // widths % heights
    column_pos = offsets % widths
    angles = jnp.concatenate(
        [
            frame_pos.astype(jnp.float32)[:, None] * first_freqs[None, :],
            line_pos.astype(jnp.float32)[:, None] * other_freqs[None, :],
            column_pos.astype(jnp.float32)[:, None] * other_freqs[None, :],
        ],
        axis=1,
    )
    cosine = jnp.repeat(jnp.cos(angles), 2, axis=1)
    sine_table = jnp.repeat(jnp.sin(angles), 2, axis=1)
    feature = jnp.arange(head_size, dtype=jnp.int32)
    is_even = (feature % 2 == 0)[None, None, :]
    head_view = matrix.reshape(row_count, -1, head_size)
    partner = jnp.where(is_even, -jnp.roll(head_view, -1, axis=2), jnp.roll(head_view, 1, axis=2))
    turned = head_view * cosine[:, None, :] + partner * sine_table[:, None, :]
    return turned.reshape(row_count, -1)


def on_any(queries, keys, values, gain_q, gain_k, clip_ids, clip_grid):
    rows_here, width_here = queries.shape
    heads_here = width_here // HD
    score_scale = 1.0 / math.sqrt(HD)
    query_wide = queries.astype(jnp.float32)
    key_wide = keys.astype(jnp.float32)
    squares = lax.psum(
        (jnp.sum(query_wide * query_wide, axis=1), jnp.sum(key_wide * key_wide, axis=1)), "row"
    )
    query_scale = lax.rsqrt(squares[0] / D + EPSILON)
    key_scale = lax.rsqrt(squares[1] / D + EPSILON)
    labels = jnp.arange(CLIPS, dtype=jnp.int32)
    local_counts = jnp.sum((clip_ids[:, None] == labels[None, :]).astype(jnp.int32), axis=0)
    totals = lax.psum(local_counts, "ctx")
    starts = jnp.cumsum(totals) - totals
    first_row = lax.axis_index("ctx") * rows_here
    offsets = first_row + jnp.arange(rows_here, dtype=jnp.int32) - lookup(starts, clip_ids)
    query_rot = spin(
        query_wide * query_scale[:, None] * gain_q[None, :], offsets, clip_ids, clip_grid, HD
    ).astype(jnp.bfloat16)
    query_heads = query_rot.reshape(rows_here, heads_here, HD)
    key_send = spin(
        key_wide * key_scale[:, None] * gain_k[None, :], offsets, clip_ids, clip_grid, HD
    ).astype(jnp.bfloat16)
    initial = (
        jnp.full((heads_here, rows_here), NEGATIVE, jnp.float32),
        jnp.zeros((heads_here, rows_here), jnp.float32),
        jnp.zeros((rows_here, heads_here, HD), jnp.float32),
    )
    running = initial
    piece_start = jnp.int32(0)
    key_piece = lax.all_gather(key_send, "ctx", axis=0, tiled=True)
    value_piece = lax.all_gather(values, "ctx", axis=0, tiled=True)
    row_count = key_piece.shape[0]
    block_rows = min(row_count, block_limit)
    for block_first in range(0, row_count, block_rows):
        block_size = min(block_rows, row_count - block_first)
        fold_key_rows = key_piece[block_first : block_first + block_size]
        fold_value_rows = value_piece[block_first : block_first + block_size]
        key_index = piece_start + block_first + jnp.arange(fold_key_rows.shape[0], dtype=jnp.int32)
        key_key_clips = (
            jnp.sum((starts[None, :] <= key_index[:, None]).astype(jnp.int32), axis=1) - 1
        )
        peak_old, total_old, summed_old = running
        key_view = fold_key_rows.reshape(fold_key_rows.shape[0], heads_here, HD)
        value_view = fold_value_rows.reshape(fold_value_rows.shape[0], heads_here, HD)
        scores = (
            jnp.einsum("qhd,khd->hqk", query_heads, key_view, preferred_element_type=jnp.float32)
            * score_scale
        )
        same = clip_ids[:, None] == key_key_clips[None, :]
        masked = jnp.where(same[None, :, :], scores, NEGATIVE)
        peak_new = jnp.maximum(peak_old, jnp.max(masked, axis=2))
        weights = jnp.where(same[None, :, :], jnp.exp(masked - peak_new[:, :, None]), 0.0)
        factor = jnp.exp(peak_old - peak_new)
        total_new = total_old * factor + jnp.sum(weights, axis=2)
        summed = summed_old * jnp.transpose(factor)[:, :, None] + jnp.einsum(
            "hqk,khd->qhd",
            weights.astype(jnp.bfloat16),
            value_view,
            preferred_element_type=jnp.float32,
        )
        running = (peak_new, total_new, summed)
    attended = running[2] / jnp.transpose(running[1])[:, :, None]
    return attended.reshape(rows_here, width_here).astype(jnp.bfloat16)


def solution(mesh):
    in_specs = (
        P(("batch", "ctx"), "row"),
        P(("batch", "ctx"), "row"),
        P(("batch", "ctx"), "row"),
        P("row"),
        P("row"),
        P(("batch", "ctx")),
        P("batch", None),
    )
    out_specs = P(("batch", "ctx"), "row")
    return jax.shard_map(
        on_device if mesh.shape["ctx"] == 4 else on_any,
        mesh=mesh, in_specs=in_specs, out_specs=out_specs, check_vma=False
    )
```

```python
import functools
import math

import jax
import jax.numpy as jnp
from jax import lax
from jax.experimental import pallas as pl
from jax.experimental.pallas import tpu as pltpu
from jax.sharding import PartitionSpec as P

HD = 128
D = 5120
CLIPS = 4
EPSILON = 1e-06
NEGATIVE = -1e30
ROTARY_BASE = 10000.0
block_limit = 1024
GROUP_HEADS = 4
ACROSS = ((0, 2), (1, 3), (2, 0), (3, 1))
BESIDE = ((0, 1), (1, 0), (2, 3), (3, 2))


def lookup(lookup_table, positions):
    labels = jnp.arange(lookup_table.shape[0], dtype=jnp.int32)
    return jnp.sum(
        jnp.where(positions[:, None] == labels[None, :], lookup_table[None, :], 0), axis=1
    )


def angles_of(offsets, clip_of, clip_grid):
    sixth_part = HD // 6
    first_dims = HD - 4 * sixth_part
    first_freqs = 1.0 / ROTARY_BASE ** (
        jnp.arange(0, first_dims, 2, dtype=jnp.float32) / first_dims
    )
    other_freqs = 1.0 / ROTARY_BASE ** (
        jnp.arange(0, 2 * sixth_part, 2, dtype=jnp.float32) / (2 * sixth_part)
    )
    heights = lookup(clip_grid[:, 0], clip_of)
    widths = lookup(clip_grid[:, 1], clip_of)
    frame_pos = (offsets // (heights * widths)).astype(jnp.float32)[:, None]
    line_pos = (offsets // widths % heights).astype(jnp.float32)[:, None]
    column_pos = (offsets % widths).astype(jnp.float32)[:, None]
    freqs = jnp.repeat(jnp.concatenate([first_freqs, other_freqs, other_freqs]), 2)[None, :]
    feature = jnp.arange(HD, dtype=jnp.int32)[None, :]
    position = jnp.where(
        feature < first_dims,
        frame_pos,
        jnp.where(feature < first_dims + 2 * sixth_part, line_pos, column_pos),
    )
    return position * freqs


def turn(x, gain, gain_s, swap, cosine, sine):
    other = jnp.dot(x, swap, preferred_element_type=jnp.float32)
    return ((x.astype(jnp.float32) * gain) * cosine + (other * gain_s) * sine).astype(jnp.bfloat16)


def flip(gain):
    size = gain.shape[1]
    even = lax.broadcasted_iota(jnp.int32, gain.shape, 1) % 2 == 0
    return jnp.where(even, pltpu.roll(gain, size - 1, 1), pltpu.roll(gain, 1, 1))


def signed_swap():
    at_row = lax.broadcasted_iota(jnp.int32, (HD, HD), 0)
    at_column = lax.broadcasted_iota(jnp.int32, (HD, HD), 1)
    sign = jnp.where(at_column % 2 == 0, -1.0, 1.0)
    return jnp.where(at_row == (at_column ^ 1), sign, 0.0).astype(jnp.bfloat16)


def attend_kernel(heads, scale, q_ref, k0, k1, f0, f1, v0, v1, cq, sq, ck, sk, gq, gk, qc, kc, o_ref, bias):
    rows = q_ref.shape[0]
    swap = signed_swap()
    bias[...] = jnp.where(qc[...] == kc[...], 0.0, NEGATIVE).astype(jnp.float32)
    for h in range(heads):
        at = slice(h * HD, (h + 1) * HD)
        gain_k = gk[:, at]
        flip_k = flip(gain_k)
        pieces = (k0[:, at], k1[:, at], f0[0, :, at], f1[0, :, at])
        keys = jnp.concatenate(
            [
                turn(x, gain_k, flip_k, swap, ck[i * rows : (i + 1) * rows], sk[i * rows : (i + 1) * rows])
                for i, x in enumerate(pieces)
            ],
            axis=0,
        )
        gain_q = gq[:, at]
        q = turn(q_ref[:, at], gain_q, flip(gain_q), swap, cq[...], sq[...])
        scores = (
            lax.dot_general(q, keys, (((1,), (1,)), ((), ())), preferred_element_type=jnp.float32)
            + bias[...]
        )
        peak = jnp.max(scores, axis=1, keepdims=True)
        weights = jnp.exp2((scores - peak) * scale)
        total = jnp.sum(weights, axis=1, keepdims=True)
        values = jnp.concatenate([v0[:, at], v1[:, at], f0[1, :, at], f1[1, :, at]], axis=0)
        out = jnp.dot(weights.astype(jnp.bfloat16), values, preferred_element_type=jnp.float32)
        o_ref[:, at] = (out / total).astype(o_ref.dtype)


def attend(group, heads, q, near, far, tables, gains, clips):
    rows = q.shape[0]
    cq, sq, ck, sk = tables
    qc, kc = clips
    tokens = ck.shape[0]
    whole = lambda a: pl.BlockSpec(a.shape, lambda i: (0,) * a.ndim)
    wide = pl.BlockSpec((rows, heads * HD), lambda i: (0, group))
    gain_spec = pl.BlockSpec((1, heads * HD), lambda i: (0, group))
    kernel = functools.partial(attend_kernel, heads, math.log2(math.e) / math.sqrt(HD))
    return pl.pallas_call(
        kernel,
        grid=(1,),
        out_shape=jax.ShapeDtypeStruct((rows, heads * HD), jnp.bfloat16),
        in_specs=[wide, wide, wide, whole(far[0]), whole(far[1]), wide, wide]
        + [whole(a) for a in (cq, sq, ck, sk)]
        + [gain_spec] * 2
        + [whole(qc), whole(kc)],
        out_specs=pl.BlockSpec((rows, heads * HD), lambda i: (0, 0)),
        scratch_shapes=[pltpu.VMEM((rows, tokens), jnp.float32)],
        compiler_params=pltpu.CompilerParams(vmem_limit_bytes=40 * 1024 * 1024),
        cost_estimate=pl.CostEstimate(
            flops=4 * heads * rows * tokens * HD * 4,
            bytes_accessed=heads * tokens * HD * 4 + tokens * HD * 8,
            transcendentals=heads * rows * tokens,
        ),
    )(q, near[0][0], near[0][1], *far, near[1][0], near[1][1], cq, sq, ck, sk, *gains, qc, kc)


def deal_kernel(groups, k_ref, v_ref, *refs):
    outs, sems = refs[:groups], refs[groups]
    wide = outs[0].shape[2]
    copies = []
    for g in range(groups):
        at = slice(g * wide, (g + 1) * wide)
        for i, ref in enumerate((k_ref, v_ref)):
            copies.append(pltpu.make_async_copy(ref.at[:, at], outs[g].at[i], sems.at[2 * g + i]))
    for copy in copies:
        copy.start()
    for copy in copies:
        copy.wait()


def deal(keys, values, heads):
    rows, width = keys.shape
    groups = width // (heads * HD)
    spec = pl.BlockSpec(memory_space=pl.ANY)
    return pl.pallas_call(
        functools.partial(deal_kernel, groups),
        out_shape=[jax.ShapeDtypeStruct((2, rows, heads * HD), keys.dtype)] * groups,
        in_specs=[spec, spec],
        out_specs=[spec] * groups,
        scratch_shapes=[pltpu.SemaphoreType.DMA((2 * groups,))],
    )(keys, values)


def on_device(queries, keys, values, gain_q, gain_k, clip_ids, clip_grid):
    rows, width = queries.shape
    me = lax.axis_index("ctx")
    tokens = 4 * rows

    q32, k32 = queries.astype(jnp.float32), keys.astype(jnp.float32)
    label = jnp.where(lax.axis_index("row") == 0, clip_ids, 0).astype(jnp.float32)
    mine = jnp.stack([jnp.sum(q32 * q32, axis=1), jnp.sum(k32 * k32, axis=1), label])
    mine_across = lax.ppermute(mine, "ctx", ACROSS)
    heads = GROUP_HEADS
    sends = deal(keys, values, heads)
    far = [lax.ppermute(piece, "ctx", ACROSS) for piece in sends]
    keys_beside = lax.ppermute(keys, "ctx", BESIDE)
    values_beside = lax.ppermute(values, "ctx", BESIDE)
    pair = jnp.stack([mine, mine_across])
    pair_beside = lax.ppermute(pair, "ctx", BESIDE)
    turned = lax.psum(
        jnp.stack([pair[0], pair_beside[0], pair[1], pair_beside[1]], axis=1), "row"
    ).reshape(3, tokens)
    order = jnp.stack([me, me ^ 1, me ^ 2, me ^ 3])
    clip_of = turned[2].astype(jnp.int32)
    labels = jnp.arange(CLIPS, dtype=jnp.int32)
    starts = jnp.sum((clip_of[:, None] < labels[None, :]).astype(jnp.int32), axis=0)
    index = (order[:, None] * rows + jnp.arange(rows)[None, :]).reshape(tokens)
    offsets = index - lookup(starts, clip_of)
    angles = angles_of(offsets, clip_of, clip_grid)
    cosine, sine = jnp.cos(angles), jnp.sin(angles)
    q_scale = lax.rsqrt(turned[0, :rows] / D + EPSILON)[:, None]
    k_scale = lax.rsqrt(turned[1] / D + EPSILON)[:, None]
    tables = (
        cosine[:rows] * q_scale,
        sine[:rows] * q_scale,
        cosine * k_scale,
        sine * k_scale,
    )

    gains = (gain_q[None, :], gain_k[None, :])
    clips = (clip_of[:rows, None], clip_of[None, :])

    outs = []
    for group, piece in enumerate(far):
        passed = lax.ppermute(piece, "ctx", BESIDE)
        outs.append(
            attend(
                group, heads, queries,
                ((keys, keys_beside), (values, values_beside)),
                (piece, passed), tables, gains, clips,
            )
        )
    return jnp.concatenate(outs, axis=1)


def spin(matrix, offsets, clip_of, clip_grid, head_size):
    row_count = matrix.shape[0]
    sixth_part = head_size // 6
    first_dims = head_size - 4 * sixth_part
    first_freqs = 1.0 / ROTARY_BASE ** (
        jnp.arange(0, first_dims, 2, dtype=jnp.float32) / first_dims
    )
    other_freqs = 1.0 / ROTARY_BASE ** (
        jnp.arange(0, 2 * sixth_part, 2, dtype=jnp.float32) / (2 * sixth_part)
    )
    heights = lookup(clip_grid[:, 0], clip_of)
    widths = lookup(clip_grid[:, 1], clip_of)
    frame_pos = offsets // (heights * widths)
    line_pos = offsets // widths % heights
    column_pos = offsets % widths
    angles = jnp.concatenate(
        [
            frame_pos.astype(jnp.float32)[:, None] * first_freqs[None, :],
            line_pos.astype(jnp.float32)[:, None] * other_freqs[None, :],
            column_pos.astype(jnp.float32)[:, None] * other_freqs[None, :],
        ],
        axis=1,
    )
    cosine = jnp.repeat(jnp.cos(angles), 2, axis=1)
    sine_table = jnp.repeat(jnp.sin(angles), 2, axis=1)
    feature = jnp.arange(head_size, dtype=jnp.int32)
    is_even = (feature % 2 == 0)[None, None, :]
    head_view = matrix.reshape(row_count, -1, head_size)
    partner = jnp.where(is_even, -jnp.roll(head_view, -1, axis=2), jnp.roll(head_view, 1, axis=2))
    turned = head_view * cosine[:, None, :] + partner * sine_table[:, None, :]
    return turned.reshape(row_count, -1)


def on_any(queries, keys, values, gain_q, gain_k, clip_ids, clip_grid):
    rows_here, width_here = queries.shape
    heads_here = width_here // HD
    score_scale = 1.0 / math.sqrt(HD)
    query_wide = queries.astype(jnp.float32)
    key_wide = keys.astype(jnp.float32)
    squares = lax.psum(
        (jnp.sum(query_wide * query_wide, axis=1), jnp.sum(key_wide * key_wide, axis=1)), "row"
    )
    query_scale = lax.rsqrt(squares[0] / D + EPSILON)
    key_scale = lax.rsqrt(squares[1] / D + EPSILON)
    labels = jnp.arange(CLIPS, dtype=jnp.int32)
    local_counts = jnp.sum((clip_ids[:, None] == labels[None, :]).astype(jnp.int32), axis=0)
    totals = lax.psum(local_counts, "ctx")
    starts = jnp.cumsum(totals) - totals
    first_row = lax.axis_index("ctx") * rows_here
    offsets = first_row + jnp.arange(rows_here, dtype=jnp.int32) - lookup(starts, clip_ids)
    query_rot = spin(
        query_wide * query_scale[:, None] * gain_q[None, :], offsets, clip_ids, clip_grid, HD
    ).astype(jnp.bfloat16)
    query_heads = query_rot.reshape(rows_here, heads_here, HD)
    key_send = spin(
        key_wide * key_scale[:, None] * gain_k[None, :], offsets, clip_ids, clip_grid, HD
    ).astype(jnp.bfloat16)
    initial = (
        jnp.full((heads_here, rows_here), NEGATIVE, jnp.float32),
        jnp.zeros((heads_here, rows_here), jnp.float32),
        jnp.zeros((rows_here, heads_here, HD), jnp.float32),
    )
    running = initial
    piece_start = jnp.int32(0)
    key_piece = lax.all_gather(key_send, "ctx", axis=0, tiled=True)
    value_piece = lax.all_gather(values, "ctx", axis=0, tiled=True)
    row_count = key_piece.shape[0]
    block_rows = min(row_count, block_limit)
    for block_first in range(0, row_count, block_rows):
        block_size = min(block_rows, row_count - block_first)
        fold_key_rows = key_piece[block_first : block_first + block_size]
        fold_value_rows = value_piece[block_first : block_first + block_size]
        key_index = piece_start + block_first + jnp.arange(fold_key_rows.shape[0], dtype=jnp.int32)
        key_key_clips = (
            jnp.sum((starts[None, :] <= key_index[:, None]).astype(jnp.int32), axis=1) - 1
        )
        peak_old, total_old, summed_old = running
        key_view = fold_key_rows.reshape(fold_key_rows.shape[0], heads_here, HD)
        value_view = fold_value_rows.reshape(fold_value_rows.shape[0], heads_here, HD)
        scores = (
            jnp.einsum("qhd,khd->hqk", query_heads, key_view, preferred_element_type=jnp.float32)
            * score_scale
        )
        same = clip_ids[:, None] == key_key_clips[None, :]
        masked = jnp.where(same[None, :, :], scores, NEGATIVE)
        peak_new = jnp.maximum(peak_old, jnp.max(masked, axis=2))
        weights = jnp.where(same[None, :, :], jnp.exp(masked - peak_new[:, :, None]), 0.0)
        factor = jnp.exp(peak_old - peak_new)
        total_new = total_old * factor + jnp.sum(weights, axis=2)
        summed = summed_old * jnp.transpose(factor)[:, :, None] + jnp.einsum(
            "hqk,khd->qhd",
            weights.astype(jnp.bfloat16),
            value_view,
            preferred_element_type=jnp.float32,
        )
        running = (peak_new, total_new, summed)
    attended = running[2] / jnp.transpose(running[1])[:, :, None]
    return attended.reshape(rows_here, width_here).astype(jnp.bfloat16)


def solution(mesh):
    in_specs = (
        P(("batch", "ctx"), "row"),
        P(("batch", "ctx"), "row"),
        P(("batch", "ctx"), "row"),
        P("row"),
        P("row"),
        P(("batch", "ctx")),
        P("batch", None),
    )
    out_specs = P(("batch", "ctx"), "row")
    return jax.shard_map(
        on_device if mesh.shape["ctx"] == 4 else on_any,
        mesh=mesh, in_specs=in_specs, out_specs=out_specs, check_vma=False
    )
```

```python
import functools
import math

import jax
import jax.numpy as jnp
from jax import lax
from jax.experimental import pallas as pl
from jax.experimental.pallas import tpu as pltpu
from jax.sharding import PartitionSpec as P

HD = 128
D = 5120
CLIPS = 4
EPSILON = 1e-06
NEGATIVE = -1e30
ROTARY_BASE = 10000.0
block_limit = 1024
GROUP_HEADS = 4
ACROSS = ((0, 2), (1, 3), (2, 0), (3, 1))
BESIDE = ((0, 1), (1, 0), (2, 3), (3, 2))


def lookup(lookup_table, positions):
    labels = jnp.arange(lookup_table.shape[0], dtype=jnp.int32)
    return jnp.sum(
        jnp.where(positions[:, None] == labels[None, :], lookup_table[None, :], 0), axis=1
    )


def angles_of(offsets, clip_of, clip_grid):
    sixth_part = HD // 6
    first_dims = HD - 4 * sixth_part
    first_freqs = 1.0 / ROTARY_BASE ** (
        jnp.arange(0, first_dims, 2, dtype=jnp.float32) / first_dims
    )
    other_freqs = 1.0 / ROTARY_BASE ** (
        jnp.arange(0, 2 * sixth_part, 2, dtype=jnp.float32) / (2 * sixth_part)
    )
    heights = lookup(clip_grid[:, 0], clip_of)
    widths = lookup(clip_grid[:, 1], clip_of)
    frame_pos = (offsets // (heights * widths)).astype(jnp.float32)[:, None]
    line_pos = (offsets // widths % heights).astype(jnp.float32)[:, None]
    column_pos = (offsets % widths).astype(jnp.float32)[:, None]
    freqs = jnp.repeat(jnp.concatenate([first_freqs, other_freqs, other_freqs]), 2)[None, :]
    feature = jnp.arange(HD, dtype=jnp.int32)[None, :]
    position = jnp.where(
        feature < first_dims,
        frame_pos,
        jnp.where(feature < first_dims + 2 * sixth_part, line_pos, column_pos),
    )
    return position * freqs


def turn(x, gain, gain_s, swap, cosine, sine):
    other = jnp.dot(x, swap, preferred_element_type=jnp.float32)
    return ((x.astype(jnp.float32) * gain) * cosine + (other * gain_s) * sine).astype(jnp.bfloat16)


def flip(gain):
    size = gain.shape[1]
    even = lax.broadcasted_iota(jnp.int32, gain.shape, 1) % 2 == 0
    return jnp.where(even, pltpu.roll(gain, size - 1, 1), pltpu.roll(gain, 1, 1))


def signed_swap():
    at_row = lax.broadcasted_iota(jnp.int32, (HD, HD), 0)
    at_column = lax.broadcasted_iota(jnp.int32, (HD, HD), 1)
    sign = jnp.where(at_column % 2 == 0, -1.0, 1.0)
    return jnp.where(at_row == (at_column ^ 1), sign, 0.0).astype(jnp.bfloat16)


def attend_kernel(heads, scale, q_ref, k0, k1, f0, f1, v0, v1, cq, sq, ck, sk, gq, gk, qc, kc, o_ref, bias):
    rows = q_ref.shape[0]
    swap = signed_swap()
    bias[...] = jnp.where(qc[...] == kc[...], 0.0, NEGATIVE).astype(jnp.float32)
    for h in range(heads):
        at = slice(h * HD, (h + 1) * HD)
        gain_k = gk[:, at]
        flip_k = flip(gain_k)
        pieces = (k0[:, at], k1[:, at], f0[0, :, at], f1[0, :, at])
        keys = jnp.concatenate(
            [
                turn(x, gain_k, flip_k, swap, ck[i * rows : (i + 1) * rows], sk[i * rows : (i + 1) * rows])
                for i, x in enumerate(pieces)
            ],
            axis=0,
        )
        gain_q = gq[:, at]
        q = turn(q_ref[:, at], gain_q, flip(gain_q), swap, cq[...], sq[...])
        scores = (
            lax.dot_general(q, keys, (((1,), (1,)), ((), ())), preferred_element_type=jnp.float32)
            + bias[...]
        )
        peak = jnp.max(scores, axis=1, keepdims=True)
        weights = jnp.exp2((scores - peak) * scale)
        total = jnp.sum(weights, axis=1, keepdims=True)
        values = jnp.concatenate([v0[:, at], v1[:, at], f0[1, :, at], f1[1, :, at]], axis=0)
        out = jnp.dot(weights.astype(jnp.bfloat16), values, preferred_element_type=jnp.float32)
        o_ref[:, at] = (out / total).astype(o_ref.dtype)


def attend(group, heads, q, near, far, tables, gains, clips):
    rows = q.shape[0]
    cq, sq, ck, sk = tables
    qc, kc = clips
    tokens = ck.shape[0]
    whole = lambda a: pl.BlockSpec(a.shape, lambda i: (0,) * a.ndim)
    wide = pl.BlockSpec((rows, heads * HD), lambda i: (0, group))
    gain_spec = pl.BlockSpec((1, heads * HD), lambda i: (0, group))
    kernel = functools.partial(attend_kernel, heads, math.log2(math.e) / math.sqrt(HD))
    return pl.pallas_call(
        kernel,
        grid=(1,),
        out_shape=jax.ShapeDtypeStruct((rows, heads * HD), jnp.bfloat16),
        in_specs=[wide, wide, wide, whole(far[0]), whole(far[1]), wide, wide]
        + [whole(a) for a in (cq, sq, ck, sk)]
        + [gain_spec] * 2
        + [whole(qc), whole(kc)],
        out_specs=pl.BlockSpec((rows, heads * HD), lambda i: (0, 0)),
        scratch_shapes=[pltpu.VMEM((rows, tokens), jnp.float32)],
        compiler_params=pltpu.CompilerParams(vmem_limit_bytes=40 * 1024 * 1024),
        cost_estimate=pl.CostEstimate(
            flops=4 * heads * rows * tokens * HD * 4,
            bytes_accessed=heads * tokens * HD * 4 + tokens * HD * 8,
            transcendentals=heads * rows * tokens,
        ),
    )(q, near[0][0], near[0][1], *far, near[1][0], near[1][1], cq, sq, ck, sk, *gains, qc, kc)


def deal_kernel(k_ref, v_ref, *outs):
    wide = outs[0].shape[2]
    for g, out in enumerate(outs):
        at = slice(g * wide, (g + 1) * wide)
        out[0] = k_ref[:, at]
        out[1] = v_ref[:, at]


def deal(keys, values, heads):
    rows, width = keys.shape
    groups = width // (heads * HD)
    return pl.pallas_call(
        deal_kernel,
        out_shape=[jax.ShapeDtypeStruct((2, rows, heads * HD), keys.dtype)] * groups,
        compiler_params=pltpu.CompilerParams(vmem_limit_bytes=24 * 1024 * 1024),
    )(keys, values)


def on_device(queries, keys, values, gain_q, gain_k, clip_ids, clip_grid):
    rows, width = queries.shape
    me = lax.axis_index("ctx")
    tokens = 4 * rows

    q32, k32 = queries.astype(jnp.float32), keys.astype(jnp.float32)
    label = jnp.where(lax.axis_index("row") == 0, clip_ids, 0).astype(jnp.float32)
    mine = jnp.stack([jnp.sum(q32 * q32, axis=1), jnp.sum(k32 * k32, axis=1), label])
    mine_across = lax.ppermute(mine, "ctx", ACROSS)
    heads = GROUP_HEADS
    sends = deal(keys, values, heads)
    far = [lax.ppermute(piece, "ctx", ACROSS) for piece in sends]
    keys_beside = lax.ppermute(keys, "ctx", BESIDE)
    values_beside = lax.ppermute(values, "ctx", BESIDE)
    pair = jnp.stack([mine, mine_across])
    pair_beside = lax.ppermute(pair, "ctx", BESIDE)
    turned = lax.psum(
        jnp.stack([pair[0], pair_beside[0], pair[1], pair_beside[1]], axis=1), "row"
    ).reshape(3, tokens)
    order = jnp.stack([me, me ^ 1, me ^ 2, me ^ 3])
    clip_of = turned[2].astype(jnp.int32)
    labels = jnp.arange(CLIPS, dtype=jnp.int32)
    starts = jnp.sum((clip_of[:, None] < labels[None, :]).astype(jnp.int32), axis=0)
    index = (order[:, None] * rows + jnp.arange(rows)[None, :]).reshape(tokens)
    offsets = index - lookup(starts, clip_of)
    angles = angles_of(offsets, clip_of, clip_grid)
    cosine, sine = jnp.cos(angles), jnp.sin(angles)
    q_scale = lax.rsqrt(turned[0, :rows] / D + EPSILON)[:, None]
    k_scale = lax.rsqrt(turned[1] / D + EPSILON)[:, None]
    tables = (
        cosine[:rows] * q_scale,
        sine[:rows] * q_scale,
        cosine * k_scale,
        sine * k_scale,
    )

    gains = (gain_q[None, :], gain_k[None, :])
    clips = (clip_of[:rows, None], clip_of[None, :])

    outs = []
    for group, piece in enumerate(far):
        if group >= 2:
            piece, outs[group - 2] = lax.optimization_barrier((piece, outs[group - 2]))
        passed = lax.ppermute(piece, "ctx", BESIDE)
        outs.append(
            attend(
                group, heads, queries,
                ((keys, keys_beside), (values, values_beside)),
                (piece, passed), tables, gains, clips,
            )
        )
    return jnp.concatenate(outs, axis=1)


def spin(matrix, offsets, clip_of, clip_grid, head_size):
    row_count = matrix.shape[0]
    sixth_part = head_size // 6
    first_dims = head_size - 4 * sixth_part
    first_freqs = 1.0 / ROTARY_BASE ** (
        jnp.arange(0, first_dims, 2, dtype=jnp.float32) / first_dims
    )
    other_freqs = 1.0 / ROTARY_BASE ** (
        jnp.arange(0, 2 * sixth_part, 2, dtype=jnp.float32) / (2 * sixth_part)
    )
    heights = lookup(clip_grid[:, 0], clip_of)
    widths = lookup(clip_grid[:, 1], clip_of)
    frame_pos = offsets // (heights * widths)
    line_pos = offsets // widths % heights
    column_pos = offsets % widths
    angles = jnp.concatenate(
        [
            frame_pos.astype(jnp.float32)[:, None] * first_freqs[None, :],
            line_pos.astype(jnp.float32)[:, None] * other_freqs[None, :],
            column_pos.astype(jnp.float32)[:, None] * other_freqs[None, :],
        ],
        axis=1,
    )
    cosine = jnp.repeat(jnp.cos(angles), 2, axis=1)
    sine_table = jnp.repeat(jnp.sin(angles), 2, axis=1)
    feature = jnp.arange(head_size, dtype=jnp.int32)
    is_even = (feature % 2 == 0)[None, None, :]
    head_view = matrix.reshape(row_count, -1, head_size)
    partner = jnp.where(is_even, -jnp.roll(head_view, -1, axis=2), jnp.roll(head_view, 1, axis=2))
    turned = head_view * cosine[:, None, :] + partner * sine_table[:, None, :]
    return turned.reshape(row_count, -1)


def on_any(queries, keys, values, gain_q, gain_k, clip_ids, clip_grid):
    rows_here, width_here = queries.shape
    heads_here = width_here // HD
    score_scale = 1.0 / math.sqrt(HD)
    query_wide = queries.astype(jnp.float32)
    key_wide = keys.astype(jnp.float32)
    squares = lax.psum(
        (jnp.sum(query_wide * query_wide, axis=1), jnp.sum(key_wide * key_wide, axis=1)), "row"
    )
    query_scale = lax.rsqrt(squares[0] / D + EPSILON)
    key_scale = lax.rsqrt(squares[1] / D + EPSILON)
    labels = jnp.arange(CLIPS, dtype=jnp.int32)
    local_counts = jnp.sum((clip_ids[:, None] == labels[None, :]).astype(jnp.int32), axis=0)
    totals = lax.psum(local_counts, "ctx")
    starts = jnp.cumsum(totals) - totals
    first_row = lax.axis_index("ctx") * rows_here
    offsets = first_row + jnp.arange(rows_here, dtype=jnp.int32) - lookup(starts, clip_ids)
    query_rot = spin(
        query_wide * query_scale[:, None] * gain_q[None, :], offsets, clip_ids, clip_grid, HD
    ).astype(jnp.bfloat16)
    query_heads = query_rot.reshape(rows_here, heads_here, HD)
    key_send = spin(
        key_wide * key_scale[:, None] * gain_k[None, :], offsets, clip_ids, clip_grid, HD
    ).astype(jnp.bfloat16)
    initial = (
        jnp.full((heads_here, rows_here), NEGATIVE, jnp.float32),
        jnp.zeros((heads_here, rows_here), jnp.float32),
        jnp.zeros((rows_here, heads_here, HD), jnp.float32),
    )
    running = initial
    piece_start = jnp.int32(0)
    key_piece = lax.all_gather(key_send, "ctx", axis=0, tiled=True)
    value_piece = lax.all_gather(values, "ctx", axis=0, tiled=True)
    row_count = key_piece.shape[0]
    block_rows = min(row_count, block_limit)
    for block_first in range(0, row_count, block_rows):
        block_size = min(block_rows, row_count - block_first)
        fold_key_rows = key_piece[block_first : block_first + block_size]
        fold_value_rows = value_piece[block_first : block_first + block_size]
        key_index = piece_start + block_first + jnp.arange(fold_key_rows.shape[0], dtype=jnp.int32)
        key_key_clips = (
            jnp.sum((starts[None, :] <= key_index[:, None]).astype(jnp.int32), axis=1) - 1
        )
        peak_old, total_old, summed_old = running
        key_view = fold_key_rows.reshape(fold_key_rows.shape[0], heads_here, HD)
        value_view = fold_value_rows.reshape(fold_value_rows.shape[0], heads_here, HD)
        scores = (
            jnp.einsum("qhd,khd->hqk", query_heads, key_view, preferred_element_type=jnp.float32)
            * score_scale
        )
        same = clip_ids[:, None] == key_key_clips[None, :]
        masked = jnp.where(same[None, :, :], scores, NEGATIVE)
        peak_new = jnp.maximum(peak_old, jnp.max(masked, axis=2))
        weights = jnp.where(same[None, :, :], jnp.exp(masked - peak_new[:, :, None]), 0.0)
        factor = jnp.exp(peak_old - peak_new)
        total_new = total_old * factor + jnp.sum(weights, axis=2)
        summed = summed_old * jnp.transpose(factor)[:, :, None] + jnp.einsum(
            "hqk,khd->qhd",
            weights.astype(jnp.bfloat16),
            value_view,
            preferred_element_type=jnp.float32,
        )
        running = (peak_new, total_new, summed)
    attended = running[2] / jnp.transpose(running[1])[:, :, None]
    return attended.reshape(rows_here, width_here).astype(jnp.bfloat16)


def solution(mesh):
    in_specs = (
        P(("batch", "ctx"), "row"),
        P(("batch", "ctx"), "row"),
        P(("batch", "ctx"), "row"),
        P("row"),
        P("row"),
        P(("batch", "ctx")),
        P("batch", None),
    )
    out_specs = P(("batch", "ctx"), "row")
    return jax.shard_map(
        on_device if mesh.shape["ctx"] == 4 else on_any,
        mesh=mesh, in_specs=in_specs, out_specs=out_specs, check_vma=False
    )
```

```python
import functools
import math

import jax
import jax.numpy as jnp
from jax import lax
from jax.experimental import pallas as pl
from jax.experimental.pallas import tpu as pltpu
from jax.sharding import PartitionSpec as P

HD = 128
D = 5120
CLIPS = 4
EPSILON = 1e-06
NEGATIVE = -1e30
ROTARY_BASE = 10000.0
block_limit = 1024

ROWS = 192
CHIP = 2 * ROWS
MOST = 480
NEAR = 96
REST = CHIP - NEAR
HALF = 5
WIDE = HALF * HD
FIRST_ROWS = 1600
SECOND_ROWS = 1600
BACK_ROWS = 640
ACROSS = ((0, 2), (1, 3), (2, 0), (3, 1))
BESIDE = ((0, 1), (1, 0), (2, 3), (3, 2))
INNER = ((1, 2), (2, 1))
OUTWARD = ((1, 0), (2, 3))
OTHER_ROW = ((0, 1), (1, 0))
SCORE_SCALE = math.log2(math.e) / math.sqrt(HD)
VMEM = 24 * 1024 * 1024


def plan(start, side):
    first = start // 16 * 16
    last = (start + MOST + 15) // 16 * 16
    below, above = CHIP - first, last - CHIP
    mine = jnp.where(side == 0, below, above)
    theirs = jnp.where(side == 0, above, below)
    most = jnp.maximum(mine, theirs)
    lent = sum((most > limit).astype(jnp.int32) for limit in (256, 272, 288, 320, 352))
    return first, mine, theirs, HALF - lent, (mine > theirs).astype(jnp.int32)


def sixteen(offset):
    return pl.multiple_of(offset, 16)


def deal_kernel(me_ref, q_ref, k_ref, v_ref, out, near, sums):
    me = me_ref[0]
    half = out.shape[2]
    at = pl.ds(pl.multiple_of((1 - lax.rem(me, 2)) * half, 128), half)
    rows = pl.ds(sixteen((1 - me // 2) * NEAR), NEAR)
    for i, ref in enumerate((q_ref, k_ref, v_ref)):
        out[i] = ref[:, at]
    for i, ref in enumerate((k_ref, v_ref)):
        near[i] = ref[rows, :]
    for i, ref in enumerate((q_ref, k_ref)):
        lanes = jnp.zeros((ROWS, HD), jnp.float32)
        for column in range(0, ref.shape[1], HD):
            x = ref[:, column : column + HD].astype(jnp.float32)
            lanes += x * x
        sums[i : i + 1, :] = jnp.sum(jnp.transpose(lanes), axis=0, keepdims=True)


def pack_kernel(me_ref, q_ref, k_ref, v_ref, mate, ids, mate_ids, first_out, second_out, chip, buffer):
    me = me_ref[0]
    side, core = me // 2, lax.rem(me, 2)
    here, there = ids[...], mate_ids[...]
    edge = jnp.where(
        side == 0,
        jnp.maximum(jnp.max(here), jnp.max(there)),
        jnp.minimum(jnp.min(here), jnp.min(there)),
    )
    count = (
        jnp.sum(jnp.where(here == edge, 1.0, 0.0)) + jnp.sum(jnp.where(there == edge, 1.0, 0.0))
    ).astype(jnp.int32)
    start = jnp.where(side == 0, CHIP - count, count - NEAR)
    first, mine, _, kept, major = plan(start, side)
    for i, ref in enumerate((q_ref, k_ref, v_ref)):
        chip[i, pl.ds(sixteen(core * ROWS), ROWS), :] = ref[...]
        chip[i, pl.ds(sixteen((1 - core) * ROWS), ROWS), :] = mate[i]
        chip[i, CHIP:, :] = jnp.zeros((NEAR, ref.shape[1]), ref.dtype)
    buffer[...] = jnp.zeros_like(buffer)
    near_at = jnp.where(side == 0, REST, 0)
    rest_at = jnp.where(side == 0, first, NEAR)
    rest = mine - NEAR

    def put(offset, which, head, row, length):
        at = slice(head * HD, (head + 1) * HD)

        def step(i, carry):
            buffer[pl.ds(sixteen(offset + i * NEAR), NEAR), :] = chip[
                which, pl.ds(sixteen(row + i * NEAR), NEAR), at
            ]
            return carry

        lax.fori_loop(0, (length + NEAR - 1) // NEAR, step, 0)

    offset = jnp.int32(0)
    for i in range(HALF):
        head = HALF + i
        lend = jnp.logical_and(i >= kept, major == 0)
        send = jnp.logical_or(i < kept, major == 0)
        put(offset, 0, head, near_at, jnp.where(lend, NEAR, 0))
        offset += jnp.where(lend, NEAR, 0)
        put(offset, 0, head, rest_at, jnp.where(lend, rest, 0))
        offset += jnp.where(lend, rest, 0)
        length = jnp.where(send, rest, 0)
        for which in (1, 2):
            put(offset, which, head, rest_at, length)
            offset += length
    for head in range(HALF):
        for which in (1, 2):
            put(offset, which, head, rest_at, rest)
            offset += rest
    first_out[...] = buffer[:FIRST_ROWS, :]
    second_out[...] = buffer[FIRST_ROWS : FIRST_ROWS + SECOND_ROWS, :]


def turn(x, gain, gain_s, swap, cosine, sine):
    other = jnp.dot(x, swap, preferred_element_type=jnp.float32)
    return ((x.astype(jnp.float32) * gain) * cosine + (other * gain_s) * sine).astype(jnp.bfloat16)


def flip(gain):
    size = gain.shape[1]
    even = lax.broadcasted_iota(jnp.int32, gain.shape, 1) % 2 == 0
    return jnp.where(even, pltpu.roll(gain, size - 1, 1), pltpu.roll(gain, 1, 1))


def signed_swap():
    at_row = lax.broadcasted_iota(jnp.int32, (HD, HD), 0)
    at_column = lax.broadcasted_iota(jnp.int32, (HD, HD), 1)
    sign = jnp.where(at_column % 2 == 0, -1.0, 1.0)
    return jnp.where(at_row == (at_column ^ 1), sign, 0.0).astype(jnp.bfloat16)


def softmax_product(scores, values):
    peak = jnp.max(scores, axis=0, keepdims=True)
    weights = jnp.exp2((scores - peak) * SCORE_SCALE)
    total = jnp.sum(weights, axis=0, keepdims=True)
    out = lax.dot_general(
        values, weights.astype(jnp.bfloat16), (((0,), (0,)), ((), ())),
        preferred_element_type=jnp.float32,
    )
    return jnp.transpose(out / total).astype(jnp.bfloat16)


def columns_of(row):
    return jnp.transpose(jnp.broadcast_to(row, (HD, row.shape[1])))


def spread_scales(sums):
    return [columns_of(lax.rsqrt(sums[i : i + 1, :] / D + EPSILON)) for i in range(2)]


def turn_kernel(me_ref, q_ref, k_ref, v_ref, mate, cosine, sine, sums, gq, gk, out, table):
    core = lax.rem(me_ref[0], 2)
    swap = signed_swap()
    for i, scale in enumerate(spread_scales(sums)):
        table[2 * i] = cosine[...] * scale
        table[2 * i + 1] = sine[...] * scale
    for here, rows in ((True, core), (False, 1 - core)):
        rows = pl.ds(sixteen(rows * ROWS), ROWS)
        out[2, rows, :] = v_ref[...] if here else mate[2]
        for i, (ref, gains) in enumerate(((q_ref, gq), (k_ref, gk))):
            cos_here, sin_here = table[2 * i, rows, :], table[2 * i + 1, rows, :]
            for h in range(out.shape[2] // HD):
                at = slice(h * HD, (h + 1) * HD)
                gain = gains[:, at]
                x = ref[:, at] if here else mate[i, :, at]
                out[i, rows, at] = turn(x, gain, flip(gain), swap, cos_here, sin_here)


def attend_kernel(flexible, info, *refs):
    (local, near_here, near_passed, cosine, sine, sums, gq, gk, ids) = refs[:9]
    refs = refs[9:]
    if flexible:
        first_in, own_out, mate_out, back = refs[:4]
        refs = refs[4:]
    else:
        first_in, second_in, own_out, mate_out = refs[:4]
        refs = refs[4:]
    near, stream, bias, scales, table, keys, values, result = refs[:8]
    core, side, theirs, kept, major = info[0], info[1], info[2], info[3], info[4]
    edge, first = info[5].astype(jnp.float32), info[7]
    inner = side != core
    rest = theirs - NEAR

    @pl.when(inner)
    def _():
        near[...] = near_here[...]

    @pl.when(jnp.logical_not(inner))
    def _():
        near[...] = near_passed[...]

    stream[:FIRST_ROWS, :] = first_in[...]
    if flexible:
        stream[FIRST_ROWS:, :] = jnp.zeros((stream.shape[0] - FIRST_ROWS, HD), stream.dtype)
    else:
        stream[FIRST_ROWS : FIRST_ROWS + SECOND_ROWS, :] = second_in[...]
        stream[FIRST_ROWS + SECOND_ROWS :, :] = jnp.zeros((REST, HD), stream.dtype)

    near_rows = pl.ds(sixteen(jnp.where(side == 0, 0, REST)), NEAR)
    rest_rows = pl.ds(sixteen(jnp.where(side == 0, NEAR, first)), REST)
    for i, scale in enumerate(spread_scales(sums)):
        if i == 1 or flexible:
            scales[:CHIP, :] = scale
            scales[CHIP:, :] = jnp.ones((REST, HD), jnp.float32)
            for j, ref in enumerate((cosine, sine)):
                table[2 * i + j, :NEAR, :] = ref[:NEAR, :] * scales[near_rows, :]
                table[2 * i + j, NEAR:, :] = ref[NEAR:, :] * scales[rest_rows, :]

    clip_of = columns_of(ids[...])
    for t in range(0, CHIP, HD):
        bias[:, t : t + HD] = jnp.where(clip_of == ids[:, t : t + HD], 0.0, NEGATIVE)
    if flexible:
        bias[:, CHIP:] = jnp.where(clip_of == edge, 0.0, NEGATIVE)

    swap = signed_swap()
    if flexible:
        base = jnp.int32(0)
    else:
        base = 2 * rest * kept + jnp.where(major == 1, (HALF - kept) * (2 * rest + theirs), 0)
    bases = []
    for h in range(HALF):
        at = slice(h * HD, (h + 1) * HD)
        gain = gk[:, at]
        key_at = base
        bases.append(base)
        if flexible:
            lend = jnp.logical_and(h >= kept, major == 1)
            took = jnp.logical_or(h < kept, major == 1)
            key_at = base + jnp.where(lend, theirs, 0)
            base += jnp.where(took, 2 * rest, 0) + jnp.where(lend, theirs, 0)
        else:
            base += 2 * rest
        far = jnp.concatenate([near[0, :, at], stream[pl.ds(sixteen(key_at), REST), :]], axis=0)
        keys[h, :CHIP, :] = local[1, :, at]
        keys[h, CHIP:, :] = turn(far, gain, flip(gain), swap, table[2], table[3])
        values[h, :CHIP, :] = local[2, :, at]
        values[h, CHIP : CHIP + NEAR, :] = near[1, :, at]
        values[h, CHIP + NEAR :, :] = stream[pl.ds(sixteen(key_at + rest), REST), :]
        for t in range(0, CHIP, HD):
            scores = lax.dot_general(
                keys[h], local[0, t : t + HD, at], (((1,), (1,)), ((), ())),
                preferred_element_type=jnp.float32,
            ) + bias[:, t : t + HD]
            result[t : t + HD, at] = softmax_product(scores, values[h])
    own_out[...] = result[pl.ds(sixteen(core * ROWS), ROWS), :]
    mate_out[...] = result[pl.ds(sixteen((1 - core) * ROWS), ROWS), :]
    if flexible:
        back_rows = refs[8]
        back_rows[...] = jnp.zeros_like(back_rows)
        for h in range(HALF):
            at = slice(h * HD, (h + 1) * HD)

            @pl.when(jnp.logical_and(h >= kept, major == 1))
            def _():
                gain = gq[:, at]
                x = stream[pl.ds(sixteen(bases[h]), 2 * HD), :]
                far_q = turn(
                    x, gain, flip(gain), swap, table[0, : 2 * HD, :], table[1, : 2 * HD, :]
                )

                def answer(t):
                    scores = lax.dot_general(
                        keys[h], far_q[t : t + HD], (((1,), (1,)), ((), ())),
                        preferred_element_type=jnp.float32,
                    ) + bias[:, CHIP:]
                    back_rows[pl.ds(sixteen((h - kept) * theirs + t), HD), :] = softmax_product(
                        scores, values[h]
                    )

                answer(0)
                pl.when(theirs > HD)(lambda: answer(HD))

        back[...] = back_rows[:BACK_ROWS, :]


def join_kernel(
    info, flex_here, fixed_here, flex_there, fixed_there, back_here, back_there, ids, out, rows, lines
):
    core, side = info[0], info[1]
    mine = info[6]
    kept, major, first = info[3], info[4], info[7]
    edge = info[5].astype(jnp.float32)
    half = 2 * WIDE
    inside = jnp.transpose(jnp.broadcast_to(ids[...], (HD, ROWS))) == edge
    for here, flex, fixed, back in (
        (True, flex_here, fixed_here, back_here),
        (False, flex_there, fixed_there, back_there),
    ):
        column = pl.multiple_of((core if here else 1 - core) * half, 128)
        out[:, pl.ds(column, WIDE)] = fixed[...]
        out[:, pl.ds(pl.multiple_of(column + WIDE, 128), WIDE)] = flex[...]

        @pl.when(jnp.logical_and(major == 0, kept < HALF))
        def _():
            rows[:BACK_ROWS, :] = back[...]
            rows[BACK_ROWS:, :] = jnp.zeros((REST, HD), rows.dtype)
            for h in range(HALF):

                @pl.when(h >= kept)
                def _():
                    base = (h - kept) * mine
                    near_at = jnp.where(side == 0, REST, 0)
                    rest_at = jnp.where(side == 0, first, NEAR)
                    lines[pl.ds(sixteen(rest_at), REST), :] = rows[
                        pl.ds(sixteen(base + NEAR), REST), :
                    ]
                    lines[pl.ds(sixteen(near_at), NEAR), :] = rows[pl.ds(sixteen(base), NEAR), :]
                    at = slice(h * HD, (h + 1) * HD)
                    place = pl.ds(pl.multiple_of(column + WIDE + h * HD, 128), HD)
                    out[:, place] = jnp.where(
                        inside, lines[pl.ds(sixteen(core * ROWS), ROWS), :], flex[:, at]
                    )


def lookup(lookup_table, positions):
    labels = jnp.arange(lookup_table.shape[0], dtype=jnp.int32)
    return jnp.sum(
        jnp.where(positions[:, None] == labels[None, :], lookup_table[None, :], 0), axis=1
    )


def angles_of(offsets, clip_of, clip_grid):
    sixth_part = HD // 6
    first_dims = HD - 4 * sixth_part
    first_freqs = 1.0 / ROTARY_BASE ** (
        jnp.arange(0, first_dims, 2, dtype=jnp.float32) / first_dims
    )
    other_freqs = 1.0 / ROTARY_BASE ** (
        jnp.arange(0, 2 * sixth_part, 2, dtype=jnp.float32) / (2 * sixth_part)
    )
    heights = lookup(clip_grid[:, 0], clip_of)
    widths = lookup(clip_grid[:, 1], clip_of)
    frame_pos = (offsets // (heights * widths)).astype(jnp.float32)[:, None]
    line_pos = (offsets // widths % heights).astype(jnp.float32)[:, None]
    column_pos = (offsets % widths).astype(jnp.float32)[:, None]
    freqs = jnp.repeat(jnp.concatenate([first_freqs, other_freqs, other_freqs]), 2)[None, :]
    feature = jnp.arange(HD, dtype=jnp.int32)[None, :]
    position = jnp.where(
        feature < first_dims,
        frame_pos,
        jnp.where(feature < first_dims + 2 * sixth_part, line_pos, column_pos),
    )
    return position * freqs


def whole(a):
    return pl.BlockSpec(a.shape, lambda i, s: (0,) * len(a.shape))


def call(kernel, out_shape, in_specs, out_specs, scratch, scalars, *operands):
    return pl.pallas_call(
        kernel,
        out_shape=out_shape,
        grid_spec=pltpu.PrefetchScalarGridSpec(
            num_scalar_prefetch=1,
            grid=(1,),
            in_specs=in_specs,
            out_specs=out_specs,
            scratch_shapes=scratch,
        ),
        compiler_params=pltpu.CompilerParams(vmem_limit_bytes=VMEM),
        cost_estimate=pl.CostEstimate(flops=0, bytes_accessed=0, transcendentals=0),
    )(scalars, *operands)


def attend(flexible, info, streams, local, near, near_passed, waves, sums, gains, ids):
    group = 1 if flexible else 0
    bf16, f32 = jnp.bfloat16, jnp.float32
    here = pl.BlockSpec((3, CHIP, WIDE), lambda i, s: (0, 0, group))
    nears = pl.BlockSpec((2, NEAR, WIDE), lambda i, s: (0, 0, 2 * s[0] + group))
    gain = pl.BlockSpec((1, WIDE), lambda i, s: (0, 2 * s[0] + group))
    far = pl.BlockSpec((CHIP, HD), lambda i, s: (1, 0))
    shapes = [jax.ShapeDtypeStruct((ROWS, WIDE), bf16)] * 2
    stream_rows = FIRST_ROWS + (0 if flexible else SECOND_ROWS) + REST
    scratch = [
        pltpu.VMEM((2, NEAR, WIDE), bf16),
        pltpu.VMEM((stream_rows, HD), bf16),
        pltpu.VMEM((2 * CHIP, CHIP + (HD if flexible else 0)), f32),
        pltpu.VMEM((CHIP + REST, HD), f32),
        pltpu.VMEM((4, CHIP, HD), f32),
        pltpu.VMEM((HALF, 2 * CHIP, HD), bf16),
        pltpu.VMEM((HALF, 2 * CHIP, HD), bf16),
        pltpu.VMEM((CHIP, WIDE), bf16),
    ]
    if flexible:
        shapes = shapes + [jax.ShapeDtypeStruct((BACK_ROWS, HD), bf16)]
        scratch = scratch + [pltpu.VMEM((BACK_ROWS + 2 * HD, HD), bf16)]
    operands = (local, near, near_passed, *waves, sums, *gains, ids, *streams)
    in_specs = [here, nears, nears, far, far, whole(sums), gain, gain, whole(ids)]
    in_specs += [whole(s) for s in streams]
    return call(
        functools.partial(attend_kernel, flexible), shapes, in_specs, [whole(s) for s in shapes],
        scratch, info, *operands,
    )


def on_device(queries, keys, values, gain_q, gain_k, clip_ids, clip_grid):
    width = queries.shape[1]
    half = width // 2
    bf16, f32 = jnp.bfloat16, jnp.float32
    me = lax.axis_index("ctx").astype(jnp.int32)
    side, core = me // 2, me % 2
    at_me = me[None]

    clip_row = clip_ids.astype(f32)[None, :]
    mate_row = lax.ppermute(clip_row, "ctx", BESIDE)

    deal_shapes = [
        jax.ShapeDtypeStruct((3, ROWS, half), bf16),
        jax.ShapeDtypeStruct((2, NEAR, width), bf16),
        jax.ShapeDtypeStruct((2, ROWS), f32),
    ]
    dealt, near_send, sums = call(
        deal_kernel, deal_shapes, [whole(queries)] * 3, [whole(s) for s in deal_shapes], [],
        at_me, queries, keys, values,
    )
    mate = lax.ppermute(dealt, "ctx", BESIDE)
    near = lax.ppermute(near_send, "ctx", INNER)
    own_spec = pl.BlockSpec((ROWS, half), lambda i, s: (0, s[0] % 2))
    stream_shapes = [
        jax.ShapeDtypeStruct((FIRST_ROWS, HD), bf16),
        jax.ShapeDtypeStruct((SECOND_ROWS, HD), bf16),
    ]
    first_send, second_send = call(
        pack_kernel, stream_shapes,
        [own_spec] * 3 + [whole(mate), whole(clip_row), whole(mate_row)],
        [whole(s) for s in stream_shapes],
        [
            pltpu.VMEM((3, CHIP + NEAR, half), bf16),
            pltpu.VMEM((FIRST_ROWS + SECOND_ROWS + NEAR, HD), bf16),
        ],
        at_me, queries, keys, values, mate, clip_row, mate_row,
    )

    sums = sums + lax.ppermute(sums, "row", OTHER_ROW)
    mate_sums = lax.ppermute(sums, "ctx", BESIDE)

    def by_core(here, there):
        return jnp.where(
            core == 0, jnp.concatenate([here, there], 1), jnp.concatenate([there, here], 1)
        )

    chip_sums = by_core(sums, mate_sums)
    far_sums = lax.ppermute(chip_sums, "ctx", ACROSS)
    first_send, chip_sums = lax.optimization_barrier((first_send, chip_sums))
    first_stream = lax.ppermute(first_send, "ctx", ACROSS)
    second_stream = lax.ppermute(second_send, "ctx", ACROSS)
    chip_ids = by_core(clip_row, mate_row)[0].astype(jnp.int32)
    chip_ids, _ = lax.optimization_barrier((chip_ids, first_send))
    edge = jnp.where(side == 0, chip_ids[CHIP - 1], chip_ids[0])
    count = jnp.sum((chip_ids == edge).astype(jnp.int32))
    start = jnp.where(side == 0, CHIP - count, count - NEAR)
    first, mine, theirs, kept, major = plan(start, side)
    info = jnp.stack([core, side, theirs, kept, major, edge, mine, first])

    slots = jnp.arange(CHIP, dtype=jnp.int32)
    near_tokens = jnp.where(side == 0, CHIP, REST) + slots[:NEAR]
    rest_tokens = jnp.where(side == 0, CHIP + NEAR, first) + slots[:REST]
    rest_end = jnp.where(side == 0, start + MOST, REST)
    rest_valid = (rest_tokens >= start) & (rest_tokens < rest_end)
    far_tokens = jnp.concatenate([near_tokens, rest_tokens])
    far_valid = jnp.concatenate([jnp.ones((NEAR,), bool), rest_valid])
    labels = jnp.arange(CLIPS, dtype=jnp.int32)
    below = jnp.sum((chip_ids[:, None] < labels[None, :]).astype(jnp.int32), axis=0)
    local_offsets = jnp.where(
        (side == 1) & (chip_ids == edge), CHIP - start + slots, slots - lookup(below, chip_ids)
    )
    far_offsets = jnp.maximum(far_tokens - start, 0)
    offsets = jnp.concatenate([local_offsets, far_offsets])
    clip_of = jnp.concatenate([chip_ids, jnp.broadcast_to(edge, (CHIP,))])
    angles = angles_of(offsets, clip_of, clip_grid)
    waves = (jnp.cos(angles), jnp.sin(angles))
    gains = (gain_q[None, :], gain_k[None, :])
    mask_ids = jnp.concatenate([chip_ids, jnp.where(far_valid, edge, -1)]).astype(f32)[None, :]

    wave_spec = pl.BlockSpec((CHIP, HD), lambda i, s: (0, 0))
    gain_spec = pl.BlockSpec((1, half), lambda i, s: (0, s[0] % 2))
    local_shape = jax.ShapeDtypeStruct((3, CHIP, half), bf16)
    local = call(
        turn_kernel, local_shape,
        [own_spec] * 3 + [whole(mate), wave_spec, wave_spec, whole(chip_sums), gain_spec, gain_spec],
        whole(local_shape), [pltpu.VMEM((4, CHIP, HD), f32)],
        at_me, queries, keys, values, mate, *waves, chip_sums, *gains,
    )
    near, _ = lax.optimization_barrier((near, second_send))
    near_passed = lax.ppermute(near, "ctx", OUTWARD)

    common = (local, near, near_passed, waves, far_sums, gains, mask_ids)
    flex_here, flex_send, back_send = attend(True, info, (first_stream,), *common)
    back_here = lax.ppermute(back_send, "ctx", ACROSS)
    flex_there = lax.ppermute(flex_send, "ctx", BESIDE)
    fixed_here, fixed_send = attend(False, info, (first_stream, second_stream), *common)
    fixed_there = lax.ppermute(fixed_send, "ctx", BESIDE)
    back_there = lax.ppermute(back_here, "ctx", BESIDE)
    out_shape = jax.ShapeDtypeStruct((ROWS, width), bf16)
    operands = (flex_here, fixed_here, flex_there, fixed_there, back_here, back_there, clip_row)
    return call(
        join_kernel, out_shape, [whole(a) for a in operands], whole(out_shape),
        [pltpu.VMEM((BACK_ROWS + REST, HD), bf16), pltpu.VMEM((2 * REST, HD), bf16)],
        info, *operands,
    )


def spin(matrix, offsets, clip_of, clip_grid, head_size):
    row_count = matrix.shape[0]
    sixth_part = head_size // 6
    first_dims = head_size - 4 * sixth_part
    first_freqs = 1.0 / ROTARY_BASE ** (
        jnp.arange(0, first_dims, 2, dtype=jnp.float32) / first_dims
    )
    other_freqs = 1.0 / ROTARY_BASE ** (
        jnp.arange(0, 2 * sixth_part, 2, dtype=jnp.float32) / (2 * sixth_part)
    )
    heights = lookup(clip_grid[:, 0], clip_of)
    widths = lookup(clip_grid[:, 1], clip_of)
    frame_pos = offsets // (heights * widths)
    line_pos = offsets // widths % heights
    column_pos = offsets % widths
    angles = jnp.concatenate(
        [
            frame_pos.astype(jnp.float32)[:, None] * first_freqs[None, :],
            line_pos.astype(jnp.float32)[:, None] * other_freqs[None, :],
            column_pos.astype(jnp.float32)[:, None] * other_freqs[None, :],
        ],
        axis=1,
    )
    cosine = jnp.repeat(jnp.cos(angles), 2, axis=1)
    sine_table = jnp.repeat(jnp.sin(angles), 2, axis=1)
    feature = jnp.arange(head_size, dtype=jnp.int32)
    is_even = (feature % 2 == 0)[None, None, :]
    head_view = matrix.reshape(row_count, -1, head_size)
    partner = jnp.where(is_even, -jnp.roll(head_view, -1, axis=2), jnp.roll(head_view, 1, axis=2))
    turned = head_view * cosine[:, None, :] + partner * sine_table[:, None, :]
    return turned.reshape(row_count, -1)


def on_any(queries, keys, values, gain_q, gain_k, clip_ids, clip_grid):
    rows_here, width_here = queries.shape
    heads_here = width_here // HD
    score_scale = 1.0 / math.sqrt(HD)
    query_wide = queries.astype(jnp.float32)
    key_wide = keys.astype(jnp.float32)
    squares = lax.psum(
        (jnp.sum(query_wide * query_wide, axis=1), jnp.sum(key_wide * key_wide, axis=1)), "row"
    )
    query_scale = lax.rsqrt(squares[0] / D + EPSILON)
    key_scale = lax.rsqrt(squares[1] / D + EPSILON)
    labels = jnp.arange(CLIPS, dtype=jnp.int32)
    local_counts = jnp.sum((clip_ids[:, None] == labels[None, :]).astype(jnp.int32), axis=0)
    totals = lax.psum(local_counts, "ctx")
    starts = jnp.cumsum(totals) - totals
    first_row = lax.axis_index("ctx") * rows_here
    offsets = first_row + jnp.arange(rows_here, dtype=jnp.int32) - lookup(starts, clip_ids)
    query_rot = spin(
        query_wide * query_scale[:, None] * gain_q[None, :], offsets, clip_ids, clip_grid, HD
    ).astype(jnp.bfloat16)
    query_heads = query_rot.reshape(rows_here, heads_here, HD)
    key_send = spin(
        key_wide * key_scale[:, None] * gain_k[None, :], offsets, clip_ids, clip_grid, HD
    ).astype(jnp.bfloat16)
    initial = (
        jnp.full((heads_here, rows_here), NEGATIVE, jnp.float32),
        jnp.zeros((heads_here, rows_here), jnp.float32),
        jnp.zeros((rows_here, heads_here, HD), jnp.float32),
    )
    running = initial
    piece_start = jnp.int32(0)
    key_piece = lax.all_gather(key_send, "ctx", axis=0, tiled=True)
    value_piece = lax.all_gather(values, "ctx", axis=0, tiled=True)
    row_count = key_piece.shape[0]
    block_rows = min(row_count, block_limit)
    for block_first in range(0, row_count, block_rows):
        block_size = min(block_rows, row_count - block_first)
        fold_key_rows = key_piece[block_first : block_first + block_size]
        fold_value_rows = value_piece[block_first : block_first + block_size]
        key_index = piece_start + block_first + jnp.arange(fold_key_rows.shape[0], dtype=jnp.int32)
        key_key_clips = (
            jnp.sum((starts[None, :] <= key_index[:, None]).astype(jnp.int32), axis=1) - 1
        )
        peak_old, total_old, summed_old = running
        key_view = fold_key_rows.reshape(fold_key_rows.shape[0], heads_here, HD)
        value_view = fold_value_rows.reshape(fold_value_rows.shape[0], heads_here, HD)
        scores = (
            jnp.einsum("qhd,khd->hqk", query_heads, key_view, preferred_element_type=jnp.float32)
            * score_scale
        )
        same = clip_ids[:, None] == key_key_clips[None, :]
        masked = jnp.where(same[None, :, :], scores, NEGATIVE)
        peak_new = jnp.maximum(peak_old, jnp.max(masked, axis=2))
        weights = jnp.where(same[None, :, :], jnp.exp(masked - peak_new[:, :, None]), 0.0)
        factor = jnp.exp(peak_old - peak_new)
        total_new = total_old * factor + jnp.sum(weights, axis=2)
        summed = summed_old * jnp.transpose(factor)[:, :, None] + jnp.einsum(
            "hqk,khd->qhd",
            weights.astype(jnp.bfloat16),
            value_view,
            preferred_element_type=jnp.float32,
        )
        running = (peak_new, total_new, summed)
    attended = running[2] / jnp.transpose(running[1])[:, :, None]
    return attended.reshape(rows_here, width_here).astype(jnp.bfloat16)


def solution(mesh):
    in_specs = (
        P(("batch", "ctx"), "row"),
        P(("batch", "ctx"), "row"),
        P(("batch", "ctx"), "row"),
        P("row"),
        P("row"),
        P(("batch", "ctx")),
        P("batch", None),
    )
    out_specs = P(("batch", "ctx"), "row")
    pair_of_chips = mesh.shape["ctx"] == 4 and mesh.shape["row"] == 2
    return jax.shard_map(
        on_device if pair_of_chips else on_any,
        mesh=mesh, in_specs=in_specs, out_specs=out_specs, check_vma=False,
    )
```

```python
import functools
import math

import jax
import jax.numpy as jnp
from jax import lax
from jax.experimental import pallas as pl
from jax.experimental.pallas import tpu as pltpu
from jax.sharding import PartitionSpec as P

HD = 128
D = 5120
CLIPS = 4
EPSILON = 1e-06
NEGATIVE = -1e30
ROTARY_BASE = 10000.0
block_limit = 1024

ROWS = 192
CHIP = 2 * ROWS
MOST = 480
NEAR = 96
REST = CHIP - NEAR
HALF = 5
WIDE = HALF * HD
TILE = 192
SHORT = 640
FIRST_ROWS = 1600
SECOND_ROWS = 1600
SUM_ROWS = 32
STREAM_ROWS = FIRST_ROWS + SECOND_ROWS
BACK_ROWS = 640
ACROSS = ((0, 2), (1, 3), (2, 0), (3, 1))
BESIDE = ((0, 1), (1, 0), (2, 3), (3, 2))
STRAIGHT = ((1, 3), (2, 0))
SLANTED = ((1, 2), (2, 1))
OTHER_ROW = ((0, 1), (1, 0))
OPPOSITE = tuple((2 * a + r, 2 * b + 1 - r) for a, b in BESIDE for r in (0, 1))
SCORE_SCALE = math.log2(math.e) / math.sqrt(HD)
VMEM = 24 * 1024 * 1024
ALL_VMEM = 60 * 1024 * 1024


def plan(start, side):
    first = start // 16 * 16
    last = (start + MOST + 15) // 16 * 16
    below, above = CHIP - first, last - CHIP
    mine = jnp.where(side == 0, below, above)
    theirs = jnp.where(side == 0, above, below)
    most = jnp.maximum(mine, theirs)
    lent = sum((most > limit).astype(jnp.int32) for limit in (256, 272, 288, 320, 352))
    return first, mine, theirs, HALF - lent, (mine > theirs).astype(jnp.int32)


def sixteen(offset):
    return pl.multiple_of(offset, 16)


def deal_kernel(me_ref, q_ref, k_ref, v_ref, ids, out, near_own, near_other, sums):
    me = me_ref[0]
    core = lax.rem(me, 2)
    half = out.shape[2]
    at = pl.ds(pl.multiple_of((1 - core) * half, 128), half)
    own = pl.ds(pl.multiple_of(core * half, 128), half)
    rows = pl.ds(sixteen((1 - me // 2) * NEAR), NEAR)
    for i, ref in enumerate((k_ref, v_ref)):
        near_own[i] = ref[rows, own]
        near_other[i] = ref[rows, at]
    for i, ref in enumerate((q_ref, k_ref, v_ref)):
        out[i] = ref[:, at]
    for i, ref in enumerate((q_ref, k_ref)):
        lanes = jnp.zeros((ROWS, HD), jnp.float32)
        for column in range(0, ref.shape[1], HD):
            x = ref[:, column : column + HD].astype(jnp.float32)
            lanes += x * x
        sums[i : i + 1, :] = jnp.sum(jnp.transpose(lanes), axis=0, keepdims=True)
    sums[2:3, :] = ids[...].astype(jnp.float32)


def side_by_side(core, here, there, out):
    for ref, at in ((here, 0), (there, 1)):

        @pl.when(core == at)
        def _():
            out[:, :ROWS] = ref

        @pl.when(core != at)
        def _():
            out[:, ROWS:] = ref


def pack_kernel(
    me_ref, q_ref, k_ref, v_ref, mate, sums, mate_sums, row_sums, mate_row_sums,
    first_out, second_out, totals, info, chip, buffer,
):
    me = me_ref[0]
    side, core = me // 2, lax.rem(me, 2)
    here, there = sums[2:3, :], mate_sums[2:3, :]
    edge = jnp.where(
        side == 0,
        jnp.maximum(jnp.max(here), jnp.max(there)),
        jnp.minimum(jnp.min(here), jnp.min(there)),
    )
    count = (
        jnp.sum(jnp.where(here == edge, 1.0, 0.0)) + jnp.sum(jnp.where(there == edge, 1.0, 0.0))
    ).astype(jnp.int32)
    start = jnp.where(side == 0, CHIP - count, count - NEAR)
    first, mine, theirs, kept, major = plan(start, side)
    known = (core, side, theirs, kept, major, edge.astype(jnp.int32), mine, first, start)
    for i, value in enumerate(known):
        info[i] = value
    half = chip.shape[2]
    columns = pl.ds(pl.multiple_of(core * half, 128), half)
    for i, ref in enumerate((q_ref, k_ref, v_ref)):
        chip[i, pl.ds(sixteen(core * ROWS), ROWS), :] = ref[:, columns]
        chip[i, pl.ds(sixteen((1 - core) * ROWS), ROWS), :] = mate[i]
        chip[i, CHIP:, :] = jnp.zeros((NEAR, half), ref.dtype)
    buffer[...] = jnp.zeros_like(buffer)
    near_at = jnp.where(side == 0, REST, 0)
    rest_at = jnp.where(side == 0, first, NEAR)
    rest = mine - NEAR

    def put(offset, which, head, row, length):
        at = slice(head * HD, (head + 1) * HD)

        def step(i, carry):
            buffer[pl.ds(sixteen(offset + i * NEAR), NEAR), :] = chip[
                which, pl.ds(sixteen(row + i * NEAR), NEAR), at
            ]
            return carry

        lax.fori_loop(0, (length + NEAR - 1) // NEAR, step, 0)

    offset = jnp.int32(0)
    for i in range(HALF):
        head = HALF + i
        lend = jnp.logical_and(i >= kept, major == 0)
        send = jnp.logical_or(i < kept, major == 0)
        put(offset, 0, head, near_at, jnp.where(lend, NEAR, 0))
        offset += jnp.where(lend, NEAR, 0)
        put(offset, 0, head, rest_at, jnp.where(lend, rest, 0))
        offset += jnp.where(lend, rest, 0)
        length = jnp.where(send, rest, 0)
        for which in (1, 2):
            put(offset, which, head, rest_at, length)
            offset += length
    for head in range(HALF):
        for which in (1, 2):
            put(offset, which, head, rest_at, rest)
            offset += rest
    side_by_side(
        core, sums[:2, :] + row_sums[:2, :], mate_sums[:2, :] + mate_row_sums[:2, :], totals
    )
    parts = []
    for i in range(2):
        left = totals[i : i + 1, :]
        for _ in range(3):
            part = left.astype(jnp.bfloat16)
            left = left - part.astype(jnp.float32)
            parts += [part[:, t : t + HD] for t in range(0, CHIP, HD)]
    parts += [jnp.zeros_like(parts[0])] * (SUM_ROWS - len(parts))
    first_out[:FIRST_ROWS, :] = buffer[:FIRST_ROWS, :]
    first_out[FIRST_ROWS:, :] = jnp.concatenate(parts, axis=0)
    second_out[...] = buffer[FIRST_ROWS:STREAM_ROWS, :]


def turn(x, gain, gain_s, swap, cosine, sine):
    other = jnp.dot(x, swap, preferred_element_type=jnp.float32)
    return ((x.astype(jnp.float32) * gain) * cosine + (other * gain_s) * sine).astype(jnp.bfloat16)


def flip(gain):
    size = gain.shape[1]
    even = lax.broadcasted_iota(jnp.int32, gain.shape, 1) % 2 == 0
    return jnp.where(even, pltpu.roll(gain, size - 1, 1), pltpu.roll(gain, 1, 1))


def signed_swap():
    at_row = lax.broadcasted_iota(jnp.int32, (HD, HD), 0)
    at_column = lax.broadcasted_iota(jnp.int32, (HD, HD), 1)
    sign = jnp.where(at_column % 2 == 0, -1.0, 1.0)
    return jnp.where(at_row == (at_column ^ 1), sign, 0.0).astype(jnp.bfloat16)


def attention(q, keys, bias, values):
    scores = lax.dot_general(
        q, keys, (((1,), (1,)), ((), ())), preferred_element_type=jnp.float32
    ) + bias
    peak = jnp.max(scores, axis=1, keepdims=True)
    weights = jnp.exp2((scores - peak) * SCORE_SCALE).astype(jnp.bfloat16)
    columns = jnp.concatenate([values, jnp.ones_like(values)], axis=1)
    sums = jnp.dot(weights, columns, preferred_element_type=jnp.float32)
    return (sums[:, :HD] / sums[:, HD:]).astype(jnp.bfloat16)


def columns_of(row):
    return jnp.transpose(jnp.broadcast_to(row, (HD, row.shape[1])))


def waves_kernel(info, grid, sums, mate_sums, freqs, cosine, sine, ids, chip_ids):
    core, side, first, start = info[0], info[1], info[7], info[8]
    edge_label = info[5]
    edge = edge_label.astype(jnp.float32)
    side_by_side(core, sums[2:3, :], mate_sums[2:3, :], chip_ids)
    here = chip_ids[...]
    slot = lax.broadcasted_iota(jnp.int32, (1, CHIP), 1)
    rest_start = jnp.where(side == 0, CHIP, first - NEAR)
    rest_end = jnp.where(side == 0, start + MOST, REST)
    token = slot + jnp.where(slot < NEAR, jnp.where(side == 0, CHIP, REST), rest_start)
    valid = jnp.logical_or(
        slot < NEAR, jnp.logical_and(token >= start, token < rest_end)
    )
    ids[:, :CHIP] = here
    ids[:, CHIP:] = jnp.where(valid, edge, -1.0)
    place = slot.astype(jnp.float32)
    offset, height, line_size = place, jnp.zeros_like(place), jnp.zeros_like(place)
    for label in range(CLIPS):
        same = here == float(label)
        below = jnp.sum(jnp.where(here < float(label), 1.0, 0.0), axis=1, keepdims=True)
        offset = offset - jnp.where(same, below, 0.0)
        height = height + jnp.where(same, grid[label, 0].astype(jnp.float32), 0.0)
        line_size = line_size + jnp.where(same, grid[label, 1].astype(jnp.float32), 0.0)
    carried = jnp.logical_and(here == edge, side == 1)
    offset = jnp.where(carried, place + (CHIP - start).astype(jnp.float32), offset)
    far_offset = jnp.maximum(token - start, 0).astype(jnp.float32)
    ones = jnp.ones_like(place)
    offset = jnp.concatenate([offset, far_offset], axis=1)
    height = jnp.concatenate([height, ones * grid[edge_label, 0].astype(jnp.float32)], axis=1)
    line_size = jnp.concatenate([line_size, ones * grid[edge_label, 1].astype(jnp.float32)], axis=1)
    frame = jnp.floor((offset + 0.5) / (height * line_size))
    offset = offset - frame * (height * line_size)
    line = jnp.floor((offset + 0.5) / line_size)
    column = offset - line * line_size
    sixth_part = HD // 6
    first_dims = HD - 4 * sixth_part
    feature = lax.broadcasted_iota(jnp.int32, (1, HD), 1)
    angles = freqs[...] * jnp.where(
        feature < first_dims,
        columns_of(frame),
        jnp.where(feature < first_dims + 2 * sixth_part, columns_of(line), columns_of(column)),
    )
    cosine[...] = jnp.cos(angles)
    sine[...] = jnp.sin(angles)


def turn_kernel(info, q_ref, k_ref, v_ref, mate, cosine, sine, totals, gq, gk, out, table):
    core = info[0]
    half = out.shape[2]
    columns = pl.ds(pl.multiple_of(core * half, 128), half)
    swap = signed_swap()
    for i in range(2):
        scale = columns_of(lax.rsqrt(totals[i : i + 1, :] / D + EPSILON))
        for j, ref in enumerate((cosine, sine)):
            table[2 * i + j] = ref[:CHIP, :] * scale
    for here, rows in ((True, core), (False, 1 - core)):
        rows = pl.ds(sixteen(rows * ROWS), ROWS)
        out[2, rows, :] = v_ref[:, columns] if here else mate[2]
        for i, (ref, gains) in enumerate(((q_ref, gq), (k_ref, gk))):
            cos_here, sin_here = table[2 * i, rows, :], table[2 * i + 1, rows, :]
            for h in range(half // HD):
                at = slice(h * HD, (h + 1) * HD)
                place = pl.ds(pl.multiple_of(core * half + h * HD, 128), HD)
                gain = gains[:, place]
                x = ref[:, place] if here else mate[i, :, at]
                out[i, rows, at] = turn(x, gain, flip(gain), swap, cos_here, sin_here)


def attend_kernel(flexible, head, count, info, *refs):
    local, near_straight, near_slanted, gq, gk, ids = refs[:6]
    streams = 1 if flexible else 2
    refs = refs[6:]
    if flexible:
        (cosine, sine), refs = refs[:2], refs[2:]
    else:
        table, refs = refs[0], refs[1:]
    arrived, refs = refs[:streams], refs[streams:]
    own_out, mate_out, refs = refs[0], refs[1], refs[2:]
    if flexible:
        back, table, refs = refs[0], refs[1], refs[2:]
    near, stream, bias, keys, values, result, sems = refs[:7]
    core, side, theirs, kept, major = info[0], info[1], info[2], info[3], info[4]
    edge = info[5].astype(jnp.float32)
    inner = side != core
    rest = theirs - NEAR
    near_columns = slice(head * HD, (head + count) * HD)
    sizes = (FIRST_ROWS, SECOND_ROWS)[:streams]
    copies, filled = [], 0
    for i, (ref, size) in enumerate(zip(arrived, sizes)):
        copies.append(
            pltpu.make_async_copy(
                ref.at[:size, :], stream.at[filled : filled + size, :], sems.at[1 + i]
            )
        )
        filled += size
    near_copies = [
        pltpu.make_async_copy(ref.at[:, :, near_columns], near, sems.at[0])
        for ref in (near_slanted, near_straight)
    ]
    for copy in copies:
        copy.start()
    pl.when(inner)(near_copies[0].start)
    pl.when(jnp.logical_not(inner))(near_copies[1].start)
    stream[filled:, :] = jnp.zeros((REST, HD), stream.dtype)

    columns = pl.ds(pl.multiple_of((2 * HALF * core + head) * HD, 128), count * HD)
    gq, gk = gq[:, columns], gk[:, columns]
    clip_of = columns_of(ids[:, :CHIP])
    for t in range(0, 2 * CHIP, HD):
        bias[:, t : t + HD] = jnp.where(clip_of == ids[:, t : t + HD], 0.0, NEGATIVE)
    for h in range(count):
        here = slice((head + h) * HD, (head + h + 1) * HD)
        keys[h, :CHIP, :] = local[1, :, here]
        values[h, :CHIP, :] = local[2, :, here]
    if flexible:
        back_rows, asked, scales, extra = refs[7:11]
        first = info[7]
        sum_copy = pltpu.make_async_copy(arrived[0].at[FIRST_ROWS:, :], extra, sems.at[4])
        sum_copy.start()
        near_rows = pl.ds(sixteen(jnp.where(side == 0, 0, REST)), NEAR)
        rest_rows = pl.ds(sixteen(jnp.where(side == 0, NEAR, first)), REST)
        scales[CHIP:, :] = jnp.ones((REST, HD), jnp.float32)
        back_rows[...] = jnp.zeros_like(back_rows)
        sum_copy.wait()
        parts = extra[...].astype(jnp.float32)
        for i, waves in enumerate((asked, table)):
            for j in range(3):
                total = sum(parts[9 * i + 3 * p + j : 9 * i + 3 * p + j + 1, :] for p in range(3))
                scales[j * HD : (j + 1) * HD, :] = columns_of(lax.rsqrt(total / D + EPSILON))
            for j, ref in enumerate((cosine, sine)):
                waves[j, :NEAR, :] = ref[CHIP : CHIP + NEAR, :] * scales[near_rows, :]
                waves[j, NEAR:, :] = ref[CHIP + NEAR :, :] * scales[rest_rows, :]
    near_copies[0].wait()
    for copy in copies:
        copy.wait()

    swap = signed_swap()
    if flexible:
        base = jnp.int32(0)
    else:
        base = 2 * rest * kept + jnp.where(major == 1, (HALF - kept) * (2 * rest + theirs), 0)
        base += 2 * rest * head
    bases = []
    for h in range(count):
        at = slice(h * HD, (h + 1) * HD)
        gain = gk[:, at]
        key_at = base
        bases.append(base)
        if flexible:
            lend = jnp.logical_and(h >= kept, major == 1)
            took = jnp.logical_or(h < kept, major == 1)
            key_at = base + jnp.where(lend, theirs, 0)
            base += jnp.where(took, 2 * rest, 0) + jnp.where(lend, theirs, 0)
        else:
            base += 2 * rest
        far = jnp.concatenate([near[0, :, at], stream[pl.ds(sixteen(key_at), REST), :]], axis=0)
        keys[h, CHIP:, :] = turn(far, gain, flip(gain), swap, table[0], table[1])
        values[h, CHIP : CHIP + NEAR, :] = near[1, :, at]
        values[h, CHIP + NEAR :, :] = stream[pl.ds(sixteen(key_at + rest), REST), :]

    def answer_here(seen):
        for h in range(count):
            at = slice(h * HD, (h + 1) * HD)
            here = slice((head + h) * HD, (head + h + 1) * HD)
            for t in range(0, CHIP, TILE):
                rows = slice(t, t + TILE)
                result[rows, at] = attention(
                    local[0, rows, here], keys[h, :seen, :], bias[rows, :seen], values[h, :seen, :]
                )

    short = theirs <= SHORT - CHIP
    pl.when(short)(lambda: answer_here(SHORT))
    pl.when(jnp.logical_not(short))(lambda: answer_here(2 * CHIP))
    own_out[...] = result[pl.ds(sixteen(core * ROWS), ROWS), :]
    mate_out[...] = result[pl.ds(sixteen((1 - core) * ROWS), ROWS), :]
    if flexible:
        far_bias = jnp.where(ids[:, :SHORT] == edge, 0.0, NEGATIVE)

        def answer_there(t):
            for h in range(HALF):
                at = slice(h * HD, (h + 1) * HD)
                gain = gq[:, at]
                x = stream[pl.ds(sixteen(bases[h] + t), HD), :]
                far_q = turn(
                    x, gain, flip(gain), swap, asked[0, t : t + HD, :], asked[1, t : t + HD, :]
                )
                place = jnp.where(h >= kept, (h - kept) * theirs + t, BACK_ROWS + HD)
                back_rows[pl.ds(sixteen(place), HD), :] = attention(
                    far_q, keys[h, :SHORT, :], far_bias, values[h, :SHORT, :]
                )

        lending = jnp.logical_and(kept < HALF, major == 1)
        pl.when(jnp.logical_and(lending, theirs > HD))(lambda: answer_there(HD))
        pl.when(lending)(lambda: answer_there(0))
        back[...] = back_rows[:BACK_ROWS, :]


def join_kernel(
    info, flex_here, fixed_here, flex_there, fixed_there, back_here, back_there, ids, out, rows, lines
):
    core, side = info[0], info[1]
    mine = info[6]
    kept, major, first = info[3], info[4], info[7]
    edge = info[5].astype(jnp.float32)
    half = 2 * WIDE
    inside = columns_of(ids[...].astype(jnp.float32)) == edge
    for here, flex, fixed, back in (
        (True, flex_here, fixed_here, back_here),
        (False, flex_there, fixed_there, back_there),
    ):
        column = pl.multiple_of((core if here else 1 - core) * half, 128)
        out[:, pl.ds(column, WIDE)] = fixed[...]
        out[:, pl.ds(pl.multiple_of(column + WIDE, 128), WIDE)] = flex[...]

        @pl.when(jnp.logical_and(major == 0, kept < HALF))
        def _():
            rows[:BACK_ROWS, :] = back[...]
            rows[BACK_ROWS:, :] = jnp.zeros((REST, HD), rows.dtype)
            for h in range(HALF):

                @pl.when(h >= kept)
                def _():
                    base = (h - kept) * mine
                    near_at = jnp.where(side == 0, REST, 0)
                    rest_at = jnp.where(side == 0, first, NEAR)
                    lines[pl.ds(sixteen(rest_at), REST), :] = rows[
                        pl.ds(sixteen(base + NEAR), REST), :
                    ]
                    lines[pl.ds(sixteen(near_at), NEAR), :] = rows[pl.ds(sixteen(base), NEAR), :]
                    at = slice(h * HD, (h + 1) * HD)
                    place = pl.ds(pl.multiple_of(column + WIDE + h * HD, 128), HD)
                    out[:, place] = jnp.where(
                        inside, lines[pl.ds(sixteen(core * ROWS), ROWS), :], flex[:, at]
                    )


def frequencies():
    sixth_part = HD // 6
    first_dims = HD - 4 * sixth_part
    first_freqs = 1.0 / ROTARY_BASE ** (
        jnp.arange(0, first_dims, 2, dtype=jnp.float32) / first_dims
    )
    other_freqs = 1.0 / ROTARY_BASE ** (
        jnp.arange(0, 2 * sixth_part, 2, dtype=jnp.float32) / (2 * sixth_part)
    )
    return jnp.repeat(jnp.concatenate([first_freqs, other_freqs, other_freqs]), 2)[None, :]


def whole(a):
    return pl.BlockSpec(a.shape, lambda i, s: (0,) * len(a.shape))


def held():
    return pl.BlockSpec(memory_space=pltpu.VMEM)


def call(kernel, out_shape, in_specs, out_specs, scratch, scalars, *operands, limit=VMEM):
    return pl.pallas_call(
        kernel,
        out_shape=out_shape,
        grid_spec=pltpu.PrefetchScalarGridSpec(
            num_scalar_prefetch=1,
            grid=(1,),
            in_specs=in_specs,
            out_specs=out_specs,
            scratch_shapes=scratch,
        ),
        compiler_params=pltpu.CompilerParams(vmem_limit_bytes=limit),
        cost_estimate=pl.CostEstimate(flops=0, bytes_accessed=0, transcendentals=0),
    )(scalars, *operands)


def attend(flexible, head, count, info, streams, waves, local, near_straight, near_slanted, gains, ids):
    bf16, f32 = jnp.bfloat16, jnp.float32
    there = pl.BlockSpec(memory_space=pl.ANY)
    shapes = [jax.ShapeDtypeStruct((ROWS, count * HD), bf16)] * 2
    stream_rows = sum((FIRST_ROWS, SECOND_ROWS)[: len(streams)]) + REST
    scratch = [
        pltpu.VMEM((2, NEAR, count * HD), bf16),
        pltpu.VMEM((stream_rows, HD), bf16),
        pltpu.VMEM((CHIP, 2 * CHIP), f32),
        pltpu.VMEM((count, 2 * CHIP, HD), bf16),
        pltpu.VMEM((count, 2 * CHIP, HD), bf16),
        pltpu.VMEM((CHIP, count * HD), bf16),
        pltpu.SemaphoreType.DMA((5,)),
    ]
    if flexible:
        far_waves = jax.ShapeDtypeStruct((2, CHIP, HD), f32)
        shapes = shapes + [jax.ShapeDtypeStruct((BACK_ROWS, HD), bf16), far_waves]
        scratch = scratch + [
            pltpu.VMEM((BACK_ROWS + 2 * HD, HD), bf16),
            pltpu.VMEM((2, CHIP, HD), f32),
            pltpu.VMEM((CHIP + REST, HD), f32),
            pltpu.VMEM((SUM_ROWS, HD), bf16),
        ]
    operands = (local, near_straight, near_slanted, *gains, ids, *waves, *streams)
    in_specs = [held(), there, there] + [held()] * (3 + len(waves)) + [there] * len(streams)
    return call(
        functools.partial(attend_kernel, flexible, head, count), shapes,
        in_specs, [held()] * len(shapes), scratch, info, *operands,
    )


def on_device(queries, keys, values, gain_q, gain_k, clip_ids, clip_grid):
    width = queries.shape[1]
    half = width // 2
    bf16, f32 = jnp.bfloat16, jnp.float32
    me = lax.axis_index("ctx").astype(jnp.int32)
    side, core = me // 2, me % 2
    at_me = me[None]

    clip_row = clip_ids[None, :]

    near_shape = jax.ShapeDtypeStruct((2, NEAR, half), bf16)
    deal_shapes = [
        jax.ShapeDtypeStruct((3, ROWS, half), bf16),
        near_shape,
        near_shape,
        jax.ShapeDtypeStruct((3, ROWS), f32),
    ]
    dealt, near_own, near_other, sums = call(
        deal_kernel, deal_shapes, [whole(queries)] * 3 + [whole(clip_row)],
        [whole(s) for s in deal_shapes], [], at_me, queries, keys, values, clip_row, limit=ALL_VMEM,
    )
    near_straight = lax.ppermute(near_own, "ctx", STRAIGHT)
    near_slanted = lax.ppermute(near_other, "ctx", SLANTED)
    mate = lax.ppermute(dealt, "ctx", BESIDE)
    mate_sums = lax.ppermute(sums, "ctx", BESIDE)
    row_sums = lax.ppermute(sums, "row", OTHER_ROW)
    mate_row_sums = lax.ppermute(sums, ("ctx", "row"), OPPOSITE)
    stream_shapes = [
        jax.ShapeDtypeStruct((FIRST_ROWS + SUM_ROWS, HD), bf16),
        jax.ShapeDtypeStruct((SECOND_ROWS, HD), bf16),
        jax.ShapeDtypeStruct((2, CHIP), f32),
    ]
    first_send, second_send, totals, info = call(
        pack_kernel, stream_shapes + [jax.ShapeDtypeStruct((9,), jnp.int32)],
        [held()] * 8, [whole(shape) for shape in stream_shapes[:2]] + [held()] + [pl.BlockSpec(memory_space=pltpu.SMEM)],
        [
            pltpu.VMEM((3, CHIP + NEAR, half), bf16),
            pltpu.VMEM((STREAM_ROWS + NEAR, HD), bf16),
        ],
        at_me, queries, keys, values, mate, sums, mate_sums, row_sums, mate_row_sums,
    )

    first_stream = lax.ppermute(first_send, "ctx", ACROSS)
    second_stream = lax.ppermute(second_send, "ctx", ACROSS)
    near_straight, near_slanted, sums, _ = lax.optimization_barrier(
        (near_straight, near_slanted, sums, first_send)
    )
    wave_shape = jax.ShapeDtypeStruct((2 * CHIP, HD), f32)
    cosine, sine, mask_ids = call(
        waves_kernel, [wave_shape, wave_shape, jax.ShapeDtypeStruct((1, 2 * CHIP), f32)],
        [pl.BlockSpec(memory_space=pltpu.SMEM)] + [held()] * 3, [held()] * 3,
        [pltpu.VMEM((1, CHIP), f32)], info, clip_grid, sums, mate_sums, frequencies(),
    )
    gains = (gain_q[None, :], gain_k[None, :])
    local_shape = jax.ShapeDtypeStruct((3, CHIP, half), bf16)
    local = call(
        turn_kernel, local_shape, [held()] * 9, held(), [pltpu.VMEM((4, CHIP, HD), f32)],
        info, queries, keys, values, mate, cosine, sine, totals, *gains,
    )
    common = (local, near_straight, near_slanted, gains, mask_ids)
    flex_here, flex_send, back_send, far_waves = attend(
        True, HALF, HALF, info, (first_stream,), (cosine, sine), *common
    )
    back_here = lax.ppermute(back_send, "ctx", ACROSS)
    flex_there = lax.ppermute(flex_send, "ctx", BESIDE)
    fixed_here, fixed_send = attend(
        False, 0, HALF, info, (first_stream, second_stream), (far_waves,), *common
    )
    fixed_there = lax.ppermute(fixed_send, "ctx", BESIDE)
    back_here, _ = lax.optimization_barrier((back_here, fixed_send))
    back_there = lax.ppermute(back_here, "ctx", BESIDE)
    out_shape = jax.ShapeDtypeStruct((ROWS, width), bf16)
    operands = (
        flex_here, fixed_here, flex_there, fixed_there, back_here, back_there, clip_row
    )
    return call(
        join_kernel, out_shape, [held()] * len(operands), whole(out_shape),
        [pltpu.VMEM((BACK_ROWS + REST, HD), bf16), pltpu.VMEM((2 * REST, HD), bf16)],
        info, *operands,
    )


def lookup(lookup_table, positions):
    labels = jnp.arange(lookup_table.shape[0], dtype=jnp.int32)
    return jnp.sum(
        jnp.where(positions[:, None] == labels[None, :], lookup_table[None, :], 0), axis=1
    )


def spin(matrix, offsets, clip_of, clip_grid, head_size):
    row_count = matrix.shape[0]
    sixth_part = head_size // 6
    first_dims = head_size - 4 * sixth_part
    first_freqs = 1.0 / ROTARY_BASE ** (
        jnp.arange(0, first_dims, 2, dtype=jnp.float32) / first_dims
    )
    other_freqs = 1.0 / ROTARY_BASE ** (
        jnp.arange(0, 2 * sixth_part, 2, dtype=jnp.float32) / (2 * sixth_part)
    )
    heights = lookup(clip_grid[:, 0], clip_of)
    widths = lookup(clip_grid[:, 1], clip_of)
    frame_pos = offsets // (heights * widths)
    line_pos = offsets // widths % heights
    column_pos = offsets % widths
    angles = jnp.concatenate(
        [
            frame_pos.astype(jnp.float32)[:, None] * first_freqs[None, :],
            line_pos.astype(jnp.float32)[:, None] * other_freqs[None, :],
            column_pos.astype(jnp.float32)[:, None] * other_freqs[None, :],
        ],
        axis=1,
    )
    cosine = jnp.repeat(jnp.cos(angles), 2, axis=1)
    sine_table = jnp.repeat(jnp.sin(angles), 2, axis=1)
    feature = jnp.arange(head_size, dtype=jnp.int32)
    is_even = (feature % 2 == 0)[None, None, :]
    head_view = matrix.reshape(row_count, -1, head_size)
    partner = jnp.where(is_even, -jnp.roll(head_view, -1, axis=2), jnp.roll(head_view, 1, axis=2))
    turned = head_view * cosine[:, None, :] + partner * sine_table[:, None, :]
    return turned.reshape(row_count, -1)


def on_any(queries, keys, values, gain_q, gain_k, clip_ids, clip_grid):
    rows_here, width_here = queries.shape
    heads_here = width_here // HD
    score_scale = 1.0 / math.sqrt(HD)
    query_wide = queries.astype(jnp.float32)
    key_wide = keys.astype(jnp.float32)
    squares = lax.psum(
        (jnp.sum(query_wide * query_wide, axis=1), jnp.sum(key_wide * key_wide, axis=1)), "row"
    )
    query_scale = lax.rsqrt(squares[0] / D + EPSILON)
    key_scale = lax.rsqrt(squares[1] / D + EPSILON)
    labels = jnp.arange(CLIPS, dtype=jnp.int32)
    local_counts = jnp.sum((clip_ids[:, None] == labels[None, :]).astype(jnp.int32), axis=0)
    totals = lax.psum(local_counts, "ctx")
    starts = jnp.cumsum(totals) - totals
    first_row = lax.axis_index("ctx") * rows_here
    offsets = first_row + jnp.arange(rows_here, dtype=jnp.int32) - lookup(starts, clip_ids)
    query_rot = spin(
        query_wide * query_scale[:, None] * gain_q[None, :], offsets, clip_ids, clip_grid, HD
    ).astype(jnp.bfloat16)
    query_heads = query_rot.reshape(rows_here, heads_here, HD)
    key_send = spin(
        key_wide * key_scale[:, None] * gain_k[None, :], offsets, clip_ids, clip_grid, HD
    ).astype(jnp.bfloat16)
    initial = (
        jnp.full((heads_here, rows_here), NEGATIVE, jnp.float32),
        jnp.zeros((heads_here, rows_here), jnp.float32),
        jnp.zeros((rows_here, heads_here, HD), jnp.float32),
    )
    running = initial
    piece_start = jnp.int32(0)
    key_piece = lax.all_gather(key_send, "ctx", axis=0, tiled=True)
    value_piece = lax.all_gather(values, "ctx", axis=0, tiled=True)
    row_count = key_piece.shape[0]
    block_rows = min(row_count, block_limit)
    for block_first in range(0, row_count, block_rows):
        block_size = min(block_rows, row_count - block_first)
        fold_key_rows = key_piece[block_first : block_first + block_size]
        fold_value_rows = value_piece[block_first : block_first + block_size]
        key_index = piece_start + block_first + jnp.arange(fold_key_rows.shape[0], dtype=jnp.int32)
        key_key_clips = (
            jnp.sum((starts[None, :] <= key_index[:, None]).astype(jnp.int32), axis=1) - 1
        )
        peak_old, total_old, summed_old = running
        key_view = fold_key_rows.reshape(fold_key_rows.shape[0], heads_here, HD)
        value_view = fold_value_rows.reshape(fold_value_rows.shape[0], heads_here, HD)
        scores = (
            jnp.einsum("qhd,khd->hqk", query_heads, key_view, preferred_element_type=jnp.float32)
            * score_scale
        )
        same = clip_ids[:, None] == key_key_clips[None, :]
        masked = jnp.where(same[None, :, :], scores, NEGATIVE)
        peak_new = jnp.maximum(peak_old, jnp.max(masked, axis=2))
        weights = jnp.where(same[None, :, :], jnp.exp(masked - peak_new[:, :, None]), 0.0)
        factor = jnp.exp(peak_old - peak_new)
        total_new = total_old * factor + jnp.sum(weights, axis=2)
        summed = summed_old * jnp.transpose(factor)[:, :, None] + jnp.einsum(
            "hqk,khd->qhd",
            weights.astype(jnp.bfloat16),
            value_view,
            preferred_element_type=jnp.float32,
        )
        running = (peak_new, total_new, summed)
    attended = running[2] / jnp.transpose(running[1])[:, :, None]
    return attended.reshape(rows_here, width_here).astype(jnp.bfloat16)


def solution(mesh):
    in_specs = (
        P(("batch", "ctx"), "row"),
        P(("batch", "ctx"), "row"),
        P(("batch", "ctx"), "row"),
        P("row"),
        P("row"),
        P(("batch", "ctx")),
        P("batch", None),
    )
    out_specs = P(("batch", "ctx"), "row")
    pair_of_chips = mesh.shape["ctx"] == 4 and mesh.shape["row"] == 2
    return jax.shard_map(
        on_device if pair_of_chips else on_any,
        mesh=mesh, in_specs=in_specs, out_specs=out_specs, check_vma=False,
    )
```

```python
import functools
import math

import jax
import jax.numpy as jnp
from jax import lax
from jax.experimental import pallas as pl
from jax.experimental.pallas import tpu as pltpu
from jax.sharding import PartitionSpec as P

HD = 128
D = 5120
CLIPS = 4
EPSILON = 1e-06
NEGATIVE = -1e30
ROTARY_BASE = 10000.0
block_limit = 1024

ROWS = 192
CHIP = 2 * ROWS
MOST = 480
NEAR = 96
REST = CHIP - NEAR
HALF = 5
WIDE = HALF * HD
TILE = 192
SHORT = 640
FIRST_ROWS = 1600
SECOND_ROWS = 1600
SUM_ROWS = 32
STREAM_ROWS = FIRST_ROWS + SECOND_ROWS
BACK_ROWS = 640
ACROSS = ((0, 2), (1, 3), (2, 0), (3, 1))
BESIDE = ((0, 1), (1, 0), (2, 3), (3, 2))
STRAIGHT = ((1, 3), (2, 0))
SLANTED = ((1, 2), (2, 1))
OTHER_ROW = ((0, 1), (1, 0))
OPPOSITE = tuple((2 * a + r, 2 * b + 1 - r) for a, b in BESIDE for r in (0, 1))
SCORE_SCALE = math.log2(math.e) / math.sqrt(HD)
VMEM = 24 * 1024 * 1024
ALL_VMEM = 60 * 1024 * 1024


def plan(start, side):
    first = start // 16 * 16
    last = (start + MOST + 15) // 16 * 16
    below, above = CHIP - first, last - CHIP
    mine = jnp.where(side == 0, below, above)
    theirs = jnp.where(side == 0, above, below)
    most = jnp.maximum(mine, theirs)
    lent = sum((most > limit).astype(jnp.int32) for limit in (256, 272, 288, 320, 352))
    return first, mine, theirs, HALF - lent, (mine > theirs).astype(jnp.int32)


def position():
    me = lax.axis_index("ctx")
    return me // 2, lax.rem(me, 2)


def known(info):
    row = info[...]
    lane = lax.broadcasted_iota(jnp.int32, row.shape, 1)
    start = jnp.sum(jnp.where(lane == 0, row, 0.0)).astype(jnp.int32)
    side, core = position()
    return side, core, start, row[:, 1:2], plan(start, side)


def sixteen(offset):
    return pl.multiple_of(offset, 16)


def deal_kernel(q_ref, k_ref, v_ref, ids, out, near_own, near_other, sums):
    side, core = position()
    half = out.shape[2]
    at = pl.ds(pl.multiple_of((1 - core) * half, 128), half)
    own = pl.ds(pl.multiple_of(core * half, 128), half)
    rows = pl.ds(sixteen((1 - side) * NEAR), NEAR)
    for i, ref in enumerate((k_ref, v_ref)):
        near_own[i] = ref[rows, own]
        near_other[i] = ref[rows, at]
    for i, ref in enumerate((q_ref, k_ref, v_ref)):
        out[i] = ref[:, at]
    for i, ref in enumerate((q_ref, k_ref)):
        lanes = jnp.zeros((ROWS, HD), jnp.float32)
        for column in range(0, ref.shape[1], HD):
            x = ref[:, column : column + HD].astype(jnp.float32)
            lanes += x * x
        sums[i : i + 1, :] = jnp.sum(jnp.transpose(lanes), axis=0, keepdims=True)
    sums[2:3, :] = ids[...].astype(jnp.float32)


def side_by_side(core, here, there, out):
    for ref, at in ((here, 0), (there, 1)):

        @pl.when(core == at)
        def _():
            out[:, :ROWS] = ref

        @pl.when(core != at)
        def _():
            out[:, ROWS:] = ref


def pack_kernel(
    q_ref, k_ref, v_ref, mate, sums, mate_sums, row_sums, mate_row_sums,
    first_out, second_out, totals, info, chip, buffer,
):
    side, core = position()
    here, there = sums[2:3, :], mate_sums[2:3, :]
    edge = jnp.where(
        side == 0,
        jnp.maximum(jnp.max(here), jnp.max(there)),
        jnp.minimum(jnp.min(here), jnp.min(there)),
    )
    count = (
        jnp.sum(jnp.where(here == edge, 1.0, 0.0)) + jnp.sum(jnp.where(there == edge, 1.0, 0.0))
    ).astype(jnp.int32)
    start = jnp.where(side == 0, CHIP - count, count - NEAR)
    first, mine, _, kept, major = plan(start, side)
    lane = lax.broadcasted_iota(jnp.int32, info.shape, 1)
    info[...] = jnp.where(lane == 0, start.astype(jnp.float32), edge)
    half = chip.shape[2]
    columns = pl.ds(pl.multiple_of(core * half, 128), half)
    for i, ref in enumerate((q_ref, k_ref, v_ref)):
        chip[i, pl.ds(sixteen(core * ROWS), ROWS), :] = ref[:, columns]
        chip[i, pl.ds(sixteen((1 - core) * ROWS), ROWS), :] = mate[i]
        chip[i, CHIP:, :] = jnp.zeros((NEAR, half), ref.dtype)
    buffer[...] = jnp.zeros_like(buffer)
    near_at = jnp.where(side == 0, REST, 0)
    rest_at = jnp.where(side == 0, first, NEAR)
    rest = mine - NEAR

    def put(offset, which, head, row, length):
        at = slice(head * HD, (head + 1) * HD)

        def step(i, carry):
            buffer[pl.ds(sixteen(offset + i * NEAR), NEAR), :] = chip[
                which, pl.ds(sixteen(row + i * NEAR), NEAR), at
            ]
            return carry

        lax.fori_loop(0, (length + NEAR - 1) // NEAR, step, 0)

    offset = jnp.int32(0)
    for i in range(HALF):
        head = HALF + i
        lend = jnp.logical_and(i >= kept, major == 0)
        send = jnp.logical_or(i < kept, major == 0)
        put(offset, 0, head, near_at, jnp.where(lend, NEAR, 0))
        offset += jnp.where(lend, NEAR, 0)
        put(offset, 0, head, rest_at, jnp.where(lend, rest, 0))
        offset += jnp.where(lend, rest, 0)
        length = jnp.where(send, rest, 0)
        for which in (1, 2):
            put(offset, which, head, rest_at, length)
            offset += length
    for head in range(HALF):
        for which in (1, 2):
            put(offset, which, head, rest_at, rest)
            offset += rest
    side_by_side(
        core, sums[:2, :] + row_sums[:2, :], mate_sums[:2, :] + mate_row_sums[:2, :], totals
    )
    parts = []
    for i in range(2):
        left = totals[i : i + 1, :]
        for _ in range(3):
            part = left.astype(jnp.bfloat16)
            left = left - part.astype(jnp.float32)
            parts += [part[:, t : t + HD] for t in range(0, CHIP, HD)]
    parts += [jnp.zeros_like(parts[0])] * (SUM_ROWS - len(parts))
    first_out[:FIRST_ROWS, :] = buffer[:FIRST_ROWS, :]
    first_out[FIRST_ROWS:, :] = jnp.concatenate(parts, axis=0)
    second_out[...] = buffer[FIRST_ROWS:STREAM_ROWS, :]


def turn(x, gain, gain_s, swap, cosine, sine):
    other = jnp.dot(x, swap, preferred_element_type=jnp.float32)
    return ((x.astype(jnp.float32) * gain) * cosine + (other * gain_s) * sine).astype(jnp.bfloat16)


def flip(gain):
    size = gain.shape[1]
    even = lax.broadcasted_iota(jnp.int32, gain.shape, 1) % 2 == 0
    return jnp.where(even, pltpu.roll(gain, size - 1, 1), pltpu.roll(gain, 1, 1))


def signed_swap():
    at_row = lax.broadcasted_iota(jnp.int32, (HD, HD), 0)
    at_column = lax.broadcasted_iota(jnp.int32, (HD, HD), 1)
    sign = jnp.where(at_column % 2 == 0, -1.0, 1.0)
    return jnp.where(at_row == (at_column ^ 1), sign, 0.0).astype(jnp.bfloat16)


def attention(q, keys, bias, values):
    scores = lax.dot_general(
        q, keys, (((1,), (1,)), ((), ())), preferred_element_type=jnp.float32
    ) + bias
    peak = jnp.max(scores, axis=1, keepdims=True)
    weights = jnp.exp2((scores - peak) * SCORE_SCALE).astype(jnp.bfloat16)
    columns = jnp.concatenate([values, jnp.ones_like(values)], axis=1)
    sums = jnp.dot(weights, columns, preferred_element_type=jnp.float32)
    return (sums[:, :HD] / sums[:, HD:]).astype(jnp.bfloat16)


def columns_of(row):
    return jnp.transpose(jnp.broadcast_to(row, (HD, row.shape[1])))


def waves_kernel(grid, info, sums, mate_sums, freqs, cosine, sine, ids, chip_ids):
    side, core, start, edge, (first, *_) = known(info)
    side_by_side(core, sums[2:3, :], mate_sums[2:3, :], chip_ids)
    here = chip_ids[...]
    slot = lax.broadcasted_iota(jnp.int32, (1, CHIP), 1)
    rest_start = jnp.where(side == 0, CHIP, first - NEAR)
    rest_end = jnp.where(side == 0, start + MOST, REST)
    token = slot + jnp.where(slot < NEAR, jnp.where(side == 0, CHIP, REST), rest_start)
    valid = jnp.logical_or(
        slot < NEAR, jnp.logical_and(token >= start, token < rest_end)
    )
    ids[:, :CHIP] = here
    ids[:, CHIP:] = jnp.where(valid, edge, -1.0)
    place = slot.astype(jnp.float32)
    offset, height, line_size = place, jnp.zeros_like(place), jnp.zeros_like(place)
    for label in range(CLIPS):
        same = here == float(label)
        below = jnp.sum(jnp.where(here < float(label), 1.0, 0.0), axis=1, keepdims=True)
        offset = offset - jnp.where(same, below, 0.0)
        height = height + jnp.where(same, grid[label, 0].astype(jnp.float32), 0.0)
        line_size = line_size + jnp.where(same, grid[label, 1].astype(jnp.float32), 0.0)
    carried = jnp.logical_and(here == edge, side == 1)
    offset = jnp.where(carried, place + (CHIP - start).astype(jnp.float32), offset)
    far_offset = jnp.maximum(token - start, 0).astype(jnp.float32)
    ones = jnp.ones_like(place)
    offset = jnp.concatenate([offset, far_offset], axis=1)
    far_sizes = []
    for axis in range(2):
        sizes = [jnp.where(edge == float(c), grid[c, axis].astype(jnp.float32), 0.0) for c in range(CLIPS)]
        far_sizes.append(ones * sum(sizes))
    height = jnp.concatenate([height, far_sizes[0]], axis=1)
    line_size = jnp.concatenate([line_size, far_sizes[1]], axis=1)
    frame = jnp.floor((offset + 0.5) / (height * line_size))
    offset = offset - frame * (height * line_size)
    line = jnp.floor((offset + 0.5) / line_size)
    column = offset - line * line_size
    sixth_part = HD // 6
    first_dims = HD - 4 * sixth_part
    feature = lax.broadcasted_iota(jnp.int32, (1, HD), 1)
    angles = freqs[...] * jnp.where(
        feature < first_dims,
        columns_of(frame),
        jnp.where(feature < first_dims + 2 * sixth_part, columns_of(line), columns_of(column)),
    )
    cosine[...] = jnp.cos(angles)
    sine[...] = jnp.sin(angles)


def turn_kernel(q_ref, k_ref, v_ref, mate, cosine, sine, totals, gq, gk, out, table):
    _, core = position()
    half = out.shape[2]
    columns = pl.ds(pl.multiple_of(core * half, 128), half)
    swap = signed_swap()
    for i in range(2):
        scale = columns_of(lax.rsqrt(totals[i : i + 1, :] / D + EPSILON))
        for j, ref in enumerate((cosine, sine)):
            table[2 * i + j] = ref[:CHIP, :] * scale
    for here, rows in ((True, core), (False, 1 - core)):
        rows = pl.ds(sixteen(rows * ROWS), ROWS)
        out[2, rows, :] = v_ref[:, columns] if here else mate[2]
        for i, (ref, gains) in enumerate(((q_ref, gq), (k_ref, gk))):
            cos_here, sin_here = table[2 * i, rows, :], table[2 * i + 1, rows, :]
            for h in range(half // HD):
                at = slice(h * HD, (h + 1) * HD)
                place = pl.ds(pl.multiple_of(core * half + h * HD, 128), HD)
                gain = gains[:, place]
                x = ref[:, place] if here else mate[i, :, at]
                out[i, rows, at] = turn(x, gain, flip(gain), swap, cos_here, sin_here)


def attend_kernel(flexible, head, count, info, *refs):
    local, near_straight, near_slanted, gq, gk, ids = refs[:6]
    streams = 1 if flexible else 2
    refs = refs[6:]
    if flexible:
        (cosine, sine), refs = refs[:2], refs[2:]
    else:
        table, refs = refs[0], refs[1:]
    arrived, refs = refs[:streams], refs[streams:]
    own_out, mate_out, refs = refs[0], refs[1], refs[2:]
    if flexible:
        back, table, refs = refs[0], refs[1], refs[2:]
    near, stream, bias, keys, values, result, sems = refs[:7]
    side, core, _, edge, (first, _, theirs, kept, major) = known(info)
    inner = side != core
    rest = theirs - NEAR
    near_columns = slice(head * HD, (head + count) * HD)
    sizes = (FIRST_ROWS, SECOND_ROWS)[:streams]
    copies, filled = [], 0
    for i, (ref, size) in enumerate(zip(arrived, sizes)):
        copies.append(
            pltpu.make_async_copy(
                ref.at[:size, :], stream.at[filled : filled + size, :], sems.at[1 + i]
            )
        )
        filled += size
    near_copies = [
        pltpu.make_async_copy(ref.at[:, :, near_columns], near, sems.at[0])
        for ref in (near_slanted, near_straight)
    ]
    for copy in copies:
        copy.start()
    pl.when(inner)(near_copies[0].start)
    pl.when(jnp.logical_not(inner))(near_copies[1].start)
    stream[filled:, :] = jnp.zeros((REST, HD), stream.dtype)

    columns = pl.ds(pl.multiple_of((2 * HALF * core + head) * HD, 128), count * HD)
    gq, gk = gq[:, columns], gk[:, columns]
    clip_of = columns_of(ids[:, :CHIP])
    for t in range(0, 2 * CHIP, HD):
        bias[:, t : t + HD] = jnp.where(clip_of == ids[:, t : t + HD], 0.0, NEGATIVE)
    for h in range(count):
        here = slice((head + h) * HD, (head + h + 1) * HD)
        keys[h, :CHIP, :] = local[1, :, here]
        values[h, :CHIP, :] = local[2, :, here]
    if flexible:
        back_rows, asked, scales, extra = refs[7:11]
        sum_copy = pltpu.make_async_copy(arrived[0].at[FIRST_ROWS:, :], extra, sems.at[4])
        sum_copy.start()
        near_rows = pl.ds(sixteen(jnp.where(side == 0, 0, REST)), NEAR)
        rest_rows = pl.ds(sixteen(jnp.where(side == 0, NEAR, first)), REST)
        scales[CHIP:, :] = jnp.ones((REST, HD), jnp.float32)
        back_rows[...] = jnp.zeros_like(back_rows)
        sum_copy.wait()
        parts = extra[...].astype(jnp.float32)
        for i, waves in enumerate((asked, table)):
            for j in range(3):
                total = sum(parts[9 * i + 3 * p + j : 9 * i + 3 * p + j + 1, :] for p in range(3))
                scales[j * HD : (j + 1) * HD, :] = columns_of(lax.rsqrt(total / D + EPSILON))
            for j, ref in enumerate((cosine, sine)):
                waves[j, :NEAR, :] = ref[CHIP : CHIP + NEAR, :] * scales[near_rows, :]
                waves[j, NEAR:, :] = ref[CHIP + NEAR :, :] * scales[rest_rows, :]
    near_copies[0].wait()
    for copy in copies:
        copy.wait()

    swap = signed_swap()
    if flexible:
        base = jnp.int32(0)
    else:
        base = 2 * rest * kept + jnp.where(major == 1, (HALF - kept) * (2 * rest + theirs), 0)
        base += 2 * rest * head
    bases = []
    for h in range(count):
        at = slice(h * HD, (h + 1) * HD)
        gain = gk[:, at]
        key_at = base
        bases.append(base)
        if flexible:
            lend = jnp.logical_and(h >= kept, major == 1)
            took = jnp.logical_or(h < kept, major == 1)
            key_at = base + jnp.where(lend, theirs, 0)
            base += jnp.where(took, 2 * rest, 0) + jnp.where(lend, theirs, 0)
        else:
            base += 2 * rest
        far = jnp.concatenate([near[0, :, at], stream[pl.ds(sixteen(key_at), REST), :]], axis=0)
        keys[h, CHIP:, :] = turn(far, gain, flip(gain), swap, table[0], table[1])
        values[h, CHIP : CHIP + NEAR, :] = near[1, :, at]
        values[h, CHIP + NEAR :, :] = stream[pl.ds(sixteen(key_at + rest), REST), :]

    def far_answer(h, t):
        at = slice(h * HD, (h + 1) * HD)
        gain = gq[:, at]
        x = stream[pl.ds(sixteen(bases[h] + t), HD), :]
        far_q = turn(x, gain, flip(gain), swap, asked[0, t : t + HD, :], asked[1, t : t + HD, :])
        place = jnp.where(h >= kept, (h - kept) * theirs + t, BACK_ROWS + HD)
        back_rows[pl.ds(sixteen(place), HD), :] = attention(
            far_q, keys[h, :SHORT, :], far_bias, values[h, :SHORT, :]
        )

    def answers(seen, lent):
        for h in range(count):
            at = slice(h * HD, (h + 1) * HD)
            here = slice((head + h) * HD, (head + h + 1) * HD)
            for t in range(0, CHIP, TILE):
                rows = slice(t, t + TILE)
                result[rows, at] = attention(
                    local[0, rows, here], keys[h, :seen, :], bias[rows, :seen], values[h, :seen, :]
                )
            if lent:
                far_answer(h, 0)

    short = theirs <= SHORT - CHIP
    if flexible:
        far_bias = jnp.where(ids[:, :SHORT] == edge, 0.0, NEGATIVE)
        lending = jnp.logical_and(kept < HALF, major == 1)

        @pl.when(jnp.logical_and(lending, theirs > HD))
        def _():
            for h in range(count):
                far_answer(h, HD)

        pl.when(lending)(lambda: answers(SHORT, True))
        pl.when(jnp.logical_and(short, jnp.logical_not(lending)))(lambda: answers(SHORT, False))
    else:
        pl.when(short)(lambda: answers(SHORT, False))
    pl.when(jnp.logical_not(short))(lambda: answers(2 * CHIP, False))
    own_out[...] = result[pl.ds(sixteen(core * ROWS), ROWS), :]
    mate_out[...] = result[pl.ds(sixteen((1 - core) * ROWS), ROWS), :]
    if flexible:
        back[...] = back_rows[:BACK_ROWS, :]


def join_kernel(
    info, flex_here, fixed_here, flex_there, fixed_there, back_here, back_there, ids, out, rows, lines
):
    side, core, _, edge, (first, mine, _, kept, major) = known(info)
    half = 2 * WIDE
    inside = columns_of(ids[...].astype(jnp.float32)) == edge
    for here, flex, fixed, back in (
        (True, flex_here, fixed_here, back_here),
        (False, flex_there, fixed_there, back_there),
    ):
        column = pl.multiple_of((core if here else 1 - core) * half, 128)
        out[:, pl.ds(column, WIDE)] = fixed[...]
        out[:, pl.ds(pl.multiple_of(column + WIDE, 128), WIDE)] = flex[...]

        @pl.when(jnp.logical_and(major == 0, kept < HALF))
        def _():
            rows[:BACK_ROWS, :] = back[...]
            rows[BACK_ROWS:, :] = jnp.zeros((REST, HD), rows.dtype)
            for h in range(HALF):

                @pl.when(h >= kept)
                def _():
                    base = (h - kept) * mine
                    near_at = jnp.where(side == 0, REST, 0)
                    rest_at = jnp.where(side == 0, first, NEAR)
                    lines[pl.ds(sixteen(rest_at), REST), :] = rows[
                        pl.ds(sixteen(base + NEAR), REST), :
                    ]
                    lines[pl.ds(sixteen(near_at), NEAR), :] = rows[pl.ds(sixteen(base), NEAR), :]
                    at = slice(h * HD, (h + 1) * HD)
                    place = pl.ds(pl.multiple_of(column + WIDE + h * HD, 128), HD)
                    out[:, place] = jnp.where(
                        inside, lines[pl.ds(sixteen(core * ROWS), ROWS), :], flex[:, at]
                    )


def frequencies():
    sixth_part = HD // 6
    first_dims = HD - 4 * sixth_part
    first_freqs = 1.0 / ROTARY_BASE ** (
        jnp.arange(0, first_dims, 2, dtype=jnp.float32) / first_dims
    )
    other_freqs = 1.0 / ROTARY_BASE ** (
        jnp.arange(0, 2 * sixth_part, 2, dtype=jnp.float32) / (2 * sixth_part)
    )
    return jnp.repeat(jnp.concatenate([first_freqs, other_freqs, other_freqs]), 2)[None, :]


def whole(a):
    return pl.BlockSpec(a.shape, lambda i: (0,) * len(a.shape))


def held():
    return pl.BlockSpec(memory_space=pltpu.VMEM)


def call(kernel, out_shape, in_specs, out_specs, scratch, *operands, limit=VMEM):
    return pl.pallas_call(
        kernel,
        grid=(1,),
        out_shape=out_shape,
        in_specs=in_specs,
        out_specs=out_specs,
        scratch_shapes=scratch,
        compiler_params=pltpu.CompilerParams(vmem_limit_bytes=limit),
        cost_estimate=pl.CostEstimate(flops=0, bytes_accessed=0, transcendentals=0),
    )(*operands)


def attend(flexible, head, count, info, streams, waves, local, near_straight, near_slanted, gains, ids):
    bf16, f32 = jnp.bfloat16, jnp.float32
    there = pl.BlockSpec(memory_space=pl.ANY)
    shapes = [jax.ShapeDtypeStruct((ROWS, count * HD), bf16)] * 2
    stream_rows = sum((FIRST_ROWS, SECOND_ROWS)[: len(streams)]) + REST
    scratch = [
        pltpu.VMEM((2, NEAR, count * HD), bf16),
        pltpu.VMEM((stream_rows, HD), bf16),
        pltpu.VMEM((CHIP, 2 * CHIP), f32),
        pltpu.VMEM((count, 2 * CHIP, HD), bf16),
        pltpu.VMEM((count, 2 * CHIP, HD), bf16),
        pltpu.VMEM((CHIP, count * HD), bf16),
        pltpu.SemaphoreType.DMA((5,)),
    ]
    if flexible:
        far_waves = jax.ShapeDtypeStruct((2, CHIP, HD), f32)
        shapes = shapes + [jax.ShapeDtypeStruct((BACK_ROWS, HD), bf16), far_waves]
        scratch = scratch + [
            pltpu.VMEM((BACK_ROWS + 2 * HD, HD), bf16),
            pltpu.VMEM((2, CHIP, HD), f32),
            pltpu.VMEM((CHIP + REST, HD), f32),
            pltpu.VMEM((SUM_ROWS, HD), bf16),
        ]
    operands = (local, near_straight, near_slanted, *gains, ids, *waves, *streams)
    in_specs = [held(), held(), there, there] + [held()] * (3 + len(waves)) + [there] * len(streams)
    return call(
        functools.partial(attend_kernel, flexible, head, count), shapes,
        in_specs, [held()] * len(shapes), scratch, info, *operands,
    )


def on_device(queries, keys, values, gain_q, gain_k, clip_ids, clip_grid):
    width = queries.shape[1]
    half = width // 2
    bf16, f32 = jnp.bfloat16, jnp.float32

    clip_row = clip_ids[None, :]

    near_shape = jax.ShapeDtypeStruct((2, NEAR, half), bf16)
    deal_shapes = [
        jax.ShapeDtypeStruct((3, ROWS, half), bf16),
        near_shape,
        near_shape,
        jax.ShapeDtypeStruct((3, ROWS), f32),
    ]
    dealt, near_own, near_other, sums = call(
        deal_kernel, deal_shapes, [whole(queries)] * 3 + [whole(clip_row)],
        [whole(s) for s in deal_shapes], [], queries, keys, values, clip_row, limit=ALL_VMEM,
    )
    near_straight = lax.ppermute(near_own, "ctx", STRAIGHT)
    near_slanted = lax.ppermute(near_other, "ctx", SLANTED)
    mate = lax.ppermute(dealt, "ctx", BESIDE)
    mate_sums = lax.ppermute(sums, "ctx", BESIDE)
    row_sums = lax.ppermute(sums, "row", OTHER_ROW)
    mate_row_sums = lax.ppermute(sums, ("ctx", "row"), OPPOSITE)
    stream_shapes = [
        jax.ShapeDtypeStruct((FIRST_ROWS + SUM_ROWS, HD), bf16),
        jax.ShapeDtypeStruct((SECOND_ROWS, HD), bf16),
        jax.ShapeDtypeStruct((2, CHIP), f32),
    ]
    first_send, second_send, totals, info = call(
        pack_kernel, stream_shapes + [jax.ShapeDtypeStruct((1, HD), f32)],
        [held()] * 8, [whole(shape) for shape in stream_shapes[:2]] + [held()] * 2,
        [
            pltpu.VMEM((3, CHIP + NEAR, half), bf16),
            pltpu.VMEM((STREAM_ROWS + NEAR, HD), bf16),
        ],
        queries, keys, values, mate, sums, mate_sums, row_sums, mate_row_sums,
    )

    first_stream = lax.ppermute(first_send, "ctx", ACROSS)
    second_stream = lax.ppermute(second_send, "ctx", ACROSS)
    near_straight, near_slanted, sums, _ = lax.optimization_barrier(
        (near_straight, near_slanted, sums, first_send)
    )
    wave_shape = jax.ShapeDtypeStruct((2 * CHIP, HD), f32)
    cosine, sine, mask_ids = call(
        waves_kernel, [wave_shape, wave_shape, jax.ShapeDtypeStruct((1, 2 * CHIP), f32)],
        [pl.BlockSpec(memory_space=pltpu.SMEM)] + [held()] * 4, [held()] * 3,
        [pltpu.VMEM((1, CHIP), f32)], clip_grid, info, sums, mate_sums, frequencies(),
    )
    gains = (gain_q[None, :], gain_k[None, :])
    local_shape = jax.ShapeDtypeStruct((3, CHIP, half), bf16)
    local = call(
        turn_kernel, local_shape, [held()] * 9, held(), [pltpu.VMEM((4, CHIP, HD), f32)],
        queries, keys, values, mate, cosine, sine, totals, *gains,
    )
    common = (local, near_straight, near_slanted, gains, mask_ids)
    flex_here, flex_send, back_send, far_waves = attend(
        True, HALF, HALF, info, (first_stream,), (cosine, sine), *common
    )
    back_here = lax.ppermute(back_send, "ctx", ACROSS)
    fixed_here, fixed_send = attend(
        False, 0, HALF, info, (first_stream, second_stream), (far_waves,), *common
    )
    flex_send, fixed_send = lax.optimization_barrier((flex_send, fixed_send))
    flex_there = lax.ppermute(flex_send, "ctx", BESIDE)
    fixed_there = lax.ppermute(fixed_send, "ctx", BESIDE)
    back_here, _ = lax.optimization_barrier((back_here, fixed_send))
    back_there = lax.ppermute(back_here, "ctx", BESIDE)
    out_shape = jax.ShapeDtypeStruct((ROWS, width), bf16)
    operands = (
        flex_here, fixed_here, flex_there, fixed_there, back_here, back_there, clip_row
    )
    return call(
        join_kernel, out_shape, [held()] * 8, whole(out_shape),
        [pltpu.VMEM((BACK_ROWS + REST, HD), bf16), pltpu.VMEM((2 * REST, HD), bf16)],
        info, *operands,
    )


def lookup(lookup_table, positions):
    labels = jnp.arange(lookup_table.shape[0], dtype=jnp.int32)
    return jnp.sum(
        jnp.where(positions[:, None] == labels[None, :], lookup_table[None, :], 0), axis=1
    )


def spin(matrix, offsets, clip_of, clip_grid, head_size):
    row_count = matrix.shape[0]
    sixth_part = head_size // 6
    first_dims = head_size - 4 * sixth_part
    first_freqs = 1.0 / ROTARY_BASE ** (
        jnp.arange(0, first_dims, 2, dtype=jnp.float32) / first_dims
    )
    other_freqs = 1.0 / ROTARY_BASE ** (
        jnp.arange(0, 2 * sixth_part, 2, dtype=jnp.float32) / (2 * sixth_part)
    )
    heights = lookup(clip_grid[:, 0], clip_of)
    widths = lookup(clip_grid[:, 1], clip_of)
    frame_pos = offsets // (heights * widths)
    line_pos = offsets // widths % heights
    column_pos = offsets % widths
    angles = jnp.concatenate(
        [
            frame_pos.astype(jnp.float32)[:, None] * first_freqs[None, :],
            line_pos.astype(jnp.float32)[:, None] * other_freqs[None, :],
            column_pos.astype(jnp.float32)[:, None] * other_freqs[None, :],
        ],
        axis=1,
    )
    cosine = jnp.repeat(jnp.cos(angles), 2, axis=1)
    sine_table = jnp.repeat(jnp.sin(angles), 2, axis=1)
    feature = jnp.arange(head_size, dtype=jnp.int32)
    is_even = (feature % 2 == 0)[None, None, :]
    head_view = matrix.reshape(row_count, -1, head_size)
    partner = jnp.where(is_even, -jnp.roll(head_view, -1, axis=2), jnp.roll(head_view, 1, axis=2))
    turned = head_view * cosine[:, None, :] + partner * sine_table[:, None, :]
    return turned.reshape(row_count, -1)


def on_any(queries, keys, values, gain_q, gain_k, clip_ids, clip_grid):
    rows_here, width_here = queries.shape
    heads_here = width_here // HD
    score_scale = 1.0 / math.sqrt(HD)
    query_wide = queries.astype(jnp.float32)
    key_wide = keys.astype(jnp.float32)
    squares = lax.psum(
        (jnp.sum(query_wide * query_wide, axis=1), jnp.sum(key_wide * key_wide, axis=1)), "row"
    )
    query_scale = lax.rsqrt(squares[0] / D + EPSILON)
    key_scale = lax.rsqrt(squares[1] / D + EPSILON)
    labels = jnp.arange(CLIPS, dtype=jnp.int32)
    local_counts = jnp.sum((clip_ids[:, None] == labels[None, :]).astype(jnp.int32), axis=0)
    totals = lax.psum(local_counts, "ctx")
    starts = jnp.cumsum(totals) - totals
    first_row = lax.axis_index("ctx") * rows_here
    offsets = first_row + jnp.arange(rows_here, dtype=jnp.int32) - lookup(starts, clip_ids)
    query_rot = spin(
        query_wide * query_scale[:, None] * gain_q[None, :], offsets, clip_ids, clip_grid, HD
    ).astype(jnp.bfloat16)
    query_heads = query_rot.reshape(rows_here, heads_here, HD)
    key_send = spin(
        key_wide * key_scale[:, None] * gain_k[None, :], offsets, clip_ids, clip_grid, HD
    ).astype(jnp.bfloat16)
    initial = (
        jnp.full((heads_here, rows_here), NEGATIVE, jnp.float32),
        jnp.zeros((heads_here, rows_here), jnp.float32),
        jnp.zeros((rows_here, heads_here, HD), jnp.float32),
    )
    running = initial
    piece_start = jnp.int32(0)
    key_piece = lax.all_gather(key_send, "ctx", axis=0, tiled=True)
    value_piece = lax.all_gather(values, "ctx", axis=0, tiled=True)
    row_count = key_piece.shape[0]
    block_rows = min(row_count, block_limit)
    for block_first in range(0, row_count, block_rows):
        block_size = min(block_rows, row_count - block_first)
        fold_key_rows = key_piece[block_first : block_first + block_size]
        fold_value_rows = value_piece[block_first : block_first + block_size]
        key_index = piece_start + block_first + jnp.arange(fold_key_rows.shape[0], dtype=jnp.int32)
        key_key_clips = (
            jnp.sum((starts[None, :] <= key_index[:, None]).astype(jnp.int32), axis=1) - 1
        )
        peak_old, total_old, summed_old = running
        key_view = fold_key_rows.reshape(fold_key_rows.shape[0], heads_here, HD)
        value_view = fold_value_rows.reshape(fold_value_rows.shape[0], heads_here, HD)
        scores = (
            jnp.einsum("qhd,khd->hqk", query_heads, key_view, preferred_element_type=jnp.float32)
            * score_scale
        )
        same = clip_ids[:, None] == key_key_clips[None, :]
        masked = jnp.where(same[None, :, :], scores, NEGATIVE)
        peak_new = jnp.maximum(peak_old, jnp.max(masked, axis=2))
        weights = jnp.where(same[None, :, :], jnp.exp(masked - peak_new[:, :, None]), 0.0)
        factor = jnp.exp(peak_old - peak_new)
        total_new = total_old * factor + jnp.sum(weights, axis=2)
        summed = summed_old * jnp.transpose(factor)[:, :, None] + jnp.einsum(
            "hqk,khd->qhd",
            weights.astype(jnp.bfloat16),
            value_view,
            preferred_element_type=jnp.float32,
        )
        running = (peak_new, total_new, summed)
    attended = running[2] / jnp.transpose(running[1])[:, :, None]
    return attended.reshape(rows_here, width_here).astype(jnp.bfloat16)


def solution(mesh):
    in_specs = (
        P(("batch", "ctx"), "row"),
        P(("batch", "ctx"), "row"),
        P(("batch", "ctx"), "row"),
        P("row"),
        P("row"),
        P(("batch", "ctx")),
        P("batch", None),
    )
    out_specs = P(("batch", "ctx"), "row")
    pair_of_chips = mesh.shape["ctx"] == 4 and mesh.shape["row"] == 2
    return jax.shard_map(
        on_device if pair_of_chips else on_any,
        mesh=mesh, in_specs=in_specs, out_specs=out_specs, check_vma=False,
    )
```

```python
import functools
import math

import jax
import jax.numpy as jnp
from jax import lax
from jax.experimental import pallas as pl
from jax.experimental.pallas import tpu as pltpu
from jax.sharding import PartitionSpec as P

HD = 128
D = 5120
CLIPS = 4
EPSILON = 1e-06
NEGATIVE = -1e30
ROTARY_BASE = 10000.0
block_limit = 1024

ROWS = 192
CHIP = 2 * ROWS
MOST = 480
NEAR = 96
REST = CHIP - NEAR
HALF = 5
WIDE = HALF * HD
TILE = 192
SHORT = 640
FIRST_ROWS = 1600
SECOND_ROWS = 1600
SUM_ROWS = 32
STREAM_ROWS = FIRST_ROWS + SECOND_ROWS
BACK_ROWS = 640
ACROSS = ((0, 2), (1, 3), (2, 0), (3, 1))
BESIDE = ((0, 1), (1, 0), (2, 3), (3, 2))
STRAIGHT = ((1, 3), (2, 0))
SLANTED = ((1, 2), (2, 1))
OTHER_ROW = ((0, 1), (1, 0))
OPPOSITE = tuple((2 * a + r, 2 * b + 1 - r) for a, b in BESIDE for r in (0, 1))
SCORE_SCALE = math.log2(math.e) / math.sqrt(HD)
VMEM = 24 * 1024 * 1024
ALL_VMEM = 60 * 1024 * 1024


def plan(start, side):
    first = start // 16 * 16
    last = (start + MOST + 15) // 16 * 16
    below, above = CHIP - first, last - CHIP
    mine = jnp.where(side == 0, below, above)
    theirs = jnp.where(side == 0, above, below)
    most = jnp.maximum(mine, theirs)
    lent = sum((most > limit).astype(jnp.int32) for limit in (256, 272, 288, 320, 352))
    return first, mine, theirs, HALF - lent, (mine > theirs).astype(jnp.int32)


def position():
    me = lax.axis_index("ctx")
    return me // 2, lax.rem(me, 2)


def known(info):
    row = info[...]
    lane = lax.broadcasted_iota(jnp.int32, row.shape, 1)
    start = jnp.sum(jnp.where(lane == 0, row, 0.0)).astype(jnp.int32)
    side, core = position()
    return side, core, start, row[:, 1:2], plan(start, side)


def sixteen(offset):
    return pl.multiple_of(offset, 16)


def deal_kernel(q_ref, k_ref, v_ref, ids, out, near_own, near_other, sums):
    side, core = position()
    half = out.shape[2]
    at = pl.ds(pl.multiple_of((1 - core) * half, 128), half)
    own = pl.ds(pl.multiple_of(core * half, 128), half)
    rows = pl.ds(sixteen((1 - side) * NEAR), NEAR)
    for i, ref in enumerate((k_ref, v_ref)):
        near_own[i] = ref[rows, own]
        near_other[i] = ref[rows, at]
    for i, ref in enumerate((q_ref, k_ref, v_ref)):
        out[i] = ref[:, at]
    for i, ref in enumerate((q_ref, k_ref)):
        lanes = jnp.zeros((ROWS, HD), jnp.float32)
        for column in range(0, ref.shape[1], HD):
            x = ref[:, column : column + HD].astype(jnp.float32)
            lanes += x * x
        sums[i : i + 1, :] = jnp.sum(jnp.transpose(lanes), axis=0, keepdims=True)
    sums[2:3, :] = ids[...].astype(jnp.float32)


def side_by_side(core, here, there, out):
    for ref, at in ((here, 0), (there, 1)):

        @pl.when(core == at)
        def _():
            out[:, :ROWS] = ref

        @pl.when(core != at)
        def _():
            out[:, ROWS:] = ref


def pack_kernel(
    q_ref, k_ref, v_ref, mate, sums, mate_sums, row_sums, mate_row_sums,
    first_out, second_out, totals, info, chip, buffer,
):
    side, core = position()
    here, there = sums[2:3, :], mate_sums[2:3, :]
    edge = jnp.where(
        side == 0,
        jnp.maximum(jnp.max(here), jnp.max(there)),
        jnp.minimum(jnp.min(here), jnp.min(there)),
    )
    count = (
        jnp.sum(jnp.where(here == edge, 1.0, 0.0)) + jnp.sum(jnp.where(there == edge, 1.0, 0.0))
    ).astype(jnp.int32)
    start = jnp.where(side == 0, CHIP - count, count - NEAR)
    first, mine, _, kept, major = plan(start, side)
    lane = lax.broadcasted_iota(jnp.int32, info.shape, 1)
    info[...] = jnp.where(lane == 0, start.astype(jnp.float32), edge)
    half = chip.shape[2]
    columns = pl.ds(pl.multiple_of(core * half, 128), half)
    for i, ref in enumerate((q_ref, k_ref, v_ref)):
        chip[i, pl.ds(sixteen(core * ROWS), ROWS), :] = ref[:, columns]
        chip[i, pl.ds(sixteen((1 - core) * ROWS), ROWS), :] = mate[i]
        chip[i, CHIP:, :] = jnp.zeros((NEAR, half), ref.dtype)
    buffer[...] = jnp.zeros_like(buffer)
    near_at = jnp.where(side == 0, REST, 0)
    rest_at = jnp.where(side == 0, first, NEAR)
    rest = mine - NEAR

    def put(offset, which, head, row, length):
        at = slice(head * HD, (head + 1) * HD)

        def step(i, carry):
            buffer[pl.ds(sixteen(offset + i * NEAR), NEAR), :] = chip[
                which, pl.ds(sixteen(row + i * NEAR), NEAR), at
            ]
            return carry

        lax.fori_loop(0, (length + NEAR - 1) // NEAR, step, 0)

    offset = jnp.int32(0)
    for i in range(HALF):
        head = HALF + i
        lend = jnp.logical_and(i >= kept, major == 0)
        send = jnp.logical_or(i < kept, major == 0)
        put(offset, 0, head, near_at, jnp.where(lend, NEAR, 0))
        offset += jnp.where(lend, NEAR, 0)
        put(offset, 0, head, rest_at, jnp.where(lend, rest, 0))
        offset += jnp.where(lend, rest, 0)
        length = jnp.where(send, rest, 0)
        for which in (1, 2):
            put(offset, which, head, rest_at, length)
            offset += length
    for head in range(HALF):
        for which in (1, 2):
            put(offset, which, head, rest_at, rest)
            offset += rest
    side_by_side(
        core, sums[:2, :] + row_sums[:2, :], mate_sums[:2, :] + mate_row_sums[:2, :], totals
    )
    parts = []
    for i in range(2):
        left = totals[i : i + 1, :]
        for _ in range(3):
            part = left.astype(jnp.bfloat16)
            left = left - part.astype(jnp.float32)
            parts += [part[:, t : t + HD] for t in range(0, CHIP, HD)]
    parts += [jnp.zeros_like(parts[0])] * (SUM_ROWS - len(parts))
    first_out[:FIRST_ROWS, :] = buffer[:FIRST_ROWS, :]
    first_out[FIRST_ROWS:, :] = jnp.concatenate(parts, axis=0)
    second_out[...] = buffer[FIRST_ROWS:STREAM_ROWS, :]


def turn(x, gain, gain_s, swap, cosine, sine):
    other = jnp.dot(x, swap, preferred_element_type=jnp.float32)
    return ((x.astype(jnp.float32) * gain) * cosine + (other * gain_s) * sine).astype(jnp.bfloat16)


def flip(gain):
    size = gain.shape[1]
    even = lax.broadcasted_iota(jnp.int32, gain.shape, 1) % 2 == 0
    return jnp.where(even, pltpu.roll(gain, size - 1, 1), pltpu.roll(gain, 1, 1))


def signed_swap():
    at_row = lax.broadcasted_iota(jnp.int32, (HD, HD), 0)
    at_column = lax.broadcasted_iota(jnp.int32, (HD, HD), 1)
    sign = jnp.where(at_column % 2 == 0, -1.0, 1.0)
    return jnp.where(at_row == (at_column ^ 1), sign, 0.0).astype(jnp.bfloat16)


def attention(q, keys, bias, values):
    scores = lax.dot_general(
        q, keys, (((1,), (1,)), ((), ())), preferred_element_type=jnp.float32
    ) + bias
    peak = jnp.max(scores, axis=1, keepdims=True)
    weights = jnp.exp2((scores - peak) * SCORE_SCALE).astype(jnp.bfloat16)
    columns = jnp.concatenate([values, jnp.ones_like(values)], axis=1)
    sums = jnp.dot(weights, columns, preferred_element_type=jnp.float32)
    return (sums[:, :HD] / sums[:, HD:]).astype(jnp.bfloat16)


def columns_of(row):
    return jnp.transpose(jnp.broadcast_to(row, (HD, row.shape[1])))


def waves_kernel(grid, info, sums, mate_sums, freqs, cosine, sine, ids, chip_ids):
    side, core, start, edge, (first, *_) = known(info)
    side_by_side(core, sums[2:3, :], mate_sums[2:3, :], chip_ids)
    here = chip_ids[...]
    slot = lax.broadcasted_iota(jnp.int32, (1, CHIP), 1)
    rest_start = jnp.where(side == 0, CHIP, first - NEAR)
    rest_end = jnp.where(side == 0, start + MOST, REST)
    token = slot + jnp.where(slot < NEAR, jnp.where(side == 0, CHIP, REST), rest_start)
    valid = jnp.logical_or(
        slot < NEAR, jnp.logical_and(token >= start, token < rest_end)
    )
    ids[:, :CHIP] = here
    ids[:, CHIP:] = jnp.where(valid, edge, -1.0)
    place = slot.astype(jnp.float32)
    offset, height, line_size = place, jnp.zeros_like(place), jnp.zeros_like(place)
    for label in range(CLIPS):
        same = here == float(label)
        below = jnp.sum(jnp.where(here < float(label), 1.0, 0.0), axis=1, keepdims=True)
        offset = offset - jnp.where(same, below, 0.0)
        height = height + jnp.where(same, grid[label, 0].astype(jnp.float32), 0.0)
        line_size = line_size + jnp.where(same, grid[label, 1].astype(jnp.float32), 0.0)
    carried = jnp.logical_and(here == edge, side == 1)
    offset = jnp.where(carried, place + (CHIP - start).astype(jnp.float32), offset)
    far_offset = jnp.maximum(token - start, 0).astype(jnp.float32)
    ones = jnp.ones_like(place)
    offset = jnp.concatenate([offset, far_offset], axis=1)
    far_sizes = []
    for axis in range(2):
        sizes = [jnp.where(edge == float(c), grid[c, axis].astype(jnp.float32), 0.0) for c in range(CLIPS)]
        far_sizes.append(ones * sum(sizes))
    height = jnp.concatenate([height, far_sizes[0]], axis=1)
    line_size = jnp.concatenate([line_size, far_sizes[1]], axis=1)
    frame = jnp.floor((offset + 0.5) / (height * line_size))
    offset = offset - frame * (height * line_size)
    line = jnp.floor((offset + 0.5) / line_size)
    column = offset - line * line_size
    sixth_part = HD // 6
    first_dims = HD - 4 * sixth_part
    feature = lax.broadcasted_iota(jnp.int32, (1, HD), 1)
    angles = freqs[...] * jnp.where(
        feature < first_dims,
        columns_of(frame),
        jnp.where(feature < first_dims + 2 * sixth_part, columns_of(line), columns_of(column)),
    )
    cosine[...] = jnp.cos(angles)
    sine[...] = jnp.sin(angles)


def turn_kernel(q_ref, k_ref, v_ref, mate, cosine, sine, totals, gq, gk, out, table):
    _, core = position()
    half = out.shape[2]
    columns = pl.ds(pl.multiple_of(core * half, 128), half)
    swap = signed_swap()
    for i in range(2):
        scale = columns_of(lax.rsqrt(totals[i : i + 1, :] / D + EPSILON))
        for j, ref in enumerate((cosine, sine)):
            table[2 * i + j] = ref[:CHIP, :] * scale
    for here, rows in ((True, core), (False, 1 - core)):
        rows = pl.ds(sixteen(rows * ROWS), ROWS)
        out[2, rows, :] = v_ref[:, columns] if here else mate[2]
        for i, (ref, gains) in enumerate(((q_ref, gq), (k_ref, gk))):
            cos_here, sin_here = table[2 * i, rows, :], table[2 * i + 1, rows, :]
            for h in range(half // HD):
                at = slice(h * HD, (h + 1) * HD)
                place = pl.ds(pl.multiple_of(core * half + h * HD, 128), HD)
                gain = gains[:, place]
                x = ref[:, place] if here else mate[i, :, at]
                out[i, rows, at] = turn(x, gain, flip(gain), swap, cos_here, sin_here)


def attend_kernel(flexible, head, count, info, *refs):
    local, near_straight, near_slanted, gq, gk, ids = refs[:6]
    streams = 1 if flexible else 2
    refs = refs[6:]
    if flexible:
        (cosine, sine), refs = refs[:2], refs[2:]
    else:
        table, refs = refs[0], refs[1:]
    arrived, refs = refs[:streams], refs[streams:]
    own_out, mate_out, refs = refs[0], refs[1], refs[2:]
    if flexible:
        back, table, refs = refs[0], refs[1], refs[2:]
    near, stream, bias, keys, values, result, sems = refs[:7]
    side, core, _, edge, (first, _, theirs, kept, major) = known(info)
    inner = side != core
    rest = theirs - NEAR
    near_columns = slice(head * HD, (head + count) * HD)
    sizes = (FIRST_ROWS, SECOND_ROWS)[:streams]
    copies, filled = [], 0
    for i, (ref, size) in enumerate(zip(arrived, sizes)):
        copies.append(
            pltpu.make_async_copy(
                ref.at[:size, :], stream.at[filled : filled + size, :], sems.at[1 + i]
            )
        )
        filled += size
    near_copies = [
        pltpu.make_async_copy(ref.at[:, :, near_columns], near, sems.at[0])
        for ref in (near_slanted, near_straight)
    ]
    for copy in copies:
        copy.start()
    pl.when(inner)(near_copies[0].start)
    pl.when(jnp.logical_not(inner))(near_copies[1].start)
    stream[filled:, :] = jnp.zeros((REST, HD), stream.dtype)

    columns = pl.ds(pl.multiple_of((2 * HALF * core + head) * HD, 128), count * HD)
    gq, gk = gq[:, columns], gk[:, columns]
    clip_of = columns_of(ids[:, :CHIP])
    for t in range(0, 2 * CHIP, HD):
        bias[:, t : t + HD] = jnp.where(clip_of == ids[:, t : t + HD], 0.0, NEGATIVE)
    for h in range(count):
        here = slice((head + h) * HD, (head + h + 1) * HD)
        keys[h, :CHIP, :] = local[1, :, here]
        values[h, :CHIP, :] = local[2, :, here]
    if flexible:
        back_rows, asked, scales, extra = refs[7:11]
        sum_copy = pltpu.make_async_copy(arrived[0].at[FIRST_ROWS:, :], extra, sems.at[4])
        sum_copy.start()
        near_rows = pl.ds(sixteen(jnp.where(side == 0, 0, REST)), NEAR)
        rest_rows = pl.ds(sixteen(jnp.where(side == 0, NEAR, first)), REST)
        scales[CHIP:, :] = jnp.ones((REST, HD), jnp.float32)
        back_rows[...] = jnp.zeros_like(back_rows)
        sum_copy.wait()
        parts = extra[...].astype(jnp.float32)
        for i, waves in enumerate((asked, table)):
            for j in range(3):
                total = sum(parts[9 * i + 3 * p + j : 9 * i + 3 * p + j + 1, :] for p in range(3))
                scales[j * HD : (j + 1) * HD, :] = columns_of(lax.rsqrt(total / D + EPSILON))
            for j, ref in enumerate((cosine, sine)):
                waves[j, :NEAR, :] = ref[CHIP : CHIP + NEAR, :] * scales[near_rows, :]
                waves[j, NEAR:, :] = ref[CHIP + NEAR :, :] * scales[rest_rows, :]
    near_copies[0].wait()
    for copy in copies:
        copy.wait()

    swap = signed_swap()
    if flexible:
        base = jnp.int32(0)
    else:
        base = 2 * rest * kept + jnp.where(major == 1, (HALF - kept) * (2 * rest + theirs), 0)
        base += 2 * rest * head
    bases = []
    for h in range(count):
        at = slice(h * HD, (h + 1) * HD)
        gain = gk[:, at]
        key_at = base
        bases.append(base)
        if flexible:
            lend = jnp.logical_and(h >= kept, major == 1)
            took = jnp.logical_or(h < kept, major == 1)
            key_at = base + jnp.where(lend, theirs, 0)
            base += jnp.where(took, 2 * rest, 0) + jnp.where(lend, theirs, 0)
        else:
            base += 2 * rest
        far = jnp.concatenate([near[0, :, at], stream[pl.ds(sixteen(key_at), REST), :]], axis=0)
        keys[h, CHIP:, :] = turn(far, gain, flip(gain), swap, table[0], table[1])
        values[h, CHIP : CHIP + NEAR, :] = near[1, :, at]
        values[h, CHIP + NEAR :, :] = stream[pl.ds(sixteen(key_at + rest), REST), :]

    def far_answer(h, size):
        at = slice(h * HD, (h + 1) * HD)
        gain = gq[:, at]
        x = stream[pl.ds(sixteen(bases[h]), size), :]
        far_q = turn(x, gain, flip(gain), swap, asked[0, :size, :], asked[1, :size, :])
        place = jnp.where(h >= kept, (h - kept) * theirs, BACK_ROWS + HD)
        back_rows[pl.ds(sixteen(place), size), :] = attention(
            far_q, keys[h, :SHORT, :], far_bias, values[h, :SHORT, :]
        )

    def answers(seen, lent):
        for h in range(count):
            at = slice(h * HD, (h + 1) * HD)
            here = slice((head + h) * HD, (head + h + 1) * HD)
            for t in range(0, CHIP, TILE):
                rows = slice(t, t + TILE)
                result[rows, at] = attention(
                    local[0, rows, here], keys[h, :seen, :], bias[rows, :seen], values[h, :seen, :]
                )
            if lent == HD or (lent and h > 0):
                far_answer(h, lent)

    short = theirs <= SHORT - CHIP
    if flexible:
        far_bias = jnp.where(ids[:, :SHORT] == edge, 0.0, NEGATIVE)
        lending = jnp.logical_and(kept < HALF, major == 1)

        wide = theirs > HD
        pl.when(jnp.logical_and(lending, wide))(lambda: answers(SHORT, 2 * HD))
        pl.when(jnp.logical_and(lending, jnp.logical_not(wide)))(lambda: answers(SHORT, HD))
        pl.when(jnp.logical_and(short, jnp.logical_not(lending)))(lambda: answers(SHORT, 0))
    else:
        pl.when(short)(lambda: answers(SHORT, 0))
    pl.when(jnp.logical_not(short))(lambda: answers(2 * CHIP, 0))
    own_out[...] = result[pl.ds(sixteen(core * ROWS), ROWS), :]
    mate_out[...] = result[pl.ds(sixteen((1 - core) * ROWS), ROWS), :]
    if flexible:
        back[...] = back_rows[:BACK_ROWS, :]


def join_kernel(
    info, flex_here, fixed_here, flex_there, fixed_there, back_here, back_there, ids, out, rows, lines
):
    side, core, _, edge, (first, mine, _, kept, major) = known(info)
    half = 2 * WIDE
    inside = columns_of(ids[...].astype(jnp.float32)) == edge
    for here, flex, fixed, back in (
        (True, flex_here, fixed_here, back_here),
        (False, flex_there, fixed_there, back_there),
    ):
        column = pl.multiple_of((core if here else 1 - core) * half, 128)
        out[:, pl.ds(column, WIDE)] = fixed[...]
        out[:, pl.ds(pl.multiple_of(column + WIDE, 128), WIDE)] = flex[...]

        @pl.when(jnp.logical_and(major == 0, kept < HALF))
        def _():
            rows[:BACK_ROWS, :] = back[...]
            rows[BACK_ROWS:, :] = jnp.zeros((REST, HD), rows.dtype)
            for h in range(HALF):

                @pl.when(h >= kept)
                def _():
                    base = (h - kept) * mine
                    near_at = jnp.where(side == 0, REST, 0)
                    rest_at = jnp.where(side == 0, first, NEAR)
                    lines[pl.ds(sixteen(rest_at), REST), :] = rows[
                        pl.ds(sixteen(base + NEAR), REST), :
                    ]
                    lines[pl.ds(sixteen(near_at), NEAR), :] = rows[pl.ds(sixteen(base), NEAR), :]
                    at = slice(h * HD, (h + 1) * HD)
                    place = pl.ds(pl.multiple_of(column + WIDE + h * HD, 128), HD)
                    out[:, place] = jnp.where(
                        inside, lines[pl.ds(sixteen(core * ROWS), ROWS), :], flex[:, at]
                    )


def frequencies():
    sixth_part = HD // 6
    first_dims = HD - 4 * sixth_part
    first_freqs = 1.0 / ROTARY_BASE ** (
        jnp.arange(0, first_dims, 2, dtype=jnp.float32) / first_dims
    )
    other_freqs = 1.0 / ROTARY_BASE ** (
        jnp.arange(0, 2 * sixth_part, 2, dtype=jnp.float32) / (2 * sixth_part)
    )
    return jnp.repeat(jnp.concatenate([first_freqs, other_freqs, other_freqs]), 2)[None, :]


def whole(a):
    return pl.BlockSpec(a.shape, lambda i: (0,) * len(a.shape))


def held():
    return pl.BlockSpec(memory_space=pltpu.VMEM)


def call(kernel, out_shape, in_specs, out_specs, scratch, *operands, limit=VMEM):
    return pl.pallas_call(
        kernel,
        grid=(1,),
        out_shape=out_shape,
        in_specs=in_specs,
        out_specs=out_specs,
        scratch_shapes=scratch,
        compiler_params=pltpu.CompilerParams(vmem_limit_bytes=limit),
        cost_estimate=pl.CostEstimate(flops=0, bytes_accessed=0, transcendentals=0),
    )(*operands)


def attend(flexible, head, count, info, streams, waves, local, near_straight, near_slanted, gains, ids):
    bf16, f32 = jnp.bfloat16, jnp.float32
    there = pl.BlockSpec(memory_space=pl.ANY)
    shapes = [jax.ShapeDtypeStruct((ROWS, count * HD), bf16)] * 2
    stream_rows = sum((FIRST_ROWS, SECOND_ROWS)[: len(streams)]) + REST
    scratch = [
        pltpu.VMEM((2, NEAR, count * HD), bf16),
        pltpu.VMEM((stream_rows, HD), bf16),
        pltpu.VMEM((CHIP, 2 * CHIP), f32),
        pltpu.VMEM((count, 2 * CHIP, HD), bf16),
        pltpu.VMEM((count, 2 * CHIP, HD), bf16),
        pltpu.VMEM((CHIP, count * HD), bf16),
        pltpu.SemaphoreType.DMA((5,)),
    ]
    if flexible:
        far_waves = jax.ShapeDtypeStruct((2, CHIP, HD), f32)
        shapes = shapes + [jax.ShapeDtypeStruct((BACK_ROWS, HD), bf16), far_waves]
        scratch = scratch + [
            pltpu.VMEM((BACK_ROWS + 3 * HD, HD), bf16),
            pltpu.VMEM((2, CHIP, HD), f32),
            pltpu.VMEM((CHIP + REST, HD), f32),
            pltpu.VMEM((SUM_ROWS, HD), bf16),
        ]
    operands = (local, near_straight, near_slanted, *gains, ids, *waves, *streams)
    in_specs = [held(), held(), there, there] + [held()] * (3 + len(waves)) + [there] * len(streams)
    return call(
        functools.partial(attend_kernel, flexible, head, count), shapes,
        in_specs, [held()] * len(shapes), scratch, info, *operands,
    )


def on_device(queries, keys, values, gain_q, gain_k, clip_ids, clip_grid):
    width = queries.shape[1]
    half = width // 2
    bf16, f32 = jnp.bfloat16, jnp.float32

    clip_row = clip_ids[None, :]

    near_shape = jax.ShapeDtypeStruct((2, NEAR, half), bf16)
    deal_shapes = [
        jax.ShapeDtypeStruct((3, ROWS, half), bf16),
        near_shape,
        near_shape,
        jax.ShapeDtypeStruct((3, ROWS), f32),
    ]
    dealt, near_own, near_other, sums = call(
        deal_kernel, deal_shapes, [whole(queries)] * 3 + [whole(clip_row)],
        [whole(s) for s in deal_shapes], [], queries, keys, values, clip_row, limit=ALL_VMEM,
    )
    near_straight = lax.ppermute(near_own, "ctx", STRAIGHT)
    near_slanted = lax.ppermute(near_other, "ctx", SLANTED)
    mate = lax.ppermute(dealt, "ctx", BESIDE)
    mate_sums = lax.ppermute(sums, "ctx", BESIDE)
    row_sums = lax.ppermute(sums, "row", OTHER_ROW)
    mate_row_sums = lax.ppermute(sums, ("ctx", "row"), OPPOSITE)
    stream_shapes = [
        jax.ShapeDtypeStruct((FIRST_ROWS + SUM_ROWS, HD), bf16),
        jax.ShapeDtypeStruct((SECOND_ROWS, HD), bf16),
        jax.ShapeDtypeStruct((2, CHIP), f32),
    ]
    first_send, second_send, totals, info = call(
        pack_kernel, stream_shapes + [jax.ShapeDtypeStruct((1, HD), f32)],
        [held()] * 8, [whole(shape) for shape in stream_shapes[:2]] + [held()] * 2,
        [
            pltpu.VMEM((3, CHIP + NEAR, half), bf16),
            pltpu.VMEM((STREAM_ROWS + NEAR, HD), bf16),
        ],
        queries, keys, values, mate, sums, mate_sums, row_sums, mate_row_sums,
    )

    first_stream = lax.ppermute(first_send, "ctx", ACROSS)
    second_stream = lax.ppermute(second_send, "ctx", ACROSS)
    near_straight, near_slanted, sums, _ = lax.optimization_barrier(
        (near_straight, near_slanted, sums, first_send)
    )
    wave_shape = jax.ShapeDtypeStruct((2 * CHIP, HD), f32)
    cosine, sine, mask_ids = call(
        waves_kernel, [wave_shape, wave_shape, jax.ShapeDtypeStruct((1, 2 * CHIP), f32)],
        [pl.BlockSpec(memory_space=pltpu.SMEM)] + [held()] * 4, [held()] * 3,
        [pltpu.VMEM((1, CHIP), f32)], clip_grid, info, sums, mate_sums, frequencies(),
    )
    gains = (gain_q[None, :], gain_k[None, :])
    local_shape = jax.ShapeDtypeStruct((3, CHIP, half), bf16)
    local = call(
        turn_kernel, local_shape, [held()] * 9, held(), [pltpu.VMEM((4, CHIP, HD), f32)],
        queries, keys, values, mate, cosine, sine, totals, *gains,
    )
    common = (local, near_straight, near_slanted, gains, mask_ids)
    flex_here, flex_send, back_send, far_waves = attend(
        True, HALF, HALF, info, (first_stream,), (cosine, sine), *common
    )
    back_here = lax.ppermute(back_send, "ctx", ACROSS)
    fixed_here, fixed_send = attend(
        False, 0, HALF, info, (first_stream, second_stream), (far_waves,), *common
    )
    flex_send, fixed_send = lax.optimization_barrier((flex_send, fixed_send))
    flex_there = lax.ppermute(flex_send, "ctx", BESIDE)
    fixed_there = lax.ppermute(fixed_send, "ctx", BESIDE)
    back_here, _ = lax.optimization_barrier((back_here, fixed_send))
    back_there = lax.ppermute(back_here, "ctx", BESIDE)
    out_shape = jax.ShapeDtypeStruct((ROWS, width), bf16)
    operands = (
        flex_here, fixed_here, flex_there, fixed_there, back_here, back_there, clip_row
    )
    return call(
        join_kernel, out_shape, [held()] * 8, whole(out_shape),
        [pltpu.VMEM((BACK_ROWS + REST, HD), bf16), pltpu.VMEM((2 * REST, HD), bf16)],
        info, *operands,
    )


def lookup(lookup_table, positions):
    labels = jnp.arange(lookup_table.shape[0], dtype=jnp.int32)
    return jnp.sum(
        jnp.where(positions[:, None] == labels[None, :], lookup_table[None, :], 0), axis=1
    )


def spin(matrix, offsets, clip_of, clip_grid, head_size):
    row_count = matrix.shape[0]
    sixth_part = head_size // 6
    first_dims = head_size - 4 * sixth_part
    first_freqs = 1.0 / ROTARY_BASE ** (
        jnp.arange(0, first_dims, 2, dtype=jnp.float32) / first_dims
    )
    other_freqs = 1.0 / ROTARY_BASE ** (
        jnp.arange(0, 2 * sixth_part, 2, dtype=jnp.float32) / (2 * sixth_part)
    )
    heights = lookup(clip_grid[:, 0], clip_of)
    widths = lookup(clip_grid[:, 1], clip_of)
    frame_pos = offsets // (heights * widths)
    line_pos = offsets // widths % heights
    column_pos = offsets % widths
    angles = jnp.concatenate(
        [
            frame_pos.astype(jnp.float32)[:, None] * first_freqs[None, :],
            line_pos.astype(jnp.float32)[:, None] * other_freqs[None, :],
            column_pos.astype(jnp.float32)[:, None] * other_freqs[None, :],
        ],
        axis=1,
    )
    cosine = jnp.repeat(jnp.cos(angles), 2, axis=1)
    sine_table = jnp.repeat(jnp.sin(angles), 2, axis=1)
    feature = jnp.arange(head_size, dtype=jnp.int32)
    is_even = (feature % 2 == 0)[None, None, :]
    head_view = matrix.reshape(row_count, -1, head_size)
    partner = jnp.where(is_even, -jnp.roll(head_view, -1, axis=2), jnp.roll(head_view, 1, axis=2))
    turned = head_view * cosine[:, None, :] + partner * sine_table[:, None, :]
    return turned.reshape(row_count, -1)


def on_any(queries, keys, values, gain_q, gain_k, clip_ids, clip_grid):
    rows_here, width_here = queries.shape
    heads_here = width_here // HD
    score_scale = 1.0 / math.sqrt(HD)
    query_wide = queries.astype(jnp.float32)
    key_wide = keys.astype(jnp.float32)
    squares = lax.psum(
        (jnp.sum(query_wide * query_wide, axis=1), jnp.sum(key_wide * key_wide, axis=1)), "row"
    )
    query_scale = lax.rsqrt(squares[0] / D + EPSILON)
    key_scale = lax.rsqrt(squares[1] / D + EPSILON)
    labels = jnp.arange(CLIPS, dtype=jnp.int32)
    local_counts = jnp.sum((clip_ids[:, None] == labels[None, :]).astype(jnp.int32), axis=0)
    totals = lax.psum(local_counts, "ctx")
    starts = jnp.cumsum(totals) - totals
    first_row = lax.axis_index("ctx") * rows_here
    offsets = first_row + jnp.arange(rows_here, dtype=jnp.int32) - lookup(starts, clip_ids)
    query_rot = spin(
        query_wide * query_scale[:, None] * gain_q[None, :], offsets, clip_ids, clip_grid, HD
    ).astype(jnp.bfloat16)
    query_heads = query_rot.reshape(rows_here, heads_here, HD)
    key_send = spin(
        key_wide * key_scale[:, None] * gain_k[None, :], offsets, clip_ids, clip_grid, HD
    ).astype(jnp.bfloat16)
    initial = (
        jnp.full((heads_here, rows_here), NEGATIVE, jnp.float32),
        jnp.zeros((heads_here, rows_here), jnp.float32),
        jnp.zeros((rows_here, heads_here, HD), jnp.float32),
    )
    running = initial
    piece_start = jnp.int32(0)
    key_piece = lax.all_gather(key_send, "ctx", axis=0, tiled=True)
    value_piece = lax.all_gather(values, "ctx", axis=0, tiled=True)
    row_count = key_piece.shape[0]
    block_rows = min(row_count, block_limit)
    for block_first in range(0, row_count, block_rows):
        block_size = min(block_rows, row_count - block_first)
        fold_key_rows = key_piece[block_first : block_first + block_size]
        fold_value_rows = value_piece[block_first : block_first + block_size]
        key_index = piece_start + block_first + jnp.arange(fold_key_rows.shape[0], dtype=jnp.int32)
        key_key_clips = (
            jnp.sum((starts[None, :] <= key_index[:, None]).astype(jnp.int32), axis=1) - 1
        )
        peak_old, total_old, summed_old = running
        key_view = fold_key_rows.reshape(fold_key_rows.shape[0], heads_here, HD)
        value_view = fold_value_rows.reshape(fold_value_rows.shape[0], heads_here, HD)
        scores = (
            jnp.einsum("qhd,khd->hqk", query_heads, key_view, preferred_element_type=jnp.float32)
            * score_scale
        )
        same = clip_ids[:, None] == key_key_clips[None, :]
        masked = jnp.where(same[None, :, :], scores, NEGATIVE)
        peak_new = jnp.maximum(peak_old, jnp.max(masked, axis=2))
        weights = jnp.where(same[None, :, :], jnp.exp(masked - peak_new[:, :, None]), 0.0)
        factor = jnp.exp(peak_old - peak_new)
        total_new = total_old * factor + jnp.sum(weights, axis=2)
        summed = summed_old * jnp.transpose(factor)[:, :, None] + jnp.einsum(
            "hqk,khd->qhd",
            weights.astype(jnp.bfloat16),
            value_view,
            preferred_element_type=jnp.float32,
        )
        running = (peak_new, total_new, summed)
    attended = running[2] / jnp.transpose(running[1])[:, :, None]
    return attended.reshape(rows_here, width_here).astype(jnp.bfloat16)


def solution(mesh):
    in_specs = (
        P(("batch", "ctx"), "row"),
        P(("batch", "ctx"), "row"),
        P(("batch", "ctx"), "row"),
        P("row"),
        P("row"),
        P(("batch", "ctx")),
        P("batch", None),
    )
    out_specs = P(("batch", "ctx"), "row")
    pair_of_chips = mesh.shape["ctx"] == 4 and mesh.shape["row"] == 2
    return jax.shard_map(
        on_device if pair_of_chips else on_any,
        mesh=mesh, in_specs=in_specs, out_specs=out_specs, check_vma=False,
    )
```

```python
import functools
import math

import jax
import jax.numpy as jnp
from jax import lax
from jax.experimental import pallas as pl
from jax.experimental.pallas import tpu as pltpu
from jax.sharding import PartitionSpec as P

HD = 128
D = 5120
CLIPS = 4
EPSILON = 1e-06
NEGATIVE = -1e30
ROTARY_BASE = 10000.0
block_limit = 1024

ROWS = 192
CHIP = 2 * ROWS
MOST = 480
NEAR = 96
REST = CHIP - NEAR
HALF = 5
WIDE = HALF * HD
TILE = 192
SHORT = 640
FIRST_ROWS = 1600
SECOND_ROWS = 1600
SUM_ROWS = 32
STREAM_ROWS = FIRST_ROWS + SECOND_ROWS
BACK_ROWS = 640
ACROSS = ((0, 2), (1, 3), (2, 0), (3, 1))
BESIDE = ((0, 1), (1, 0), (2, 3), (3, 2))
STRAIGHT = ((1, 3), (2, 0))
SLANTED = ((1, 2), (2, 1))
OTHER_ROW = ((0, 1), (1, 0))
OPPOSITE = tuple((2 * a + r, 2 * b + 1 - r) for a, b in BESIDE for r in (0, 1))
SCORE_SCALE = math.log2(math.e) / math.sqrt(HD)
VMEM = 24 * 1024 * 1024
ALL_VMEM = 60 * 1024 * 1024


def plan(start, side):
    first = start // 16 * 16
    last = (start + MOST + 15) // 16 * 16
    below, above = CHIP - first, last - CHIP
    mine = jnp.where(side == 0, below, above)
    theirs = jnp.where(side == 0, above, below)
    most = jnp.maximum(mine, theirs)
    lent = sum((most > limit).astype(jnp.int32) for limit in (256, 272, 288, 320, 352))
    return first, mine, theirs, HALF - lent, (mine > theirs).astype(jnp.int32)


def position():
    me = lax.axis_index("ctx")
    return me // 2, lax.rem(me, 2)


def known(info):
    row = info[...]
    lane = lax.broadcasted_iota(jnp.int32, row.shape, 1)
    start = jnp.sum(jnp.where(lane == 0, row, 0.0)).astype(jnp.int32)
    side, core = position()
    return side, core, start, row[:, 1:2], plan(start, side)


def sixteen(offset):
    return pl.multiple_of(offset, 16)


def deal_kernel(q_ref, k_ref, v_ref, ids, out, near_own, near_other, sums):
    side, core = position()
    half = out.shape[2]
    at = pl.ds(pl.multiple_of((1 - core) * half, 128), half)
    own = pl.ds(pl.multiple_of(core * half, 128), half)
    rows = pl.ds(sixteen((1 - side) * NEAR), NEAR)
    for i, ref in enumerate((k_ref, v_ref)):
        near_own[i] = ref[rows, own]
        near_other[i] = ref[rows, at]
    for i, ref in enumerate((q_ref, k_ref, v_ref)):
        out[i] = ref[:, at]
    for i, ref in enumerate((q_ref, k_ref)):
        lanes = jnp.zeros((ROWS, HD), jnp.float32)
        for column in range(0, ref.shape[1], HD):
            x = ref[:, column : column + HD].astype(jnp.float32)
            lanes += x * x
        sums[i : i + 1, :] = jnp.sum(jnp.transpose(lanes), axis=0, keepdims=True)
    sums[2:3, :] = ids[...].astype(jnp.float32)


def side_by_side(core, here, there, out):
    for ref, at in ((here, 0), (there, 1)):

        @pl.when(core == at)
        def _():
            out[:, :ROWS] = ref

        @pl.when(core != at)
        def _():
            out[:, ROWS:] = ref


def pack_kernel(
    q_ref, k_ref, v_ref, mate, sums, mate_sums, row_sums, mate_row_sums,
    first_out, second_out, totals, info, chip, buffer,
):
    side, core = position()
    here, there = sums[2:3, :], mate_sums[2:3, :]
    edge = jnp.where(
        side == 0,
        jnp.maximum(jnp.max(here), jnp.max(there)),
        jnp.minimum(jnp.min(here), jnp.min(there)),
    )
    count = (
        jnp.sum(jnp.where(here == edge, 1.0, 0.0)) + jnp.sum(jnp.where(there == edge, 1.0, 0.0))
    ).astype(jnp.int32)
    start = jnp.where(side == 0, CHIP - count, count - NEAR)
    first, mine, _, kept, major = plan(start, side)
    lane = lax.broadcasted_iota(jnp.int32, info.shape, 1)
    info[...] = jnp.where(lane == 0, start.astype(jnp.float32), edge)
    half = chip.shape[2]
    columns = pl.ds(pl.multiple_of(core * half, 128), half)
    for i, ref in enumerate((q_ref, k_ref, v_ref)):
        chip[i, pl.ds(sixteen(core * ROWS), ROWS), :] = ref[:, columns]
        chip[i, pl.ds(sixteen((1 - core) * ROWS), ROWS), :] = mate[i]
        chip[i, CHIP:, :] = jnp.zeros((NEAR, half), ref.dtype)
    buffer[...] = jnp.zeros_like(buffer)
    near_at = jnp.where(side == 0, REST, 0)
    rest_at = jnp.where(side == 0, first, NEAR)
    rest = mine - NEAR

    def put(offset, which, head, row, length):
        at = slice(head * HD, (head + 1) * HD)

        def step(i, carry):
            buffer[pl.ds(sixteen(offset + i * NEAR), NEAR), :] = chip[
                which, pl.ds(sixteen(row + i * NEAR), NEAR), at
            ]
            return carry

        lax.fori_loop(0, (length + NEAR - 1) // NEAR, step, 0)

    offset = jnp.int32(0)
    for i in range(HALF):
        head = HALF + i
        lend = jnp.logical_and(i >= kept, major == 0)
        send = jnp.logical_or(i < kept, major == 0)
        put(offset, 0, head, near_at, jnp.where(lend, NEAR, 0))
        offset += jnp.where(lend, NEAR, 0)
        put(offset, 0, head, rest_at, jnp.where(lend, rest, 0))
        offset += jnp.where(lend, rest, 0)
        length = jnp.where(send, rest, 0)
        for which in (1, 2):
            put(offset, which, head, rest_at, length)
            offset += length
    for head in range(HALF):
        for which in (1, 2):
            put(offset, which, head, rest_at, rest)
            offset += rest
    side_by_side(
        core, sums[:2, :] + row_sums[:2, :], mate_sums[:2, :] + mate_row_sums[:2, :], totals
    )
    parts = []
    for i in range(2):
        left = totals[i : i + 1, :]
        for _ in range(3):
            part = left.astype(jnp.bfloat16)
            left = left - part.astype(jnp.float32)
            parts += [part[:, t : t + HD] for t in range(0, CHIP, HD)]
    parts += [jnp.zeros_like(parts[0])] * (SUM_ROWS - len(parts))
    first_out[:FIRST_ROWS, :] = buffer[:FIRST_ROWS, :]
    first_out[FIRST_ROWS:, :] = jnp.concatenate(parts, axis=0)
    second_out[...] = buffer[FIRST_ROWS:STREAM_ROWS, :]


def turn(x, gain, gain_s, swap, cosine, sine):
    other = jnp.dot(x, swap, preferred_element_type=jnp.float32)
    return ((x.astype(jnp.float32) * gain) * cosine + (other * gain_s) * sine).astype(jnp.bfloat16)


def flip(gain):
    size = gain.shape[1]
    even = lax.broadcasted_iota(jnp.int32, gain.shape, 1) % 2 == 0
    return jnp.where(even, pltpu.roll(gain, size - 1, 1), pltpu.roll(gain, 1, 1))


def signed_swap():
    at_row = lax.broadcasted_iota(jnp.int32, (HD, HD), 0)
    at_column = lax.broadcasted_iota(jnp.int32, (HD, HD), 1)
    sign = jnp.where(at_column % 2 == 0, -1.0, 1.0)
    return jnp.where(at_row == (at_column ^ 1), sign, 0.0).astype(jnp.bfloat16)


def attention(q, keys, bias, values):
    scores = lax.dot_general(
        q, keys, (((1,), (1,)), ((), ())), preferred_element_type=jnp.float32
    ) + bias
    peak = jnp.max(scores, axis=1, keepdims=True)
    weights = jnp.exp2((scores - peak) * SCORE_SCALE).astype(jnp.bfloat16)
    columns = jnp.concatenate([values, jnp.ones_like(values)], axis=1)
    sums = jnp.dot(weights, columns, preferred_element_type=jnp.float32)
    return (sums[:, :HD] / sums[:, HD:]).astype(jnp.bfloat16)


def columns_of(row):
    return jnp.transpose(jnp.broadcast_to(row, (HD, row.shape[1])))


def waves_kernel(grid, info, sums, mate_sums, freqs, cosine, sine, ids, chip_ids):
    side, core, start, edge, (first, *_) = known(info)
    side_by_side(core, sums[2:3, :], mate_sums[2:3, :], chip_ids)
    here = chip_ids[...]
    slot = lax.broadcasted_iota(jnp.int32, (1, CHIP), 1)
    rest_start = jnp.where(side == 0, CHIP, first - NEAR)
    rest_end = jnp.where(side == 0, start + MOST, REST)
    token = slot + jnp.where(slot < NEAR, jnp.where(side == 0, CHIP, REST), rest_start)
    valid = jnp.logical_or(
        slot < NEAR, jnp.logical_and(token >= start, token < rest_end)
    )
    ids[:, :CHIP] = here
    ids[:, CHIP:] = jnp.where(valid, edge, -1.0)
    place = slot.astype(jnp.float32)
    offset, height, line_size = place, jnp.zeros_like(place), jnp.zeros_like(place)
    for label in range(CLIPS):
        same = here == float(label)
        below = jnp.sum(jnp.where(here < float(label), 1.0, 0.0), axis=1, keepdims=True)
        offset = offset - jnp.where(same, below, 0.0)
        height = height + jnp.where(same, grid[label, 0].astype(jnp.float32), 0.0)
        line_size = line_size + jnp.where(same, grid[label, 1].astype(jnp.float32), 0.0)
    carried = jnp.logical_and(here == edge, side == 1)
    offset = jnp.where(carried, place + (CHIP - start).astype(jnp.float32), offset)
    far_offset = jnp.maximum(token - start, 0).astype(jnp.float32)
    ones = jnp.ones_like(place)
    offset = jnp.concatenate([offset, far_offset], axis=1)
    far_sizes = []
    for axis in range(2):
        sizes = [jnp.where(edge == float(c), grid[c, axis].astype(jnp.float32), 0.0) for c in range(CLIPS)]
        far_sizes.append(ones * sum(sizes))
    height = jnp.concatenate([height, far_sizes[0]], axis=1)
    line_size = jnp.concatenate([line_size, far_sizes[1]], axis=1)
    frame = jnp.floor((offset + 0.5) / (height * line_size))
    offset = offset - frame * (height * line_size)
    line = jnp.floor((offset + 0.5) / line_size)
    column = offset - line * line_size
    sixth_part = HD // 6
    first_dims = HD - 4 * sixth_part
    feature = lax.broadcasted_iota(jnp.int32, (1, HD), 1)
    angles = freqs[...] * jnp.where(
        feature < first_dims,
        columns_of(frame),
        jnp.where(feature < first_dims + 2 * sixth_part, columns_of(line), columns_of(column)),
    )
    cosine[...] = jnp.cos(angles)
    sine[...] = jnp.sin(angles)


def turn_kernel(q_ref, k_ref, v_ref, mate, cosine, sine, totals, gq, gk, out, table):
    _, core = position()
    half = out.shape[2]
    columns = pl.ds(pl.multiple_of(core * half, 128), half)
    swap = signed_swap()
    for i in range(2):
        scale = columns_of(lax.rsqrt(totals[i : i + 1, :] / D + EPSILON))
        for j, ref in enumerate((cosine, sine)):
            table[2 * i + j] = ref[:CHIP, :] * scale
    for here, rows in ((True, core), (False, 1 - core)):
        rows = pl.ds(sixteen(rows * ROWS), ROWS)
        out[2, rows, :] = v_ref[:, columns] if here else mate[2]
        for i, (ref, gains) in enumerate(((q_ref, gq), (k_ref, gk))):
            cos_here, sin_here = table[2 * i, rows, :], table[2 * i + 1, rows, :]
            for h in range(half // HD):
                at = slice(h * HD, (h + 1) * HD)
                place = pl.ds(pl.multiple_of(core * half + h * HD, 128), HD)
                gain = gains[:, place]
                x = ref[:, place] if here else mate[i, :, at]
                out[i, rows, at] = turn(x, gain, flip(gain), swap, cos_here, sin_here)


def local_kernel(local, ids, partial, peaks, bias):
    clip_of = columns_of(ids[:, :CHIP])
    for t in range(0, CHIP, HD):
        bias[:, t : t + HD] = jnp.where(clip_of == ids[:, t : t + HD], 0.0, NEGATIVE)
    for h in range(HALF):
        at = slice(h * HD, (h + 1) * HD)
        values = local[2, :, at]
        columns = jnp.concatenate([values, jnp.ones_like(values)], axis=1)
        for t in range(0, CHIP, TILE):
            rows = slice(t, t + TILE)
            scores = lax.dot_general(
                local[0, rows, at], local[1, :, at], (((1,), (1,)), ((), ())),
                preferred_element_type=jnp.float32,
            ) + bias[rows, :]
            peak = jnp.max(scores, axis=1, keepdims=True)
            weights = jnp.exp2((scores - peak) * SCORE_SCALE).astype(jnp.bfloat16)
            partial[rows, 2 * h * HD : 2 * (h + 1) * HD] = jnp.dot(
                weights, columns, preferred_element_type=jnp.float32
            )
            peaks[rows, at] = jnp.broadcast_to(peak, (TILE, HD))


def attend_kernel(flexible, head, count, info, *refs):
    local, near_straight, near_slanted, gq, gk, ids = refs[:6]
    streams = 1 if flexible else 2
    refs = refs[6:]
    if flexible:
        (cosine, sine), refs = refs[:2], refs[2:]
    else:
        (table, partial, peaks), refs = refs[:3], refs[3:]
    arrived, refs = refs[:streams], refs[streams:]
    own_out, mate_out, refs = refs[0], refs[1], refs[2:]
    if flexible:
        back, table, refs = refs[0], refs[1], refs[2:]
    near, stream, bias, keys, values, result, sems = refs[:7]
    side, core, _, edge, (first, _, theirs, kept, major) = known(info)
    inner = side != core
    rest = theirs - NEAR
    near_columns = slice(head * HD, (head + count) * HD)
    sizes = (FIRST_ROWS, SECOND_ROWS)[:streams]
    copies, filled = [], 0
    for i, (ref, size) in enumerate(zip(arrived, sizes)):
        copies.append(
            pltpu.make_async_copy(
                ref.at[:size, :], stream.at[filled : filled + size, :], sems.at[1 + i]
            )
        )
        filled += size
    near_copies = [
        pltpu.make_async_copy(ref.at[:, :, near_columns], near, sems.at[0])
        for ref in (near_slanted, near_straight)
    ]
    for copy in copies:
        copy.start()
    pl.when(inner)(near_copies[0].start)
    pl.when(jnp.logical_not(inner))(near_copies[1].start)
    stream[filled:, :] = jnp.zeros((REST, HD), stream.dtype)

    columns = pl.ds(pl.multiple_of((2 * HALF * core + head) * HD, 128), count * HD)
    gq, gk = gq[:, columns], gk[:, columns]
    clip_of = columns_of(ids[:, :CHIP])
    for t in range(0 if flexible else CHIP, 2 * CHIP, HD):
        bias[:, t : t + HD] = jnp.where(clip_of == ids[:, t : t + HD], 0.0, NEGATIVE)
    for h in range(count if flexible else 0):
        here = slice((head + h) * HD, (head + h + 1) * HD)
        keys[h, :CHIP, :] = local[1, :, here]
        values[h, :CHIP, :] = local[2, :, here]
    if flexible:
        back_rows, asked, scales, extra = refs[7:11]
        sum_copy = pltpu.make_async_copy(arrived[0].at[FIRST_ROWS:, :], extra, sems.at[4])
        sum_copy.start()
        near_rows = pl.ds(sixteen(jnp.where(side == 0, 0, REST)), NEAR)
        rest_rows = pl.ds(sixteen(jnp.where(side == 0, NEAR, first)), REST)
        scales[CHIP:, :] = jnp.ones((REST, HD), jnp.float32)
        back_rows[...] = jnp.zeros_like(back_rows)
        sum_copy.wait()
        parts = extra[...].astype(jnp.float32)
        for i, waves in enumerate((asked, table)):
            for j in range(3):
                total = sum(parts[9 * i + 3 * p + j : 9 * i + 3 * p + j + 1, :] for p in range(3))
                scales[j * HD : (j + 1) * HD, :] = columns_of(lax.rsqrt(total / D + EPSILON))
            for j, ref in enumerate((cosine, sine)):
                waves[j, :NEAR, :] = ref[CHIP : CHIP + NEAR, :] * scales[near_rows, :]
                waves[j, NEAR:, :] = ref[CHIP + NEAR :, :] * scales[rest_rows, :]
    near_copies[0].wait()
    for copy in copies:
        copy.wait()

    swap = signed_swap()
    if flexible:
        base = jnp.int32(0)
    else:
        base = 2 * rest * kept + jnp.where(major == 1, (HALF - kept) * (2 * rest + theirs), 0)
        base += 2 * rest * head
    bases = []
    for h in range(count):
        at = slice(h * HD, (h + 1) * HD)
        gain = gk[:, at]
        key_at = base
        bases.append(base)
        if flexible:
            lend = jnp.logical_and(h >= kept, major == 1)
            took = jnp.logical_or(h < kept, major == 1)
            key_at = base + jnp.where(lend, theirs, 0)
            base += jnp.where(took, 2 * rest, 0) + jnp.where(lend, theirs, 0)
        else:
            base += 2 * rest
        far = jnp.concatenate([near[0, :, at], stream[pl.ds(sixteen(key_at), REST), :]], axis=0)
        keys[h, CHIP:, :] = turn(far, gain, flip(gain), swap, table[0], table[1])
        values[h, CHIP : CHIP + NEAR, :] = near[1, :, at]
        values[h, CHIP + NEAR :, :] = stream[pl.ds(sixteen(key_at + rest), REST), :]

    def far_answer(h, size):
        at = slice(h * HD, (h + 1) * HD)
        gain = gq[:, at]
        x = stream[pl.ds(sixteen(bases[h]), size), :]
        far_q = turn(x, gain, flip(gain), swap, asked[0, :size, :], asked[1, :size, :])
        place = jnp.where(h >= kept, (h - kept) * theirs, BACK_ROWS + HD)
        back_rows[pl.ds(sixteen(place), size), :] = attention(
            far_q, keys[h, :SHORT, :], far_bias, values[h, :SHORT, :]
        )

    def answers(seen, lent):
        for h in range(count):
            at = slice(h * HD, (h + 1) * HD)
            here = slice((head + h) * HD, (head + h + 1) * HD)
            for t in range(0, CHIP, TILE):
                rows = slice(t, t + TILE)
                result[rows, at] = attention(
                    local[0, rows, here], keys[h, :seen, :], bias[rows, :seen], values[h, :seen, :]
                )
            if lent == HD or (lent and h > 0):
                far_answer(h, lent)

    def merged(seen):
        for h in range(count):
            at = slice(h * HD, (h + 1) * HD)
            here = slice((head + h) * HD, (head + h + 1) * HD)
            far = values[h, CHIP:seen, :]
            columns = jnp.concatenate([far, jnp.ones_like(far)], axis=1)
            for t in range(0, CHIP, TILE):
                rows = slice(t, t + TILE)
                scores = lax.dot_general(
                    local[0, rows, here], keys[h, CHIP:seen, :], (((1,), (1,)), ((), ())),
                    preferred_element_type=jnp.float32,
                ) + bias[rows, CHIP:seen]
                before = peaks[rows, h * HD : h * HD + 1]
                peak = jnp.maximum(before, jnp.max(scores, axis=1, keepdims=True))
                weights = jnp.exp2((scores - peak) * SCORE_SCALE).astype(jnp.bfloat16)
                sums = jnp.dot(weights, columns, preferred_element_type=jnp.float32)
                sums += jnp.exp2((before - peak) * SCORE_SCALE) * partial[
                    rows, 2 * h * HD : 2 * (h + 1) * HD
                ]
                result[rows, at] = (sums[:, :HD] / sums[:, HD:]).astype(jnp.bfloat16)

    short = theirs <= SHORT - CHIP
    if flexible:
        far_bias = jnp.where(ids[:, :SHORT] == edge, 0.0, NEGATIVE)
        lending = jnp.logical_and(kept < HALF, major == 1)

        wide = theirs > HD
        pl.when(jnp.logical_and(lending, wide))(lambda: answers(SHORT, 2 * HD))
        pl.when(jnp.logical_and(lending, jnp.logical_not(wide)))(lambda: answers(SHORT, HD))
        pl.when(jnp.logical_and(short, jnp.logical_not(lending)))(lambda: answers(SHORT, 0))
        pl.when(jnp.logical_not(short))(lambda: answers(2 * CHIP, 0))
    else:
        pl.when(short)(lambda: merged(SHORT))
        pl.when(jnp.logical_not(short))(lambda: merged(2 * CHIP))
    own_out[...] = result[pl.ds(sixteen(core * ROWS), ROWS), :]
    mate_out[...] = result[pl.ds(sixteen((1 - core) * ROWS), ROWS), :]
    if flexible:
        back[...] = back_rows[:BACK_ROWS, :]


def join_kernel(
    info, flex_here, fixed_here, flex_there, fixed_there, back_here, back_there, ids, out, rows, lines
):
    side, core, _, edge, (first, mine, _, kept, major) = known(info)
    half = 2 * WIDE
    inside = columns_of(ids[...].astype(jnp.float32)) == edge
    for here, flex, fixed, back in (
        (True, flex_here, fixed_here, back_here),
        (False, flex_there, fixed_there, back_there),
    ):
        column = pl.multiple_of((core if here else 1 - core) * half, 128)
        out[:, pl.ds(column, WIDE)] = fixed[...]
        out[:, pl.ds(pl.multiple_of(column + WIDE, 128), WIDE)] = flex[...]

        @pl.when(jnp.logical_and(major == 0, kept < HALF))
        def _():
            rows[:BACK_ROWS, :] = back[...]
            rows[BACK_ROWS:, :] = jnp.zeros((REST, HD), rows.dtype)
            for h in range(HALF):

                @pl.when(h >= kept)
                def _():
                    base = (h - kept) * mine
                    near_at = jnp.where(side == 0, REST, 0)
                    rest_at = jnp.where(side == 0, first, NEAR)
                    lines[pl.ds(sixteen(rest_at), REST), :] = rows[
                        pl.ds(sixteen(base + NEAR), REST), :
                    ]
                    lines[pl.ds(sixteen(near_at), NEAR), :] = rows[pl.ds(sixteen(base), NEAR), :]
                    at = slice(h * HD, (h + 1) * HD)
                    place = pl.ds(pl.multiple_of(column + WIDE + h * HD, 128), HD)
                    out[:, place] = jnp.where(
                        inside, lines[pl.ds(sixteen(core * ROWS), ROWS), :], flex[:, at]
                    )


def frequencies():
    sixth_part = HD // 6
    first_dims = HD - 4 * sixth_part
    first_freqs = 1.0 / ROTARY_BASE ** (
        jnp.arange(0, first_dims, 2, dtype=jnp.float32) / first_dims
    )
    other_freqs = 1.0 / ROTARY_BASE ** (
        jnp.arange(0, 2 * sixth_part, 2, dtype=jnp.float32) / (2 * sixth_part)
    )
    return jnp.repeat(jnp.concatenate([first_freqs, other_freqs, other_freqs]), 2)[None, :]


def whole(a):
    return pl.BlockSpec(a.shape, lambda i: (0,) * len(a.shape))


def held():
    return pl.BlockSpec(memory_space=pltpu.VMEM)


def call(kernel, out_shape, in_specs, out_specs, scratch, *operands, limit=VMEM):
    return pl.pallas_call(
        kernel,
        grid=(1,),
        out_shape=out_shape,
        in_specs=in_specs,
        out_specs=out_specs,
        scratch_shapes=scratch,
        compiler_params=pltpu.CompilerParams(vmem_limit_bytes=limit),
        cost_estimate=pl.CostEstimate(flops=0, bytes_accessed=0, transcendentals=0),
    )(*operands)


def attend(flexible, head, count, info, streams, waves, local, near_straight, near_slanted, gains, ids):
    bf16, f32 = jnp.bfloat16, jnp.float32
    there = pl.BlockSpec(memory_space=pl.ANY)
    shapes = [jax.ShapeDtypeStruct((ROWS, count * HD), bf16)] * 2
    stream_rows = sum((FIRST_ROWS, SECOND_ROWS)[: len(streams)]) + REST
    scratch = [
        pltpu.VMEM((2, NEAR, count * HD), bf16),
        pltpu.VMEM((stream_rows, HD), bf16),
        pltpu.VMEM((CHIP, 2 * CHIP), f32),
        pltpu.VMEM((count, 2 * CHIP, HD), bf16),
        pltpu.VMEM((count, 2 * CHIP, HD), bf16),
        pltpu.VMEM((CHIP, count * HD), bf16),
        pltpu.SemaphoreType.DMA((5,)),
    ]
    if flexible:
        far_waves = jax.ShapeDtypeStruct((2, CHIP, HD), f32)
        shapes = shapes + [jax.ShapeDtypeStruct((BACK_ROWS, HD), bf16), far_waves]
        scratch = scratch + [
            pltpu.VMEM((BACK_ROWS + 3 * HD, HD), bf16),
            pltpu.VMEM((2, CHIP, HD), f32),
            pltpu.VMEM((CHIP + REST, HD), f32),
            pltpu.VMEM((SUM_ROWS, HD), bf16),
        ]
    operands = (local, near_straight, near_slanted, *gains, ids, *waves, *streams)
    in_specs = [held(), held(), there, there] + [held()] * (3 + len(waves)) + [there] * len(streams)
    return call(
        functools.partial(attend_kernel, flexible, head, count), shapes,
        in_specs, [held()] * len(shapes), scratch, info, *operands,
    )


def on_device(queries, keys, values, gain_q, gain_k, clip_ids, clip_grid):
    width = queries.shape[1]
    half = width // 2
    bf16, f32 = jnp.bfloat16, jnp.float32

    clip_row = clip_ids[None, :]

    near_shape = jax.ShapeDtypeStruct((2, NEAR, half), bf16)
    deal_shapes = [
        jax.ShapeDtypeStruct((3, ROWS, half), bf16),
        near_shape,
        near_shape,
        jax.ShapeDtypeStruct((3, ROWS), f32),
    ]
    dealt, near_own, near_other, sums = call(
        deal_kernel, deal_shapes, [whole(queries)] * 3 + [whole(clip_row)],
        [whole(s) for s in deal_shapes], [], queries, keys, values, clip_row, limit=ALL_VMEM,
    )
    near_straight = lax.ppermute(near_own, "ctx", STRAIGHT)
    near_slanted = lax.ppermute(near_other, "ctx", SLANTED)
    mate = lax.ppermute(dealt, "ctx", BESIDE)
    mate_sums = lax.ppermute(sums, "ctx", BESIDE)
    row_sums = lax.ppermute(sums, "row", OTHER_ROW)
    mate_row_sums = lax.ppermute(sums, ("ctx", "row"), OPPOSITE)
    stream_shapes = [
        jax.ShapeDtypeStruct((FIRST_ROWS + SUM_ROWS, HD), bf16),
        jax.ShapeDtypeStruct((SECOND_ROWS, HD), bf16),
        jax.ShapeDtypeStruct((2, CHIP), f32),
    ]
    first_send, second_send, totals, info = call(
        pack_kernel, stream_shapes + [jax.ShapeDtypeStruct((1, HD), f32)],
        [held()] * 8, [whole(shape) for shape in stream_shapes[:2]] + [held()] * 2,
        [
            pltpu.VMEM((3, CHIP + NEAR, half), bf16),
            pltpu.VMEM((STREAM_ROWS + NEAR, HD), bf16),
        ],
        queries, keys, values, mate, sums, mate_sums, row_sums, mate_row_sums,
    )

    first_stream = lax.ppermute(first_send, "ctx", ACROSS)
    second_stream = lax.ppermute(second_send, "ctx", ACROSS)
    near_straight, near_slanted, sums, _ = lax.optimization_barrier(
        (near_straight, near_slanted, sums, first_send)
    )
    wave_shape = jax.ShapeDtypeStruct((2 * CHIP, HD), f32)
    cosine, sine, mask_ids = call(
        waves_kernel, [wave_shape, wave_shape, jax.ShapeDtypeStruct((1, 2 * CHIP), f32)],
        [pl.BlockSpec(memory_space=pltpu.SMEM)] + [held()] * 4, [held()] * 3,
        [pltpu.VMEM((1, CHIP), f32)], clip_grid, info, sums, mate_sums, frequencies(),
    )
    gains = (gain_q[None, :], gain_k[None, :])
    local_shape = jax.ShapeDtypeStruct((3, CHIP, half), bf16)
    local = call(
        turn_kernel, local_shape, [held()] * 9, held(), [pltpu.VMEM((4, CHIP, HD), f32)],
        queries, keys, values, mate, cosine, sine, totals, *gains,
    )
    common = (local, near_straight, near_slanted, gains, mask_ids)
    partial, peaks = call(
        local_kernel,
        [
            jax.ShapeDtypeStruct((CHIP, 2 * WIDE), f32),
            jax.ShapeDtypeStruct((CHIP, WIDE), f32),
        ],
        [held()] * 2, [held()] * 2, [pltpu.VMEM((CHIP, CHIP), f32)], local, mask_ids,
    )
    first_stream, partial = lax.optimization_barrier((first_stream, partial))
    flex_here, flex_send, back_send, far_waves = attend(
        True, HALF, HALF, info, (first_stream,), (cosine, sine), *common
    )
    back_here = lax.ppermute(back_send, "ctx", ACROSS)
    fixed_here, fixed_send = attend(
        False, 0, HALF, info, (first_stream, second_stream),
        (far_waves, partial, peaks), *common
    )
    flex_send, fixed_send = lax.optimization_barrier((flex_send, fixed_send))
    flex_there = lax.ppermute(flex_send, "ctx", BESIDE)
    fixed_there = lax.ppermute(fixed_send, "ctx", BESIDE)
    back_here, _ = lax.optimization_barrier((back_here, fixed_send))
    back_there = lax.ppermute(back_here, "ctx", BESIDE)
    out_shape = jax.ShapeDtypeStruct((ROWS, width), bf16)
    operands = (
        flex_here, fixed_here, flex_there, fixed_there, back_here, back_there, clip_row
    )
    return call(
        join_kernel, out_shape, [held()] * 8, whole(out_shape),
        [pltpu.VMEM((BACK_ROWS + REST, HD), bf16), pltpu.VMEM((2 * REST, HD), bf16)],
        info, *operands,
    )


def lookup(lookup_table, positions):
    labels = jnp.arange(lookup_table.shape[0], dtype=jnp.int32)
    return jnp.sum(
        jnp.where(positions[:, None] == labels[None, :], lookup_table[None, :], 0), axis=1
    )


def spin(matrix, offsets, clip_of, clip_grid, head_size):
    row_count = matrix.shape[0]
    sixth_part = head_size // 6
    first_dims = head_size - 4 * sixth_part
    first_freqs = 1.0 / ROTARY_BASE ** (
        jnp.arange(0, first_dims, 2, dtype=jnp.float32) / first_dims
    )
    other_freqs = 1.0 / ROTARY_BASE ** (
        jnp.arange(0, 2 * sixth_part, 2, dtype=jnp.float32) / (2 * sixth_part)
    )
    heights = lookup(clip_grid[:, 0], clip_of)
    widths = lookup(clip_grid[:, 1], clip_of)
    frame_pos = offsets // (heights * widths)
    line_pos = offsets // widths % heights
    column_pos = offsets % widths
    angles = jnp.concatenate(
        [
            frame_pos.astype(jnp.float32)[:, None] * first_freqs[None, :],
            line_pos.astype(jnp.float32)[:, None] * other_freqs[None, :],
            column_pos.astype(jnp.float32)[:, None] * other_freqs[None, :],
        ],
        axis=1,
    )
    cosine = jnp.repeat(jnp.cos(angles), 2, axis=1)
    sine_table = jnp.repeat(jnp.sin(angles), 2, axis=1)
    feature = jnp.arange(head_size, dtype=jnp.int32)
    is_even = (feature % 2 == 0)[None, None, :]
    head_view = matrix.reshape(row_count, -1, head_size)
    partner = jnp.where(is_even, -jnp.roll(head_view, -1, axis=2), jnp.roll(head_view, 1, axis=2))
    turned = head_view * cosine[:, None, :] + partner * sine_table[:, None, :]
    return turned.reshape(row_count, -1)


def on_any(queries, keys, values, gain_q, gain_k, clip_ids, clip_grid):
    rows_here, width_here = queries.shape
    heads_here = width_here // HD
    score_scale = 1.0 / math.sqrt(HD)
    query_wide = queries.astype(jnp.float32)
    key_wide = keys.astype(jnp.float32)
    squares = lax.psum(
        (jnp.sum(query_wide * query_wide, axis=1), jnp.sum(key_wide * key_wide, axis=1)), "row"
    )
    query_scale = lax.rsqrt(squares[0] / D + EPSILON)
    key_scale = lax.rsqrt(squares[1] / D + EPSILON)
    labels = jnp.arange(CLIPS, dtype=jnp.int32)
    local_counts = jnp.sum((clip_ids[:, None] == labels[None, :]).astype(jnp.int32), axis=0)
    totals = lax.psum(local_counts, "ctx")
    starts = jnp.cumsum(totals) - totals
    first_row = lax.axis_index("ctx") * rows_here
    offsets = first_row + jnp.arange(rows_here, dtype=jnp.int32) - lookup(starts, clip_ids)
    query_rot = spin(
        query_wide * query_scale[:, None] * gain_q[None, :], offsets, clip_ids, clip_grid, HD
    ).astype(jnp.bfloat16)
    query_heads = query_rot.reshape(rows_here, heads_here, HD)
    key_send = spin(
        key_wide * key_scale[:, None] * gain_k[None, :], offsets, clip_ids, clip_grid, HD
    ).astype(jnp.bfloat16)
    initial = (
        jnp.full((heads_here, rows_here), NEGATIVE, jnp.float32),
        jnp.zeros((heads_here, rows_here), jnp.float32),
        jnp.zeros((rows_here, heads_here, HD), jnp.float32),
    )
    running = initial
    piece_start = jnp.int32(0)
    key_piece = lax.all_gather(key_send, "ctx", axis=0, tiled=True)
    value_piece = lax.all_gather(values, "ctx", axis=0, tiled=True)
    row_count = key_piece.shape[0]
    block_rows = min(row_count, block_limit)
    for block_first in range(0, row_count, block_rows):
        block_size = min(block_rows, row_count - block_first)
        fold_key_rows = key_piece[block_first : block_first + block_size]
        fold_value_rows = value_piece[block_first : block_first + block_size]
        key_index = piece_start + block_first + jnp.arange(fold_key_rows.shape[0], dtype=jnp.int32)
        key_key_clips = (
            jnp.sum((starts[None, :] <= key_index[:, None]).astype(jnp.int32), axis=1) - 1
        )
        peak_old, total_old, summed_old = running
        key_view = fold_key_rows.reshape(fold_key_rows.shape[0], heads_here, HD)
        value_view = fold_value_rows.reshape(fold_value_rows.shape[0], heads_here, HD)
        scores = (
            jnp.einsum("qhd,khd->hqk", query_heads, key_view, preferred_element_type=jnp.float32)
            * score_scale
        )
        same = clip_ids[:, None] == key_key_clips[None, :]
        masked = jnp.where(same[None, :, :], scores, NEGATIVE)
        peak_new = jnp.maximum(peak_old, jnp.max(masked, axis=2))
        weights = jnp.where(same[None, :, :], jnp.exp(masked - peak_new[:, :, None]), 0.0)
        factor = jnp.exp(peak_old - peak_new)
        total_new = total_old * factor + jnp.sum(weights, axis=2)
        summed = summed_old * jnp.transpose(factor)[:, :, None] + jnp.einsum(
            "hqk,khd->qhd",
            weights.astype(jnp.bfloat16),
            value_view,
            preferred_element_type=jnp.float32,
        )
        running = (peak_new, total_new, summed)
    attended = running[2] / jnp.transpose(running[1])[:, :, None]
    return attended.reshape(rows_here, width_here).astype(jnp.bfloat16)


def solution(mesh):
    in_specs = (
        P(("batch", "ctx"), "row"),
        P(("batch", "ctx"), "row"),
        P(("batch", "ctx"), "row"),
        P("row"),
        P("row"),
        P(("batch", "ctx")),
        P("batch", None),
    )
    out_specs = P(("batch", "ctx"), "row")
    pair_of_chips = mesh.shape["ctx"] == 4 and mesh.shape["row"] == 2
    return jax.shard_map(
        on_device if pair_of_chips else on_any,
        mesh=mesh, in_specs=in_specs, out_specs=out_specs, check_vma=False,
    )
```

```python
import functools
import math

import jax
import jax.numpy as jnp
from jax import lax
from jax.experimental import pallas as pl
from jax.experimental.pallas import tpu as pltpu
from jax.sharding import PartitionSpec as P

HD = 128
D = 5120
CLIPS = 4
EPSILON = 1e-06
NEGATIVE = -1e30
ROTARY_BASE = 10000.0
block_limit = 1024

ROWS = 192
CHIP = 2 * ROWS
MOST = 480
NEAR = 96
REST = CHIP - NEAR
HALF = 5
WIDE = HALF * HD
TILE = 192
SHORT = 640
FIRST_ROWS = 1600
SECOND_ROWS = 1600
SUM_ROWS = 32
STREAM_ROWS = FIRST_ROWS + SECOND_ROWS
BACK_ROWS = 640
ACROSS = ((0, 2), (1, 3), (2, 0), (3, 1))
BESIDE = ((0, 1), (1, 0), (2, 3), (3, 2))
STRAIGHT = ((1, 3), (2, 0))
SLANTED = ((1, 2), (2, 1))
OTHER_ROW = ((0, 1), (1, 0))
OPPOSITE = tuple((2 * a + r, 2 * b + 1 - r) for a, b in BESIDE for r in (0, 1))
SCORE_SCALE = math.log2(math.e) / math.sqrt(HD)
VMEM = 24 * 1024 * 1024
ALL_VMEM = 60 * 1024 * 1024


def plan(start, side):
    first = start // 16 * 16
    last = (start + MOST + 15) // 16 * 16
    below, above = CHIP - first, last - CHIP
    mine = jnp.where(side == 0, below, above)
    theirs = jnp.where(side == 0, above, below)
    most = jnp.maximum(mine, theirs)
    lent = sum((most > limit).astype(jnp.int32) for limit in (256, 272, 288, 320, 352))
    return first, mine, theirs, HALF - lent, (mine > theirs).astype(jnp.int32)


def position():
    me = lax.axis_index("ctx")
    return me // 2, lax.rem(me, 2)


def known(info):
    row = info[...]
    lane = lax.broadcasted_iota(jnp.int32, row.shape, 1)
    start = jnp.sum(jnp.where(lane == 0, row, 0.0)).astype(jnp.int32)
    side, core = position()
    return side, core, start, row[:, 1:2], plan(start, side)


def sixteen(offset):
    return pl.multiple_of(offset, 16)


def deal_kernel(q_ref, k_ref, v_ref, ids, out, near_own, near_other, sums):
    side, core = position()
    half = out.shape[2]
    at = pl.ds(pl.multiple_of((1 - core) * half, 128), half)
    own = pl.ds(pl.multiple_of(core * half, 128), half)
    rows = pl.ds(sixteen((1 - side) * NEAR), NEAR)
    for i, ref in enumerate((k_ref, v_ref)):
        near_own[i] = ref[rows, own]
        near_other[i] = ref[rows, at]
    for i, ref in enumerate((q_ref, k_ref, v_ref)):
        out[i] = ref[:, at]
    for i, ref in enumerate((q_ref, k_ref)):
        lanes = jnp.zeros((ROWS, HD), jnp.float32)
        for column in range(0, ref.shape[1], HD):
            x = ref[:, column : column + HD].astype(jnp.float32)
            lanes += x * x
        sums[i : i + 1, :] = jnp.sum(jnp.transpose(lanes), axis=0, keepdims=True)
    sums[2:3, :] = ids[...].astype(jnp.float32)


def side_by_side(core, here, there, out):
    for ref, at in ((here, 0), (there, 1)):

        @pl.when(core == at)
        def _():
            out[:, :ROWS] = ref

        @pl.when(core != at)
        def _():
            out[:, ROWS:] = ref


def pack_kernel(
    q_ref, k_ref, v_ref, mate, sums, mate_sums, row_sums, mate_row_sums,
    first_out, second_out, totals, info, chip, buffer,
):
    side, core = position()
    here, there = sums[2:3, :], mate_sums[2:3, :]
    edge = jnp.where(
        side == 0,
        jnp.maximum(jnp.max(here), jnp.max(there)),
        jnp.minimum(jnp.min(here), jnp.min(there)),
    )
    count = (
        jnp.sum(jnp.where(here == edge, 1.0, 0.0)) + jnp.sum(jnp.where(there == edge, 1.0, 0.0))
    ).astype(jnp.int32)
    start = jnp.where(side == 0, CHIP - count, count - NEAR)
    first, mine, _, kept, major = plan(start, side)
    lane = lax.broadcasted_iota(jnp.int32, info.shape, 1)
    info[...] = jnp.where(lane == 0, start.astype(jnp.float32), edge)
    half = chip.shape[2]
    columns = pl.ds(pl.multiple_of(core * half, 128), half)
    for i, ref in enumerate((q_ref, k_ref, v_ref)):
        chip[i, pl.ds(sixteen(core * ROWS), ROWS), :] = ref[:, columns]
        chip[i, pl.ds(sixteen((1 - core) * ROWS), ROWS), :] = mate[i]
        chip[i, CHIP:, :] = jnp.zeros((NEAR, half), ref.dtype)
    buffer[...] = jnp.zeros_like(buffer)
    near_at = jnp.where(side == 0, REST, 0)
    rest_at = jnp.where(side == 0, first, NEAR)
    rest = mine - NEAR

    def put(offset, which, head, row, length):
        at = slice(head * HD, (head + 1) * HD)

        def step(i, carry):
            buffer[pl.ds(sixteen(offset + i * NEAR), NEAR), :] = chip[
                which, pl.ds(sixteen(row + i * NEAR), NEAR), at
            ]
            return carry

        lax.fori_loop(0, (length + NEAR - 1) // NEAR, step, 0)

    offset = jnp.int32(0)
    for i in range(HALF):
        head = HALF + i
        lend = jnp.logical_and(i >= kept, major == 0)
        send = jnp.logical_or(i < kept, major == 0)
        put(offset, 0, head, near_at, jnp.where(lend, NEAR, 0))
        offset += jnp.where(lend, NEAR, 0)
        put(offset, 0, head, rest_at, jnp.where(lend, rest, 0))
        offset += jnp.where(lend, rest, 0)
        length = jnp.where(send, rest, 0)
        for which in (1, 2):
            put(offset, which, head, rest_at, length)
            offset += length
    for head in range(HALF):
        for which in (1, 2):
            put(offset, which, head, rest_at, rest)
            offset += rest
    side_by_side(
        core, sums[:2, :] + row_sums[:2, :], mate_sums[:2, :] + mate_row_sums[:2, :], totals
    )
    parts = []
    for i in range(2):
        left = totals[i : i + 1, :]
        for _ in range(3):
            part = left.astype(jnp.bfloat16)
            left = left - part.astype(jnp.float32)
            parts += [part[:, t : t + HD] for t in range(0, CHIP, HD)]
    parts += [jnp.zeros_like(parts[0])] * (SUM_ROWS - len(parts))
    first_out[:FIRST_ROWS, :] = buffer[:FIRST_ROWS, :]
    first_out[FIRST_ROWS:, :] = jnp.concatenate(parts, axis=0)
    second_out[...] = buffer[FIRST_ROWS:STREAM_ROWS, :]


def turn(x, gain, gain_s, swap, cosine, sine):
    other = jnp.dot(x, swap, preferred_element_type=jnp.float32)
    return ((x.astype(jnp.float32) * gain) * cosine + (other * gain_s) * sine).astype(jnp.bfloat16)


def flip(gain):
    size = gain.shape[1]
    even = lax.broadcasted_iota(jnp.int32, gain.shape, 1) % 2 == 0
    return jnp.where(even, pltpu.roll(gain, size - 1, 1), pltpu.roll(gain, 1, 1))


def signed_swap():
    at_row = lax.broadcasted_iota(jnp.int32, (HD, HD), 0)
    at_column = lax.broadcasted_iota(jnp.int32, (HD, HD), 1)
    sign = jnp.where(at_column % 2 == 0, -1.0, 1.0)
    return jnp.where(at_row == (at_column ^ 1), sign, 0.0).astype(jnp.bfloat16)


def attention(q, keys, bias, values):
    scores = lax.dot_general(
        q, keys, (((1,), (1,)), ((), ())), preferred_element_type=jnp.float32
    ) + bias
    peak = jnp.max(scores, axis=1, keepdims=True)
    weights = jnp.exp2((scores - peak) * SCORE_SCALE).astype(jnp.bfloat16)
    columns = jnp.concatenate([values, jnp.ones_like(values)], axis=1)
    sums = jnp.dot(weights, columns, preferred_element_type=jnp.float32)
    return (sums[:, :HD] / sums[:, HD:]).astype(jnp.bfloat16)


def columns_of(row):
    return jnp.transpose(jnp.broadcast_to(row, (HD, row.shape[1])))


def waves_kernel(grid, info, sums, mate_sums, freqs, cosine, sine, ids, chip_ids):
    side, core, start, edge, (first, *_) = known(info)
    side_by_side(core, sums[2:3, :], mate_sums[2:3, :], chip_ids)
    here = chip_ids[...]
    slot = lax.broadcasted_iota(jnp.int32, (1, CHIP), 1)
    rest_start = jnp.where(side == 0, CHIP, first - NEAR)
    rest_end = jnp.where(side == 0, start + MOST, REST)
    token = slot + jnp.where(slot < NEAR, jnp.where(side == 0, CHIP, REST), rest_start)
    valid = jnp.logical_or(
        slot < NEAR, jnp.logical_and(token >= start, token < rest_end)
    )
    ids[:, :CHIP] = here
    ids[:, CHIP:] = jnp.where(valid, edge, -1.0)
    place = slot.astype(jnp.float32)
    offset, height, line_size = place, jnp.zeros_like(place), jnp.zeros_like(place)
    for label in range(CLIPS):
        same = here == float(label)
        below = jnp.sum(jnp.where(here < float(label), 1.0, 0.0), axis=1, keepdims=True)
        offset = offset - jnp.where(same, below, 0.0)
        height = height + jnp.where(same, grid[label, 0].astype(jnp.float32), 0.0)
        line_size = line_size + jnp.where(same, grid[label, 1].astype(jnp.float32), 0.0)
    carried = jnp.logical_and(here == edge, side == 1)
    offset = jnp.where(carried, place + (CHIP - start).astype(jnp.float32), offset)
    far_offset = jnp.maximum(token - start, 0).astype(jnp.float32)
    ones = jnp.ones_like(place)
    offset = jnp.concatenate([offset, far_offset], axis=1)
    far_sizes = []
    for axis in range(2):
        sizes = [jnp.where(edge == float(c), grid[c, axis].astype(jnp.float32), 0.0) for c in range(CLIPS)]
        far_sizes.append(ones * sum(sizes))
    height = jnp.concatenate([height, far_sizes[0]], axis=1)
    line_size = jnp.concatenate([line_size, far_sizes[1]], axis=1)
    frame = jnp.floor((offset + 0.5) / (height * line_size))
    offset = offset - frame * (height * line_size)
    line = jnp.floor((offset + 0.5) / line_size)
    column = offset - line * line_size
    sixth_part = HD // 6
    first_dims = HD - 4 * sixth_part
    feature = lax.broadcasted_iota(jnp.int32, (1, HD), 1)
    angles = freqs[...] * jnp.where(
        feature < first_dims,
        columns_of(frame),
        jnp.where(feature < first_dims + 2 * sixth_part, columns_of(line), columns_of(column)),
    )
    cosine[...] = jnp.cos(angles)
    sine[...] = jnp.sin(angles)


def turn_kernel(q_ref, k_ref, v_ref, mate, cosine, sine, totals, gq, gk, out, table):
    _, core = position()
    half = out.shape[2]
    columns = pl.ds(pl.multiple_of(core * half, 128), half)
    swap = signed_swap()
    for i in range(2):
        scale = columns_of(lax.rsqrt(totals[i : i + 1, :] / D + EPSILON))
        for j, ref in enumerate((cosine, sine)):
            table[2 * i + j] = ref[:CHIP, :] * scale
    for here, rows in ((True, core), (False, 1 - core)):
        rows = pl.ds(sixteen(rows * ROWS), ROWS)
        out[2, rows, :] = v_ref[:, columns] if here else mate[2]
        for i, (ref, gains) in enumerate(((q_ref, gq), (k_ref, gk))):
            cos_here, sin_here = table[2 * i, rows, :], table[2 * i + 1, rows, :]
            for h in range(half // HD):
                at = slice(h * HD, (h + 1) * HD)
                place = pl.ds(pl.multiple_of(core * half + h * HD, 128), HD)
                gain = gains[:, place]
                x = ref[:, place] if here else mate[i, :, at]
                out[i, rows, at] = turn(x, gain, flip(gain), swap, cos_here, sin_here)


def local_kernel(local, ids, partial, peaks, bias):
    clip_of = columns_of(ids[:, :CHIP])
    for t in range(0, CHIP, HD):
        bias[:, t : t + HD] = jnp.where(clip_of == ids[:, t : t + HD], 0.0, NEGATIVE)
    for h in range(HALF):
        at = slice(h * HD, (h + 1) * HD)
        values = local[2, :, at]
        columns = jnp.concatenate([values, jnp.ones_like(values)], axis=1)
        for t in range(0, CHIP, TILE):
            rows = slice(t, t + TILE)
            scores = lax.dot_general(
                local[0, rows, at], local[1, :, at], (((1,), (1,)), ((), ())),
                preferred_element_type=jnp.float32,
            ) + bias[rows, :]
            peak = jnp.max(scores, axis=1, keepdims=True)
            weights = jnp.exp2((scores - peak) * SCORE_SCALE).astype(jnp.bfloat16)
            partial[rows, 2 * h * HD : 2 * (h + 1) * HD] = jnp.dot(
                weights, columns, preferred_element_type=jnp.float32
            )
            peaks[rows, at] = jnp.broadcast_to(peak, (TILE, HD))


def attend_kernel(flexible, head, count, info, *refs):
    local, near_straight, near_slanted, gq, gk, ids = refs[:6]
    streams = 1 if flexible else 2
    refs = refs[6:]
    if flexible:
        (cosine, sine), refs = refs[:2], refs[2:]
    else:
        (table, partial, peaks), refs = refs[:3], refs[3:]
    arrived, refs = refs[:streams], refs[streams:]
    own_out, mate_out, refs = refs[0], refs[1], refs[2:]
    if flexible:
        back, table, refs = refs[0], refs[1], refs[2:]
    near, stream, bias, keys, values, result, sems = refs[:7]
    side, core, _, edge, (first, _, theirs, kept, major) = known(info)
    inner = side != core
    rest = theirs - NEAR
    near_columns = slice(head * HD, (head + count) * HD)
    sizes = (FIRST_ROWS, SECOND_ROWS)[:streams]
    copies, filled = [], 0
    for i, (ref, size) in enumerate(zip(arrived, sizes)):
        copies.append(
            pltpu.make_async_copy(
                ref.at[:size, :], stream.at[filled : filled + size, :], sems.at[1 + i]
            )
        )
        filled += size
    near_copies = [
        pltpu.make_async_copy(ref.at[:, :, near_columns], near, sems.at[0])
        for ref in (near_slanted, near_straight)
    ]
    for copy in copies:
        copy.start()
    pl.when(inner)(near_copies[0].start)
    pl.when(jnp.logical_not(inner))(near_copies[1].start)
    stream[filled:, :] = jnp.zeros((REST, HD), stream.dtype)

    columns = pl.ds(pl.multiple_of((2 * HALF * core + head) * HD, 128), count * HD)
    gq, gk = gq[:, columns], gk[:, columns]
    clip_of = columns_of(ids[:, :CHIP])
    for t in range(0 if flexible else CHIP, 2 * CHIP, HD):
        bias[:, t : t + HD] = jnp.where(clip_of == ids[:, t : t + HD], 0.0, NEGATIVE)
    for h in range(count if flexible else 0):
        here = slice((head + h) * HD, (head + h + 1) * HD)
        keys[h, :CHIP, :] = local[1, :, here]
        values[h, :CHIP, :] = local[2, :, here]
    if flexible:
        back_rows, asked, scales, extra = refs[7:11]
        sum_copy = pltpu.make_async_copy(arrived[0].at[FIRST_ROWS:, :], extra, sems.at[4])
        sum_copy.start()
        near_rows = pl.ds(sixteen(jnp.where(side == 0, 0, REST)), NEAR)
        rest_rows = pl.ds(sixteen(jnp.where(side == 0, NEAR, first)), REST)
        scales[CHIP:, :] = jnp.ones((REST, HD), jnp.float32)
        back_rows[...] = jnp.zeros_like(back_rows)
        sum_copy.wait()
        parts = extra[...].astype(jnp.float32)
        for i, waves in enumerate((asked, table)):
            for j in range(3):
                total = sum(parts[9 * i + 3 * p + j : 9 * i + 3 * p + j + 1, :] for p in range(3))
                scales[j * HD : (j + 1) * HD, :] = columns_of(lax.rsqrt(total / D + EPSILON))
            for j, ref in enumerate((cosine, sine)):
                waves[j, :NEAR, :] = ref[CHIP : CHIP + NEAR, :] * scales[near_rows, :]
                waves[j, NEAR:, :] = ref[CHIP + NEAR :, :] * scales[rest_rows, :]
    near_copies[0].wait()
    for copy in copies:
        copy.wait()

    swap = signed_swap()
    if flexible:
        base = jnp.int32(0)
    else:
        base = 2 * rest * kept + jnp.where(major == 1, (HALF - kept) * (2 * rest + theirs), 0)
        base += 2 * rest * head
    bases = []
    for h in range(count):
        at = slice(h * HD, (h + 1) * HD)
        gain = gk[:, at]
        key_at = base
        bases.append(base)
        if flexible:
            lend = jnp.logical_and(h >= kept, major == 1)
            took = jnp.logical_or(h < kept, major == 1)
            key_at = base + jnp.where(lend, theirs, 0)
            base += jnp.where(took, 2 * rest, 0) + jnp.where(lend, theirs, 0)
        else:
            base += 2 * rest
        far = jnp.concatenate([near[0, :, at], stream[pl.ds(sixteen(key_at), REST), :]], axis=0)
        keys[h, CHIP:, :] = turn(far, gain, flip(gain), swap, table[0], table[1])
        values[h, CHIP : CHIP + NEAR, :] = near[1, :, at]
        values[h, CHIP + NEAR :, :] = stream[pl.ds(sixteen(key_at + rest), REST), :]

    def far_answer(h, size):
        at = slice(h * HD, (h + 1) * HD)
        gain = gq[:, at]
        x = stream[pl.ds(sixteen(bases[h]), size), :]
        far_q = turn(x, gain, flip(gain), swap, asked[0, :size, :], asked[1, :size, :])
        place = jnp.where(h >= kept, (h - kept) * theirs, BACK_ROWS + HD)
        back_rows[pl.ds(sixteen(place), size), :] = attention(
            far_q, keys[h, :SHORT, :], far_bias, values[h, :SHORT, :]
        )

    def answers(seen, lent):
        for h in range(count):
            at = slice(h * HD, (h + 1) * HD)
            here = slice((head + h) * HD, (head + h + 1) * HD)
            for t in range(0, CHIP, TILE):
                rows = slice(t, t + TILE)
                result[rows, at] = attention(
                    local[0, rows, here], keys[h, :seen, :], bias[rows, :seen], values[h, :seen, :]
                )
            if lent == HD or (lent and h > 0):
                far_answer(h, lent)

    def merged(seen):
        for h in range(count):
            at = slice(h * HD, (h + 1) * HD)
            here = slice((head + h) * HD, (head + h + 1) * HD)
            far = values[h, CHIP:seen, :]
            columns = jnp.concatenate([far, jnp.ones_like(far)], axis=1)
            for t in range(0, CHIP, HD):
                rows = slice(t, t + HD)
                scores = lax.dot_general(
                    local[0, rows, here], keys[h, CHIP:seen, :], (((1,), (1,)), ((), ())),
                    preferred_element_type=jnp.float32,
                ) + bias[rows, CHIP:seen]
                before = peaks[rows, h * HD : h * HD + 1]
                peak = jnp.maximum(before, jnp.max(scores, axis=1, keepdims=True))
                weights = jnp.exp2((scores - peak) * SCORE_SCALE).astype(jnp.bfloat16)
                sums = jnp.dot(weights, columns, preferred_element_type=jnp.float32)
                sums += jnp.exp2((before - peak) * SCORE_SCALE) * partial[
                    rows, 2 * h * HD : 2 * (h + 1) * HD
                ]
                result[rows, at] = (sums[:, :HD] / sums[:, HD:]).astype(jnp.bfloat16)

    short = theirs <= SHORT - CHIP
    if flexible:
        far_bias = jnp.where(ids[:, :SHORT] == edge, 0.0, NEGATIVE)
        lending = jnp.logical_and(kept < HALF, major == 1)

        wide = theirs > HD
        pl.when(jnp.logical_and(lending, wide))(lambda: answers(SHORT, 2 * HD))
        pl.when(jnp.logical_and(lending, jnp.logical_not(wide)))(lambda: answers(SHORT, HD))
        pl.when(jnp.logical_and(short, jnp.logical_not(lending)))(lambda: answers(SHORT, 0))
        pl.when(jnp.logical_not(short))(lambda: answers(2 * CHIP, 0))
    else:
        pl.when(short)(lambda: merged(SHORT))
        pl.when(jnp.logical_not(short))(lambda: merged(2 * CHIP))
    own_out[...] = result[pl.ds(sixteen(core * ROWS), ROWS), :]
    mate_out[...] = result[pl.ds(sixteen((1 - core) * ROWS), ROWS), :]
    if flexible:
        back[...] = back_rows[:BACK_ROWS, :]


def join_kernel(
    info, flex_here, fixed_here, flex_there, fixed_there, back_here, back_there, ids, out, rows, lines
):
    side, core, _, edge, (first, mine, _, kept, major) = known(info)
    half = 2 * WIDE
    inside = columns_of(ids[...].astype(jnp.float32)) == edge
    for here, flex, fixed, back in (
        (True, flex_here, fixed_here, back_here),
        (False, flex_there, fixed_there, back_there),
    ):
        column = pl.multiple_of((core if here else 1 - core) * half, 128)
        out[:, pl.ds(column, WIDE)] = fixed[...]
        out[:, pl.ds(pl.multiple_of(column + WIDE, 128), WIDE)] = flex[...]

        @pl.when(jnp.logical_and(major == 0, kept < HALF))
        def _():
            rows[:BACK_ROWS, :] = back[...]
            rows[BACK_ROWS:, :] = jnp.zeros((REST, HD), rows.dtype)
            for h in range(HALF):

                @pl.when(h >= kept)
                def _():
                    base = (h - kept) * mine
                    near_at = jnp.where(side == 0, REST, 0)
                    rest_at = jnp.where(side == 0, first, NEAR)
                    lines[pl.ds(sixteen(rest_at), REST), :] = rows[
                        pl.ds(sixteen(base + NEAR), REST), :
                    ]
                    lines[pl.ds(sixteen(near_at), NEAR), :] = rows[pl.ds(sixteen(base), NEAR), :]
                    at = slice(h * HD, (h + 1) * HD)
                    place = pl.ds(pl.multiple_of(column + WIDE + h * HD, 128), HD)
                    out[:, place] = jnp.where(
                        inside, lines[pl.ds(sixteen(core * ROWS), ROWS), :], flex[:, at]
                    )


def frequencies():
    sixth_part = HD // 6
    first_dims = HD - 4 * sixth_part
    first_freqs = 1.0 / ROTARY_BASE ** (
        jnp.arange(0, first_dims, 2, dtype=jnp.float32) / first_dims
    )
    other_freqs = 1.0 / ROTARY_BASE ** (
        jnp.arange(0, 2 * sixth_part, 2, dtype=jnp.float32) / (2 * sixth_part)
    )
    return jnp.repeat(jnp.concatenate([first_freqs, other_freqs, other_freqs]), 2)[None, :]


def whole(a):
    return pl.BlockSpec(a.shape, lambda i: (0,) * len(a.shape))


def held():
    return pl.BlockSpec(memory_space=pltpu.VMEM)


def call(kernel, out_shape, in_specs, out_specs, scratch, *operands, limit=VMEM):
    return pl.pallas_call(
        kernel,
        grid=(1,),
        out_shape=out_shape,
        in_specs=in_specs,
        out_specs=out_specs,
        scratch_shapes=scratch,
        compiler_params=pltpu.CompilerParams(vmem_limit_bytes=limit),
        cost_estimate=pl.CostEstimate(flops=0, bytes_accessed=0, transcendentals=0),
    )(*operands)


def attend(flexible, head, count, info, streams, waves, local, near_straight, near_slanted, gains, ids):
    bf16, f32 = jnp.bfloat16, jnp.float32
    there = pl.BlockSpec(memory_space=pl.ANY)
    shapes = [jax.ShapeDtypeStruct((ROWS, count * HD), bf16)] * 2
    stream_rows = sum((FIRST_ROWS, SECOND_ROWS)[: len(streams)]) + REST
    scratch = [
        pltpu.VMEM((2, NEAR, count * HD), bf16),
        pltpu.VMEM((stream_rows, HD), bf16),
        pltpu.VMEM((CHIP, 2 * CHIP), f32),
        pltpu.VMEM((count, 2 * CHIP, HD), bf16),
        pltpu.VMEM((count, 2 * CHIP, HD), bf16),
        pltpu.VMEM((CHIP, count * HD), bf16),
        pltpu.SemaphoreType.DMA((5,)),
    ]
    if flexible:
        far_waves = jax.ShapeDtypeStruct((2, CHIP, HD), f32)
        shapes = shapes + [jax.ShapeDtypeStruct((BACK_ROWS, HD), bf16), far_waves]
        scratch = scratch + [
            pltpu.VMEM((BACK_ROWS + 3 * HD, HD), bf16),
            pltpu.VMEM((2, CHIP, HD), f32),
            pltpu.VMEM((CHIP + REST, HD), f32),
            pltpu.VMEM((SUM_ROWS, HD), bf16),
        ]
    operands = (local, near_straight, near_slanted, *gains, ids, *waves, *streams)
    in_specs = [held(), held(), there, there] + [held()] * (3 + len(waves)) + [there] * len(streams)
    return call(
        functools.partial(attend_kernel, flexible, head, count), shapes,
        in_specs, [held()] * len(shapes), scratch, info, *operands,
    )


def on_device(queries, keys, values, gain_q, gain_k, clip_ids, clip_grid):
    width = queries.shape[1]
    half = width // 2
    bf16, f32 = jnp.bfloat16, jnp.float32

    clip_row = clip_ids[None, :]

    near_shape = jax.ShapeDtypeStruct((2, NEAR, half), bf16)
    deal_shapes = [
        jax.ShapeDtypeStruct((3, ROWS, half), bf16),
        near_shape,
        near_shape,
        jax.ShapeDtypeStruct((3, ROWS), f32),
    ]
    dealt, near_own, near_other, sums = call(
        deal_kernel, deal_shapes, [whole(queries)] * 3 + [whole(clip_row)],
        [whole(s) for s in deal_shapes], [], queries, keys, values, clip_row, limit=ALL_VMEM,
    )
    near_straight = lax.ppermute(near_own, "ctx", STRAIGHT)
    near_slanted = lax.ppermute(near_other, "ctx", SLANTED)
    mate = lax.ppermute(dealt, "ctx", BESIDE)
    mate_sums = lax.ppermute(sums, "ctx", BESIDE)
    row_sums = lax.ppermute(sums, "row", OTHER_ROW)
    mate_row_sums = lax.ppermute(sums, ("ctx", "row"), OPPOSITE)
    stream_shapes = [
        jax.ShapeDtypeStruct((FIRST_ROWS + SUM_ROWS, HD), bf16),
        jax.ShapeDtypeStruct((SECOND_ROWS, HD), bf16),
        jax.ShapeDtypeStruct((2, CHIP), f32),
    ]
    first_send, second_send, totals, info = call(
        pack_kernel, stream_shapes + [jax.ShapeDtypeStruct((1, HD), f32)],
        [held()] * 8, [whole(shape) for shape in stream_shapes[:2]] + [held()] * 2,
        [
            pltpu.VMEM((3, CHIP + NEAR, half), bf16),
            pltpu.VMEM((STREAM_ROWS + NEAR, HD), bf16),
        ],
        queries, keys, values, mate, sums, mate_sums, row_sums, mate_row_sums,
    )

    first_stream = lax.ppermute(first_send, "ctx", ACROSS)
    second_stream = lax.ppermute(second_send, "ctx", ACROSS)
    near_straight, near_slanted, sums, _ = lax.optimization_barrier(
        (near_straight, near_slanted, sums, first_send)
    )
    wave_shape = jax.ShapeDtypeStruct((2 * CHIP, HD), f32)
    cosine, sine, mask_ids = call(
        waves_kernel, [wave_shape, wave_shape, jax.ShapeDtypeStruct((1, 2 * CHIP), f32)],
        [pl.BlockSpec(memory_space=pltpu.SMEM)] + [held()] * 4, [held()] * 3,
        [pltpu.VMEM((1, CHIP), f32)], clip_grid, info, sums, mate_sums, frequencies(),
    )
    gains = (gain_q[None, :], gain_k[None, :])
    local_shape = jax.ShapeDtypeStruct((3, CHIP, half), bf16)
    local = call(
        turn_kernel, local_shape, [held()] * 9, held(), [pltpu.VMEM((4, CHIP, HD), f32)],
        queries, keys, values, mate, cosine, sine, totals, *gains,
    )
    common = (local, near_straight, near_slanted, gains, mask_ids)
    partial, peaks = call(
        local_kernel,
        [
            jax.ShapeDtypeStruct((CHIP, 2 * WIDE), f32),
            jax.ShapeDtypeStruct((CHIP, WIDE), f32),
        ],
        [held()] * 2, [held()] * 2, [pltpu.VMEM((CHIP, CHIP), f32)], local, mask_ids,
    )
    first_stream, partial = lax.optimization_barrier((first_stream, partial))
    flex_here, flex_send, back_send, far_waves = attend(
        True, HALF, HALF, info, (first_stream,), (cosine, sine), *common
    )
    back_here = lax.ppermute(back_send, "ctx", ACROSS)
    fixed_here, fixed_send = attend(
        False, 0, HALF, info, (first_stream, second_stream),
        (far_waves, partial, peaks), *common
    )
    flex_send, fixed_send = lax.optimization_barrier((flex_send, fixed_send))
    flex_there = lax.ppermute(flex_send, "ctx", BESIDE)
    fixed_there = lax.ppermute(fixed_send, "ctx", BESIDE)
    back_here, _ = lax.optimization_barrier((back_here, fixed_send))
    back_there = lax.ppermute(back_here, "ctx", BESIDE)
    out_shape = jax.ShapeDtypeStruct((ROWS, width), bf16)
    operands = (
        flex_here, fixed_here, flex_there, fixed_there, back_here, back_there, clip_row
    )
    return call(
        join_kernel, out_shape, [held()] * 8, whole(out_shape),
        [pltpu.VMEM((BACK_ROWS + REST, HD), bf16), pltpu.VMEM((2 * REST, HD), bf16)],
        info, *operands,
    )


def lookup(lookup_table, positions):
    labels = jnp.arange(lookup_table.shape[0], dtype=jnp.int32)
    return jnp.sum(
        jnp.where(positions[:, None] == labels[None, :], lookup_table[None, :], 0), axis=1
    )


def spin(matrix, offsets, clip_of, clip_grid, head_size):
    row_count = matrix.shape[0]
    sixth_part = head_size // 6
    first_dims = head_size - 4 * sixth_part
    first_freqs = 1.0 / ROTARY_BASE ** (
        jnp.arange(0, first_dims, 2, dtype=jnp.float32) / first_dims
    )
    other_freqs = 1.0 / ROTARY_BASE ** (
        jnp.arange(0, 2 * sixth_part, 2, dtype=jnp.float32) / (2 * sixth_part)
    )
    heights = lookup(clip_grid[:, 0], clip_of)
    widths = lookup(clip_grid[:, 1], clip_of)
    frame_pos = offsets // (heights * widths)
    line_pos = offsets // widths % heights
    column_pos = offsets % widths
    angles = jnp.concatenate(
        [
            frame_pos.astype(jnp.float32)[:, None] * first_freqs[None, :],
            line_pos.astype(jnp.float32)[:, None] * other_freqs[None, :],
            column_pos.astype(jnp.float32)[:, None] * other_freqs[None, :],
        ],
        axis=1,
    )
    cosine = jnp.repeat(jnp.cos(angles), 2, axis=1)
    sine_table = jnp.repeat(jnp.sin(angles), 2, axis=1)
    feature = jnp.arange(head_size, dtype=jnp.int32)
    is_even = (feature % 2 == 0)[None, None, :]
    head_view = matrix.reshape(row_count, -1, head_size)
    partner = jnp.where(is_even, -jnp.roll(head_view, -1, axis=2), jnp.roll(head_view, 1, axis=2))
    turned = head_view * cosine[:, None, :] + partner * sine_table[:, None, :]
    return turned.reshape(row_count, -1)


def on_any(queries, keys, values, gain_q, gain_k, clip_ids, clip_grid):
    rows_here, width_here = queries.shape
    heads_here = width_here // HD
    score_scale = 1.0 / math.sqrt(HD)
    query_wide = queries.astype(jnp.float32)
    key_wide = keys.astype(jnp.float32)
    squares = lax.psum(
        (jnp.sum(query_wide * query_wide, axis=1), jnp.sum(key_wide * key_wide, axis=1)), "row"
    )
    query_scale = lax.rsqrt(squares[0] / D + EPSILON)
    key_scale = lax.rsqrt(squares[1] / D + EPSILON)
    labels = jnp.arange(CLIPS, dtype=jnp.int32)
    local_counts = jnp.sum((clip_ids[:, None] == labels[None, :]).astype(jnp.int32), axis=0)
    totals = lax.psum(local_counts, "ctx")
    starts = jnp.cumsum(totals) - totals
    first_row = lax.axis_index("ctx") * rows_here
    offsets = first_row + jnp.arange(rows_here, dtype=jnp.int32) - lookup(starts, clip_ids)
    query_rot = spin(
        query_wide * query_scale[:, None] * gain_q[None, :], offsets, clip_ids, clip_grid, HD
    ).astype(jnp.bfloat16)
    query_heads = query_rot.reshape(rows_here, heads_here, HD)
    key_send = spin(
        key_wide * key_scale[:, None] * gain_k[None, :], offsets, clip_ids, clip_grid, HD
    ).astype(jnp.bfloat16)
    initial = (
        jnp.full((heads_here, rows_here), NEGATIVE, jnp.float32),
        jnp.zeros((heads_here, rows_here), jnp.float32),
        jnp.zeros((rows_here, heads_here, HD), jnp.float32),
    )
    running = initial
    piece_start = jnp.int32(0)
    key_piece = lax.all_gather(key_send, "ctx", axis=0, tiled=True)
    value_piece = lax.all_gather(values, "ctx", axis=0, tiled=True)
    row_count = key_piece.shape[0]
    block_rows = min(row_count, block_limit)
    for block_first in range(0, row_count, block_rows):
        block_size = min(block_rows, row_count - block_first)
        fold_key_rows = key_piece[block_first : block_first + block_size]
        fold_value_rows = value_piece[block_first : block_first + block_size]
        key_index = piece_start + block_first + jnp.arange(fold_key_rows.shape[0], dtype=jnp.int32)
        key_key_clips = (
            jnp.sum((starts[None, :] <= key_index[:, None]).astype(jnp.int32), axis=1) - 1
        )
        peak_old, total_old, summed_old = running
        key_view = fold_key_rows.reshape(fold_key_rows.shape[0], heads_here, HD)
        value_view = fold_value_rows.reshape(fold_value_rows.shape[0], heads_here, HD)
        scores = (
            jnp.einsum("qhd,khd->hqk", query_heads, key_view, preferred_element_type=jnp.float32)
            * score_scale
        )
        same = clip_ids[:, None] == key_key_clips[None, :]
        masked = jnp.where(same[None, :, :], scores, NEGATIVE)
        peak_new = jnp.maximum(peak_old, jnp.max(masked, axis=2))
        weights = jnp.where(same[None, :, :], jnp.exp(masked - peak_new[:, :, None]), 0.0)
        factor = jnp.exp(peak_old - peak_new)
        total_new = total_old * factor + jnp.sum(weights, axis=2)
        summed = summed_old * jnp.transpose(factor)[:, :, None] + jnp.einsum(
            "hqk,khd->qhd",
            weights.astype(jnp.bfloat16),
            value_view,
            preferred_element_type=jnp.float32,
        )
        running = (peak_new, total_new, summed)
    attended = running[2] / jnp.transpose(running[1])[:, :, None]
    return attended.reshape(rows_here, width_here).astype(jnp.bfloat16)


def solution(mesh):
    in_specs = (
        P(("batch", "ctx"), "row"),
        P(("batch", "ctx"), "row"),
        P(("batch", "ctx"), "row"),
        P("row"),
        P("row"),
        P(("batch", "ctx")),
        P("batch", None),
    )
    out_specs = P(("batch", "ctx"), "row")
    pair_of_chips = mesh.shape["ctx"] == 4 and mesh.shape["row"] == 2
    return jax.shard_map(
        on_device if pair_of_chips else on_any,
        mesh=mesh, in_specs=in_specs, out_specs=out_specs, check_vma=False,
    )
```

```python
import functools
import math

import jax
import jax.numpy as jnp
from jax import lax
from jax.experimental import pallas as pl
from jax.experimental.pallas import tpu as pltpu
from jax.sharding import PartitionSpec as P

HD = 128
D = 5120
CLIPS = 4
EPSILON = 1e-06
NEGATIVE = -1e30
ROTARY_BASE = 10000.0
block_limit = 1024

ROWS = 192
CHIP = 2 * ROWS
MOST = 480
NEAR = 96
REST = CHIP - NEAR
HALF = 5
WIDE = HALF * HD
TILE = 128
SHORT = 640
FIRST_ROWS = 1600
SECOND_ROWS = 1600
SUM_ROWS = 32
STREAM_ROWS = FIRST_ROWS + SECOND_ROWS
BACK_ROWS = 640
ACROSS = ((0, 2), (1, 3), (2, 0), (3, 1))
BESIDE = ((0, 1), (1, 0), (2, 3), (3, 2))
STRAIGHT = ((1, 3), (2, 0))
SLANTED = ((1, 2), (2, 1))
OTHER_ROW = ((0, 1), (1, 0))
OPPOSITE = tuple((2 * a + r, 2 * b + 1 - r) for a, b in BESIDE for r in (0, 1))
SCORE_SCALE = math.log2(math.e) / math.sqrt(HD)
VMEM = 24 * 1024 * 1024
ALL_VMEM = 60 * 1024 * 1024


def plan(start, side):
    first = start // 16 * 16
    last = (start + MOST + 15) // 16 * 16
    below, above = CHIP - first, last - CHIP
    mine = jnp.where(side == 0, below, above)
    theirs = jnp.where(side == 0, above, below)
    most = jnp.maximum(mine, theirs)
    lent = sum((most > limit).astype(jnp.int32) for limit in (256, 272, 288, 320, 352))
    return first, mine, theirs, HALF - lent, (mine > theirs).astype(jnp.int32)


def position():
    me = lax.axis_index("ctx")
    return me // 2, lax.rem(me, 2)


def known(info):
    row = info[...]
    lane = lax.broadcasted_iota(jnp.int32, row.shape, 1)
    start = jnp.sum(jnp.where(lane == 0, row, 0.0)).astype(jnp.int32)
    side, core = position()
    return side, core, start, row[:, 1:2], plan(start, side)


def sixteen(offset):
    return pl.multiple_of(offset, 16)


def deal_kernel(q_ref, k_ref, v_ref, ids, out, near_own, near_other, sums):
    side, core = position()
    half = out.shape[2]
    at = pl.ds(pl.multiple_of((1 - core) * half, 128), half)
    own = pl.ds(pl.multiple_of(core * half, 128), half)
    rows = pl.ds(sixteen((1 - side) * NEAR), NEAR)
    for i, ref in enumerate((k_ref, v_ref)):
        near_own[i] = ref[rows, own]
        near_other[i] = ref[rows, at]
    for i, ref in enumerate((q_ref, k_ref, v_ref)):
        out[i] = ref[:, at]
    for i, ref in enumerate((q_ref, k_ref)):
        lanes = jnp.zeros((ROWS, HD), jnp.float32)
        for column in range(0, ref.shape[1], HD):
            x = ref[:, column : column + HD].astype(jnp.float32)
            lanes += x * x
        sums[i : i + 1, :] = jnp.sum(jnp.transpose(lanes), axis=0, keepdims=True)
    sums[2:3, :] = ids[...].astype(jnp.float32)


def side_by_side(core, here, there, out):
    for ref, at in ((here, 0), (there, 1)):

        @pl.when(core == at)
        def _():
            out[:, :ROWS] = ref

        @pl.when(core != at)
        def _():
            out[:, ROWS:] = ref


def pack_kernel(
    q_ref, k_ref, v_ref, mate, sums, mate_sums, row_sums, mate_row_sums,
    first_out, second_out, totals, info, chip, buffer,
):
    side, core = position()
    here, there = sums[2:3, :], mate_sums[2:3, :]
    edge = jnp.where(
        side == 0,
        jnp.maximum(jnp.max(here), jnp.max(there)),
        jnp.minimum(jnp.min(here), jnp.min(there)),
    )
    count = (
        jnp.sum(jnp.where(here == edge, 1.0, 0.0)) + jnp.sum(jnp.where(there == edge, 1.0, 0.0))
    ).astype(jnp.int32)
    start = jnp.where(side == 0, CHIP - count, count - NEAR)
    first, mine, _, kept, major = plan(start, side)
    lane = lax.broadcasted_iota(jnp.int32, info.shape, 1)
    info[...] = jnp.where(lane == 0, start.astype(jnp.float32), edge)
    half = chip.shape[2]
    columns = pl.ds(pl.multiple_of(core * half, 128), half)
    for i, ref in enumerate((q_ref, k_ref, v_ref)):
        chip[i, pl.ds(sixteen(core * ROWS), ROWS), :] = ref[:, columns]
        chip[i, pl.ds(sixteen((1 - core) * ROWS), ROWS), :] = mate[i]
        chip[i, CHIP:, :] = jnp.zeros((NEAR, half), ref.dtype)
    buffer[...] = jnp.zeros_like(buffer)
    near_at = jnp.where(side == 0, REST, 0)
    rest_at = jnp.where(side == 0, first, NEAR)
    rest = mine - NEAR

    def put(offset, which, head, row, length):
        at = slice(head * HD, (head + 1) * HD)

        def step(i, carry):
            buffer[pl.ds(sixteen(offset + i * NEAR), NEAR), :] = chip[
                which, pl.ds(sixteen(row + i * NEAR), NEAR), at
            ]
            return carry

        lax.fori_loop(0, (length + NEAR - 1) // NEAR, step, 0)

    offset = jnp.int32(0)
    for i in range(HALF):
        head = HALF + i
        lend = jnp.logical_and(i >= kept, major == 0)
        send = jnp.logical_or(i < kept, major == 0)
        put(offset, 0, head, near_at, jnp.where(lend, NEAR, 0))
        offset += jnp.where(lend, NEAR, 0)
        put(offset, 0, head, rest_at, jnp.where(lend, rest, 0))
        offset += jnp.where(lend, rest, 0)
        length = jnp.where(send, rest, 0)
        for which in (1, 2):
            put(offset, which, head, rest_at, length)
            offset += length
    for head in range(HALF):
        for which in (1, 2):
            put(offset, which, head, rest_at, rest)
            offset += rest
    side_by_side(
        core, sums[:2, :] + row_sums[:2, :], mate_sums[:2, :] + mate_row_sums[:2, :], totals
    )
    parts = []
    for i in range(2):
        left = totals[i : i + 1, :]
        for _ in range(3):
            part = left.astype(jnp.bfloat16)
            left = left - part.astype(jnp.float32)
            parts += [part[:, t : t + HD] for t in range(0, CHIP, HD)]
    parts += [jnp.zeros_like(parts[0])] * (SUM_ROWS - len(parts))
    first_out[:FIRST_ROWS, :] = buffer[:FIRST_ROWS, :]
    first_out[FIRST_ROWS:, :] = jnp.concatenate(parts, axis=0)
    second_out[...] = buffer[FIRST_ROWS:STREAM_ROWS, :]


def turn(x, gain, gain_s, swap, cosine, sine):
    other = jnp.dot(x, swap, preferred_element_type=jnp.float32)
    return ((x.astype(jnp.float32) * gain) * cosine + (other * gain_s) * sine).astype(jnp.bfloat16)


def flip(gain):
    size = gain.shape[1]
    even = lax.broadcasted_iota(jnp.int32, gain.shape, 1) % 2 == 0
    return jnp.where(even, pltpu.roll(gain, size - 1, 1), pltpu.roll(gain, 1, 1))


def signed_swap():
    at_row = lax.broadcasted_iota(jnp.int32, (HD, HD), 0)
    at_column = lax.broadcasted_iota(jnp.int32, (HD, HD), 1)
    sign = jnp.where(at_column % 2 == 0, -1.0, 1.0)
    return jnp.where(at_row == (at_column ^ 1), sign, 0.0).astype(jnp.bfloat16)


def attention(q, keys, bias, values):
    scores = lax.dot_general(
        q, keys, (((1,), (1,)), ((), ())), preferred_element_type=jnp.float32
    ) + bias
    peak = jnp.max(scores, axis=1, keepdims=True)
    weights = jnp.exp2((scores - peak) * SCORE_SCALE).astype(jnp.bfloat16)
    columns = jnp.concatenate([values, jnp.ones_like(values)], axis=1)
    sums = jnp.dot(weights, columns, preferred_element_type=jnp.float32)
    return (sums[:, :HD] / sums[:, HD:]).astype(jnp.bfloat16)


def columns_of(row):
    return jnp.transpose(jnp.broadcast_to(row, (HD, row.shape[1])))


def waves_kernel(grid, info, sums, mate_sums, freqs, cosine, sine, ids, chip_ids):
    side, core, start, edge, (first, *_) = known(info)
    side_by_side(core, sums[2:3, :], mate_sums[2:3, :], chip_ids)
    here = chip_ids[...]
    slot = lax.broadcasted_iota(jnp.int32, (1, CHIP), 1)
    rest_start = jnp.where(side == 0, CHIP, first - NEAR)
    rest_end = jnp.where(side == 0, start + MOST, REST)
    token = slot + jnp.where(slot < NEAR, jnp.where(side == 0, CHIP, REST), rest_start)
    valid = jnp.logical_or(
        slot < NEAR, jnp.logical_and(token >= start, token < rest_end)
    )
    ids[:, :CHIP] = here
    ids[:, CHIP:] = jnp.where(valid, edge, -1.0)
    place = slot.astype(jnp.float32)
    offset, height, line_size = place, jnp.zeros_like(place), jnp.zeros_like(place)
    for label in range(CLIPS):
        same = here == float(label)
        below = jnp.sum(jnp.where(here < float(label), 1.0, 0.0), axis=1, keepdims=True)
        offset = offset - jnp.where(same, below, 0.0)
        height = height + jnp.where(same, grid[label, 0].astype(jnp.float32), 0.0)
        line_size = line_size + jnp.where(same, grid[label, 1].astype(jnp.float32), 0.0)
    carried = jnp.logical_and(here == edge, side == 1)
    offset = jnp.where(carried, place + (CHIP - start).astype(jnp.float32), offset)
    far_offset = jnp.maximum(token - start, 0).astype(jnp.float32)
    ones = jnp.ones_like(place)
    offset = jnp.concatenate([offset, far_offset], axis=1)
    far_sizes = []
    for axis in range(2):
        sizes = [jnp.where(edge == float(c), grid[c, axis].astype(jnp.float32), 0.0) for c in range(CLIPS)]
        far_sizes.append(ones * sum(sizes))
    height = jnp.concatenate([height, far_sizes[0]], axis=1)
    line_size = jnp.concatenate([line_size, far_sizes[1]], axis=1)
    frame = jnp.floor((offset + 0.5) / (height * line_size))
    offset = offset - frame * (height * line_size)
    line = jnp.floor((offset + 0.5) / line_size)
    column = offset - line * line_size
    sixth_part = HD // 6
    first_dims = HD - 4 * sixth_part
    feature = lax.broadcasted_iota(jnp.int32, (1, HD), 1)
    angles = freqs[...] * jnp.where(
        feature < first_dims,
        columns_of(frame),
        jnp.where(feature < first_dims + 2 * sixth_part, columns_of(line), columns_of(column)),
    )
    cosine[...] = jnp.cos(angles)
    sine[...] = jnp.sin(angles)


def turn_kernel(q_ref, k_ref, v_ref, mate, cosine, sine, totals, gq, gk, out, table):
    _, core = position()
    half = out.shape[2]
    columns = pl.ds(pl.multiple_of(core * half, 128), half)
    swap = signed_swap()
    for i in range(2):
        scale = columns_of(lax.rsqrt(totals[i : i + 1, :] / D + EPSILON))
        for j, ref in enumerate((cosine, sine)):
            table[2 * i + j] = ref[:CHIP, :] * scale
    for here, rows in ((True, core), (False, 1 - core)):
        rows = pl.ds(sixteen(rows * ROWS), ROWS)
        out[2, rows, :] = v_ref[:, columns] if here else mate[2]
        for i, (ref, gains) in enumerate(((q_ref, gq), (k_ref, gk))):
            cos_here, sin_here = table[2 * i, rows, :], table[2 * i + 1, rows, :]
            for h in range(half // HD):
                at = slice(h * HD, (h + 1) * HD)
                place = pl.ds(pl.multiple_of(core * half + h * HD, 128), HD)
                gain = gains[:, place]
                x = ref[:, place] if here else mate[i, :, at]
                out[i, rows, at] = turn(x, gain, flip(gain), swap, cos_here, sin_here)


def local_kernel(local, ids, partial, peaks, bias):
    clip_of = columns_of(ids[:, :CHIP])
    for t in range(0, CHIP, HD):
        bias[:, t : t + HD] = jnp.where(clip_of == ids[:, t : t + HD], 0.0, NEGATIVE)
    for h in range(HALF):
        at = slice(h * HD, (h + 1) * HD)
        values = local[2, :, at]
        columns = jnp.concatenate([values, jnp.ones_like(values)], axis=1)
        for t in range(0, CHIP, TILE):
            rows = slice(t, t + TILE)
            scores = lax.dot_general(
                local[0, rows, at], local[1, :, at], (((1,), (1,)), ((), ())),
                preferred_element_type=jnp.float32,
            ) + bias[rows, :]
            peak = jnp.max(scores, axis=1, keepdims=True)
            weights = jnp.exp2((scores - peak) * SCORE_SCALE).astype(jnp.bfloat16)
            partial[rows, 2 * h * HD : 2 * (h + 1) * HD] = jnp.dot(
                weights, columns, preferred_element_type=jnp.float32
            )
            peaks[rows, at] = jnp.broadcast_to(peak, (TILE, HD))


def attend_kernel(flexible, head, count, info, *refs):
    local, near_straight, near_slanted, gq, gk, ids = refs[:6]
    streams = 1 if flexible else 2
    refs = refs[6:]
    if flexible:
        (cosine, sine), refs = refs[:2], refs[2:]
    else:
        (table, partial, peaks), refs = refs[:3], refs[3:]
    arrived, refs = refs[:streams], refs[streams:]
    own_out, mate_out, refs = refs[0], refs[1], refs[2:]
    if flexible:
        back, table, refs = refs[0], refs[1], refs[2:]
    near, stream, bias, keys, values, result, sems = refs[:7]
    side, core, _, edge, (first, _, theirs, kept, major) = known(info)
    inner = side != core
    rest = theirs - NEAR
    near_columns = slice(head * HD, (head + count) * HD)
    sizes = (FIRST_ROWS, SECOND_ROWS)[:streams]
    copies, filled = [], 0
    for i, (ref, size) in enumerate(zip(arrived, sizes)):
        copies.append(
            pltpu.make_async_copy(
                ref.at[:size, :], stream.at[filled : filled + size, :], sems.at[1 + i]
            )
        )
        filled += size
    near_copies = [
        pltpu.make_async_copy(ref.at[:, :, near_columns], near, sems.at[0])
        for ref in (near_slanted, near_straight)
    ]
    for copy in copies:
        copy.start()
    pl.when(inner)(near_copies[0].start)
    pl.when(jnp.logical_not(inner))(near_copies[1].start)
    stream[filled:, :] = jnp.zeros((REST, HD), stream.dtype)

    columns = pl.ds(pl.multiple_of((2 * HALF * core + head) * HD, 128), count * HD)
    gq, gk = gq[:, columns], gk[:, columns]
    clip_of = columns_of(ids[:, :CHIP])
    for t in range(0 if flexible else CHIP, 2 * CHIP, HD):
        bias[:, t : t + HD] = jnp.where(clip_of == ids[:, t : t + HD], 0.0, NEGATIVE)
    for h in range(count if flexible else 0):
        here = slice((head + h) * HD, (head + h + 1) * HD)
        keys[h, :CHIP, :] = local[1, :, here]
        values[h, :CHIP, :] = local[2, :, here]
    if flexible:
        back_rows, asked, scales, extra = refs[7:11]
        sum_copy = pltpu.make_async_copy(arrived[0].at[FIRST_ROWS:, :], extra, sems.at[4])
        sum_copy.start()
        near_rows = pl.ds(sixteen(jnp.where(side == 0, 0, REST)), NEAR)
        rest_rows = pl.ds(sixteen(jnp.where(side == 0, NEAR, first)), REST)
        scales[CHIP:, :] = jnp.ones((REST, HD), jnp.float32)
        back_rows[...] = jnp.zeros_like(back_rows)
        sum_copy.wait()
        parts = extra[...].astype(jnp.float32)
        for i, waves in enumerate((asked, table)):
            for j in range(3):
                total = sum(parts[9 * i + 3 * p + j : 9 * i + 3 * p + j + 1, :] for p in range(3))
                scales[j * HD : (j + 1) * HD, :] = columns_of(lax.rsqrt(total / D + EPSILON))
            for j, ref in enumerate((cosine, sine)):
                waves[j, :NEAR, :] = ref[CHIP : CHIP + NEAR, :] * scales[near_rows, :]
                waves[j, NEAR:, :] = ref[CHIP + NEAR :, :] * scales[rest_rows, :]
    near_copies[0].wait()
    for copy in copies:
        copy.wait()

    swap = signed_swap()
    if flexible:
        base = jnp.int32(0)
    else:
        base = 2 * rest * kept + jnp.where(major == 1, (HALF - kept) * (2 * rest + theirs), 0)
        base += 2 * rest * head
    bases = []
    for h in range(count):
        at = slice(h * HD, (h + 1) * HD)
        gain = gk[:, at]
        key_at = base
        bases.append(base)
        if flexible:
            lend = jnp.logical_and(h >= kept, major == 1)
            took = jnp.logical_or(h < kept, major == 1)
            key_at = base + jnp.where(lend, theirs, 0)
            base += jnp.where(took, 2 * rest, 0) + jnp.where(lend, theirs, 0)
        else:
            base += 2 * rest
        far = jnp.concatenate([near[0, :, at], stream[pl.ds(sixteen(key_at), REST), :]], axis=0)
        keys[h, CHIP:, :] = turn(far, gain, flip(gain), swap, table[0], table[1])
        values[h, CHIP : CHIP + NEAR, :] = near[1, :, at]
        values[h, CHIP + NEAR :, :] = stream[pl.ds(sixteen(key_at + rest), REST), :]

    def far_answer(h, size):
        at = slice(h * HD, (h + 1) * HD)
        gain = gq[:, at]
        x = stream[pl.ds(sixteen(bases[h]), size), :]
        far_q = turn(x, gain, flip(gain), swap, asked[0, :size, :], asked[1, :size, :])
        place = jnp.where(h >= kept, (h - kept) * theirs, BACK_ROWS + HD)
        back_rows[pl.ds(sixteen(place), size), :] = attention(
            far_q, keys[h, :SHORT, :], far_bias, values[h, :SHORT, :]
        )

    def answers(seen, lent):
        for h in range(count):
            at = slice(h * HD, (h + 1) * HD)
            here = slice((head + h) * HD, (head + h + 1) * HD)
            for t in range(0, CHIP, TILE):
                rows = slice(t, t + TILE)
                result[rows, at] = attention(
                    local[0, rows, here], keys[h, :seen, :], bias[rows, :seen], values[h, :seen, :]
                )
            if lent == HD or (lent and h > 0):
                far_answer(h, lent)

    def merged(seen):
        for h in range(count):
            at = slice(h * HD, (h + 1) * HD)
            here = slice((head + h) * HD, (head + h + 1) * HD)
            far = values[h, CHIP:seen, :]
            columns = jnp.concatenate([far, jnp.ones_like(far)], axis=1)
            for t in range(0, CHIP, HD):
                rows = slice(t, t + HD)
                scores = lax.dot_general(
                    local[0, rows, here], keys[h, CHIP:seen, :], (((1,), (1,)), ((), ())),
                    preferred_element_type=jnp.float32,
                ) + bias[rows, CHIP:seen]
                before = peaks[rows, h * HD : h * HD + 1]
                peak = jnp.maximum(before, jnp.max(scores, axis=1, keepdims=True))
                weights = jnp.exp2((scores - peak) * SCORE_SCALE).astype(jnp.bfloat16)
                sums = jnp.dot(weights, columns, preferred_element_type=jnp.float32)
                sums += jnp.exp2((before - peak) * SCORE_SCALE) * partial[
                    rows, 2 * h * HD : 2 * (h + 1) * HD
                ]
                result[rows, at] = (sums[:, :HD] / sums[:, HD:]).astype(jnp.bfloat16)

    short = theirs <= SHORT - CHIP
    if flexible:
        far_bias = jnp.where(ids[:, :SHORT] == edge, 0.0, NEGATIVE)
        lending = jnp.logical_and(kept < HALF, major == 1)

        wide = theirs > HD
        pl.when(jnp.logical_and(lending, wide))(lambda: answers(SHORT, 2 * HD))
        pl.when(jnp.logical_and(lending, jnp.logical_not(wide)))(lambda: answers(SHORT, HD))
        pl.when(jnp.logical_and(short, jnp.logical_not(lending)))(lambda: answers(SHORT, 0))
        pl.when(jnp.logical_not(short))(lambda: answers(2 * CHIP, 0))
    else:
        pl.when(short)(lambda: merged(SHORT))
        pl.when(jnp.logical_not(short))(lambda: merged(2 * CHIP))
    own_out[...] = result[pl.ds(sixteen(core * ROWS), ROWS), :]
    mate_out[...] = result[pl.ds(sixteen((1 - core) * ROWS), ROWS), :]
    if flexible:
        back[...] = back_rows[:BACK_ROWS, :]


def join_kernel(
    info, flex_here, fixed_here, flex_there, fixed_there, back_here, back_there, ids, out, rows, lines
):
    side, core, _, edge, (first, mine, _, kept, major) = known(info)
    half = 2 * WIDE
    inside = columns_of(ids[...].astype(jnp.float32)) == edge
    for here, flex, fixed, back in (
        (True, flex_here, fixed_here, back_here),
        (False, flex_there, fixed_there, back_there),
    ):
        column = pl.multiple_of((core if here else 1 - core) * half, 128)
        out[:, pl.ds(column, WIDE)] = fixed[...]
        out[:, pl.ds(pl.multiple_of(column + WIDE, 128), WIDE)] = flex[...]

        @pl.when(jnp.logical_and(major == 0, kept < HALF))
        def _():
            rows[:BACK_ROWS, :] = back[...]
            rows[BACK_ROWS:, :] = jnp.zeros((REST, HD), rows.dtype)
            for h in range(HALF):

                @pl.when(h >= kept)
                def _():
                    base = (h - kept) * mine
                    near_at = jnp.where(side == 0, REST, 0)
                    rest_at = jnp.where(side == 0, first, NEAR)
                    lines[pl.ds(sixteen(rest_at), REST), :] = rows[
                        pl.ds(sixteen(base + NEAR), REST), :
                    ]
                    lines[pl.ds(sixteen(near_at), NEAR), :] = rows[pl.ds(sixteen(base), NEAR), :]
                    at = slice(h * HD, (h + 1) * HD)
                    place = pl.ds(pl.multiple_of(column + WIDE + h * HD, 128), HD)
                    out[:, place] = jnp.where(
                        inside, lines[pl.ds(sixteen(core * ROWS), ROWS), :], flex[:, at]
                    )


def frequencies():
    sixth_part = HD // 6
    first_dims = HD - 4 * sixth_part
    first_freqs = 1.0 / ROTARY_BASE ** (
        jnp.arange(0, first_dims, 2, dtype=jnp.float32) / first_dims
    )
    other_freqs = 1.0 / ROTARY_BASE ** (
        jnp.arange(0, 2 * sixth_part, 2, dtype=jnp.float32) / (2 * sixth_part)
    )
    return jnp.repeat(jnp.concatenate([first_freqs, other_freqs, other_freqs]), 2)[None, :]


def whole(a):
    return pl.BlockSpec(a.shape, lambda i: (0,) * len(a.shape))


def held():
    return pl.BlockSpec(memory_space=pltpu.VMEM)


def call(kernel, out_shape, in_specs, out_specs, scratch, *operands, limit=VMEM):
    return pl.pallas_call(
        kernel,
        grid=(1,),
        out_shape=out_shape,
        in_specs=in_specs,
        out_specs=out_specs,
        scratch_shapes=scratch,
        compiler_params=pltpu.CompilerParams(vmem_limit_bytes=limit),
        cost_estimate=pl.CostEstimate(flops=0, bytes_accessed=0, transcendentals=0),
    )(*operands)


def attend(flexible, head, count, info, streams, waves, local, near_straight, near_slanted, gains, ids):
    bf16, f32 = jnp.bfloat16, jnp.float32
    there = pl.BlockSpec(memory_space=pl.ANY)
    shapes = [jax.ShapeDtypeStruct((ROWS, count * HD), bf16)] * 2
    stream_rows = sum((FIRST_ROWS, SECOND_ROWS)[: len(streams)]) + REST
    scratch = [
        pltpu.VMEM((2, NEAR, count * HD), bf16),
        pltpu.VMEM((stream_rows, HD), bf16),
        pltpu.VMEM((CHIP, 2 * CHIP), f32),
        pltpu.VMEM((count, 2 * CHIP, HD), bf16),
        pltpu.VMEM((count, 2 * CHIP, HD), bf16),
        pltpu.VMEM((CHIP, count * HD), bf16),
        pltpu.SemaphoreType.DMA((5,)),
    ]
    if flexible:
        far_waves = jax.ShapeDtypeStruct((2, CHIP, HD), f32)
        shapes = shapes + [jax.ShapeDtypeStruct((BACK_ROWS, HD), bf16), far_waves]
        scratch = scratch + [
            pltpu.VMEM((BACK_ROWS + 3 * HD, HD), bf16),
            pltpu.VMEM((2, CHIP, HD), f32),
            pltpu.VMEM((CHIP + REST, HD), f32),
            pltpu.VMEM((SUM_ROWS, HD), bf16),
        ]
    operands = (local, near_straight, near_slanted, *gains, ids, *waves, *streams)
    in_specs = [held(), held(), there, there] + [held()] * (3 + len(waves)) + [there] * len(streams)
    return call(
        functools.partial(attend_kernel, flexible, head, count), shapes,
        in_specs, [held()] * len(shapes), scratch, info, *operands,
    )


def on_device(queries, keys, values, gain_q, gain_k, clip_ids, clip_grid):
    width = queries.shape[1]
    half = width // 2
    bf16, f32 = jnp.bfloat16, jnp.float32

    clip_row = clip_ids[None, :]

    near_shape = jax.ShapeDtypeStruct((2, NEAR, half), bf16)
    deal_shapes = [
        jax.ShapeDtypeStruct((3, ROWS, half), bf16),
        near_shape,
        near_shape,
        jax.ShapeDtypeStruct((3, ROWS), f32),
    ]
    dealt, near_own, near_other, sums = call(
        deal_kernel, deal_shapes, [whole(queries)] * 3 + [whole(clip_row)],
        [whole(s) for s in deal_shapes], [], queries, keys, values, clip_row, limit=ALL_VMEM,
    )
    near_straight = lax.ppermute(near_own, "ctx", STRAIGHT)
    near_slanted = lax.ppermute(near_other, "ctx", SLANTED)
    mate = lax.ppermute(dealt, "ctx", BESIDE)
    mate_sums = lax.ppermute(sums, "ctx", BESIDE)
    row_sums = lax.ppermute(sums, "row", OTHER_ROW)
    mate_row_sums = lax.ppermute(sums, ("ctx", "row"), OPPOSITE)
    stream_shapes = [
        jax.ShapeDtypeStruct((FIRST_ROWS + SUM_ROWS, HD), bf16),
        jax.ShapeDtypeStruct((SECOND_ROWS, HD), bf16),
        jax.ShapeDtypeStruct((2, CHIP), f32),
    ]
    first_send, second_send, totals, info = call(
        pack_kernel, stream_shapes + [jax.ShapeDtypeStruct((1, HD), f32)],
        [held()] * 8, [whole(shape) for shape in stream_shapes[:2]] + [held()] * 2,
        [
            pltpu.VMEM((3, CHIP + NEAR, half), bf16),
            pltpu.VMEM((STREAM_ROWS + NEAR, HD), bf16),
        ],
        queries, keys, values, mate, sums, mate_sums, row_sums, mate_row_sums,
    )

    first_stream = lax.ppermute(first_send, "ctx", ACROSS)
    second_stream = lax.ppermute(second_send, "ctx", ACROSS)
    near_straight, near_slanted, sums, _ = lax.optimization_barrier(
        (near_straight, near_slanted, sums, first_send)
    )
    wave_shape = jax.ShapeDtypeStruct((2 * CHIP, HD), f32)
    cosine, sine, mask_ids = call(
        waves_kernel, [wave_shape, wave_shape, jax.ShapeDtypeStruct((1, 2 * CHIP), f32)],
        [pl.BlockSpec(memory_space=pltpu.SMEM)] + [held()] * 4, [held()] * 3,
        [pltpu.VMEM((1, CHIP), f32)], clip_grid, info, sums, mate_sums, frequencies(),
    )
    gains = (gain_q[None, :], gain_k[None, :])
    local_shape = jax.ShapeDtypeStruct((3, CHIP, half), bf16)
    local = call(
        turn_kernel, local_shape, [held()] * 9, held(), [pltpu.VMEM((4, CHIP, HD), f32)],
        queries, keys, values, mate, cosine, sine, totals, *gains,
    )
    common = (local, near_straight, near_slanted, gains, mask_ids)
    partial, peaks = call(
        local_kernel,
        [
            jax.ShapeDtypeStruct((CHIP, 2 * WIDE), f32),
            jax.ShapeDtypeStruct((CHIP, WIDE), f32),
        ],
        [held()] * 2, [held()] * 2, [pltpu.VMEM((CHIP, CHIP), f32)], local, mask_ids,
    )
    first_stream, partial = lax.optimization_barrier((first_stream, partial))
    flex_here, flex_send, back_send, far_waves = attend(
        True, HALF, HALF, info, (first_stream,), (cosine, sine), *common
    )
    back_here = lax.ppermute(back_send, "ctx", ACROSS)
    fixed_here, fixed_send = attend(
        False, 0, HALF, info, (first_stream, second_stream),
        (far_waves, partial, peaks), *common
    )
    flex_send, fixed_send = lax.optimization_barrier((flex_send, fixed_send))
    flex_there = lax.ppermute(flex_send, "ctx", BESIDE)
    fixed_there = lax.ppermute(fixed_send, "ctx", BESIDE)
    back_here, _ = lax.optimization_barrier((back_here, fixed_send))
    back_there = lax.ppermute(back_here, "ctx", BESIDE)
    out_shape = jax.ShapeDtypeStruct((ROWS, width), bf16)
    operands = (
        flex_here, fixed_here, flex_there, fixed_there, back_here, back_there, clip_row
    )
    return call(
        join_kernel, out_shape, [held()] * 8, whole(out_shape),
        [pltpu.VMEM((BACK_ROWS + REST, HD), bf16), pltpu.VMEM((2 * REST, HD), bf16)],
        info, *operands,
    )


def lookup(lookup_table, positions):
    labels = jnp.arange(lookup_table.shape[0], dtype=jnp.int32)
    return jnp.sum(
        jnp.where(positions[:, None] == labels[None, :], lookup_table[None, :], 0), axis=1
    )


def spin(matrix, offsets, clip_of, clip_grid, head_size):
    row_count = matrix.shape[0]
    sixth_part = head_size // 6
    first_dims = head_size - 4 * sixth_part
    first_freqs = 1.0 / ROTARY_BASE ** (
        jnp.arange(0, first_dims, 2, dtype=jnp.float32) / first_dims
    )
    other_freqs = 1.0 / ROTARY_BASE ** (
        jnp.arange(0, 2 * sixth_part, 2, dtype=jnp.float32) / (2 * sixth_part)
    )
    heights = lookup(clip_grid[:, 0], clip_of)
    widths = lookup(clip_grid[:, 1], clip_of)
    frame_pos = offsets // (heights * widths)
    line_pos = offsets // widths % heights
    column_pos = offsets % widths
    angles = jnp.concatenate(
        [
            frame_pos.astype(jnp.float32)[:, None] * first_freqs[None, :],
            line_pos.astype(jnp.float32)[:, None] * other_freqs[None, :],
            column_pos.astype(jnp.float32)[:, None] * other_freqs[None, :],
        ],
        axis=1,
    )
    cosine = jnp.repeat(jnp.cos(angles), 2, axis=1)
    sine_table = jnp.repeat(jnp.sin(angles), 2, axis=1)
    feature = jnp.arange(head_size, dtype=jnp.int32)
    is_even = (feature % 2 == 0)[None, None, :]
    head_view = matrix.reshape(row_count, -1, head_size)
    partner = jnp.where(is_even, -jnp.roll(head_view, -1, axis=2), jnp.roll(head_view, 1, axis=2))
    turned = head_view * cosine[:, None, :] + partner * sine_table[:, None, :]
    return turned.reshape(row_count, -1)


def on_any(queries, keys, values, gain_q, gain_k, clip_ids, clip_grid):
    rows_here, width_here = queries.shape
    heads_here = width_here // HD
    score_scale = 1.0 / math.sqrt(HD)
    query_wide = queries.astype(jnp.float32)
    key_wide = keys.astype(jnp.float32)
    squares = lax.psum(
        (jnp.sum(query_wide * query_wide, axis=1), jnp.sum(key_wide * key_wide, axis=1)), "row"
    )
    query_scale = lax.rsqrt(squares[0] / D + EPSILON)
    key_scale = lax.rsqrt(squares[1] / D + EPSILON)
    labels = jnp.arange(CLIPS, dtype=jnp.int32)
    local_counts = jnp.sum((clip_ids[:, None] == labels[None, :]).astype(jnp.int32), axis=0)
    totals = lax.psum(local_counts, "ctx")
    starts = jnp.cumsum(totals) - totals
    first_row = lax.axis_index("ctx") * rows_here
    offsets = first_row + jnp.arange(rows_here, dtype=jnp.int32) - lookup(starts, clip_ids)
    query_rot = spin(
        query_wide * query_scale[:, None] * gain_q[None, :], offsets, clip_ids, clip_grid, HD
    ).astype(jnp.bfloat16)
    query_heads = query_rot.reshape(rows_here, heads_here, HD)
    key_send = spin(
        key_wide * key_scale[:, None] * gain_k[None, :], offsets, clip_ids, clip_grid, HD
    ).astype(jnp.bfloat16)
    initial = (
        jnp.full((heads_here, rows_here), NEGATIVE, jnp.float32),
        jnp.zeros((heads_here, rows_here), jnp.float32),
        jnp.zeros((rows_here, heads_here, HD), jnp.float32),
    )
    running = initial
    piece_start = jnp.int32(0)
    key_piece = lax.all_gather(key_send, "ctx", axis=0, tiled=True)
    value_piece = lax.all_gather(values, "ctx", axis=0, tiled=True)
    row_count = key_piece.shape[0]
    block_rows = min(row_count, block_limit)
    for block_first in range(0, row_count, block_rows):
        block_size = min(block_rows, row_count - block_first)
        fold_key_rows = key_piece[block_first : block_first + block_size]
        fold_value_rows = value_piece[block_first : block_first + block_size]
        key_index = piece_start + block_first + jnp.arange(fold_key_rows.shape[0], dtype=jnp.int32)
        key_key_clips = (
            jnp.sum((starts[None, :] <= key_index[:, None]).astype(jnp.int32), axis=1) - 1
        )
        peak_old, total_old, summed_old = running
        key_view = fold_key_rows.reshape(fold_key_rows.shape[0], heads_here, HD)
        value_view = fold_value_rows.reshape(fold_value_rows.shape[0], heads_here, HD)
        scores = (
            jnp.einsum("qhd,khd->hqk", query_heads, key_view, preferred_element_type=jnp.float32)
            * score_scale
        )
        same = clip_ids[:, None] == key_key_clips[None, :]
        masked = jnp.where(same[None, :, :], scores, NEGATIVE)
        peak_new = jnp.maximum(peak_old, jnp.max(masked, axis=2))
        weights = jnp.where(same[None, :, :], jnp.exp(masked - peak_new[:, :, None]), 0.0)
        factor = jnp.exp(peak_old - peak_new)
        total_new = total_old * factor + jnp.sum(weights, axis=2)
        summed = summed_old * jnp.transpose(factor)[:, :, None] + jnp.einsum(
            "hqk,khd->qhd",
            weights.astype(jnp.bfloat16),
            value_view,
            preferred_element_type=jnp.float32,
        )
        running = (peak_new, total_new, summed)
    attended = running[2] / jnp.transpose(running[1])[:, :, None]
    return attended.reshape(rows_here, width_here).astype(jnp.bfloat16)


def solution(mesh):
    in_specs = (
        P(("batch", "ctx"), "row"),
        P(("batch", "ctx"), "row"),
        P(("batch", "ctx"), "row"),
        P("row"),
        P("row"),
        P(("batch", "ctx")),
        P("batch", None),
    )
    out_specs = P(("batch", "ctx"), "row")
    pair_of_chips = mesh.shape["ctx"] == 4 and mesh.shape["row"] == 2
    return jax.shard_map(
        on_device if pair_of_chips else on_any,
        mesh=mesh, in_specs=in_specs, out_specs=out_specs, check_vma=False,
    )
```
